32 devices in a mesh: groups: 2 (over y), col: 4 (over x, core), row: 4 (over z).
Axes of the slice: x: 2, y: 2, z: 4, core: 2. Of those that a mesh axis runs over, the one named last changes fastest.
Arguments:
- momentum: float32 [7168, 18432], P(('groups', 'row'), 'col'), parts along dimension 0, may hold values from -300 to 300
Outputs:
- update: float32 [7168, 18432], P(('groups', 'row'), 'col'), parts along dimension 0
The draws below stay inside these ranges and needn't reach their ends.
There are 2 independent parts, one for each index of `groups`. The reference program is written for one: setup_inputs(seed, part) draws one part's arguments, and reference() takes and returns one part's arrays. A program takes and returns all parts, laid end to end along the dimension named above; each array names one. Nothing has to cross between parts.
All inputs are finite; a program needn't handle non-finite values.
Results may differ from the reference program's by a relative error of at most 0.017.
Values may be sent and summed in bfloat16 or wider, within the bound.
No kernel may reach another device: no remote copies, remote signals or barrier semaphores. Data moves between devices by JAX's collectives and lax.ppermute only.
A program may use at most 192 MiB of HBM per device.

```python
import math
import jax
import jax.numpy as jnp
from jax import lax

M = 3584
N = 18432
N_COL = 4


def draw_momentum(key, part):
    key = jax.random.fold_in(key, 11)
    subkeys = jax.random.split(key, 5)
    row_place = jnp.arange(M, dtype=jnp.float32)[:, None] / M
    col_place = jnp.arange(N, dtype=jnp.float32)[None, :] / N
    row_scale = jnp.exp(jax.random.uniform(subkeys[0], (M, 1), jnp.float32, 0.0, math.log(1.5))) * (1.0 + 0.75 * row_place)
    col_scale = jnp.exp(jax.random.uniform(subkeys[1], (1, N), jnp.float32, 0.0, math.log(4.0))) * (1.0 + 0.75 * col_place)
    row_factor = jax.random.truncated_normal(subkeys[3], -3.0, 3.0, (M, 1), jnp.float32)
    col_factor = jax.random.truncated_normal(subkeys[4], -3.0, 3.0, (1, N), jnp.float32)
    rough_part = jax.random.truncated_normal(subkeys[2], -4.0, 4.0, (M, N), jnp.float32)
    common_weight = 0.5 / math.sqrt(M)
    return row_scale * col_scale * (rough_part + common_weight * row_factor * col_factor)


def setup_inputs(seed: int = 0, part: int = 0) -> dict:
    key_of = jax.random.split(jax.random.key(seed), 2)
    part_splits = jax.random.split(jax.random.fold_in(key_of[1], part), 2)
    return {
        "momentum": draw_momentum(jax.random.fold_in(jax.random.fold_in(key_of[1], part), 71), part),
    }


coef_linear = 3.4445
coef_cubic = -4.775
coef_quintic = 2.0315

def reference(momentum):
    sum_sq = jnp.sum(momentum * momentum)
    spectral_edge = 1.0 + math.sqrt(M / N)
    scaled = (momentum / (jnp.sqrt(sum_sq / M) * spectral_edge + 1e-07)).astype(jnp.bfloat16)
    widened = scaled.astype(jnp.float32)
    col_blocks = widened.reshape(M, N_COL, N // N_COL).transpose(1, 0, 2)

    def add_block(running, segment):
        partial_value = jnp.dot(segment, segment.T, precision=lax.Precision.HIGHEST)
        rounded = lax.optimization_barrier(partial_value.astype(jnp.bfloat16))
        return (running + rounded.astype(jnp.float32), None)
    gram_sum, unused = lax.scan(add_block, jnp.zeros((M, M), jnp.float32), col_blocks)
    gram = lax.optimization_barrier(gram_sum.astype(jnp.bfloat16)).astype(jnp.float32)
    squared = jnp.dot(gram, gram, precision=lax.Precision.HIGHEST)
    poly = lax.optimization_barrier((coef_cubic * gram + coef_quintic * squared).astype(jnp.bfloat16)).astype(jnp.float32)
    newton = coef_linear * widened + jnp.dot(poly, widened, precision=lax.Precision.HIGHEST)
    newton_sq = jnp.sum(newton * newton)
    return newton / (jnp.sqrt(newton_sq) / math.sqrt(M * N) + 1e-07)
```

```python
import math

import jax
import jax.numpy as jnp
from jax import lax
from jax.sharding import PartitionSpec as P

M = 3584
N = 18432

coef_linear = 3.4445
coef_cubic = -4.775
coef_quintic = 2.0315


def orientation(i, j, n):
    low, high = min(i, j), max(i, j)
    return (low, high) if i + j <= n - 1 else (high, low)


def per_device(momentum):
    n_row = lax.axis_size("row")
    n_col = lax.axis_size("col")
    rows, cols = momentum.shape
    half = n_row // 2
    width = cols // 2
    z = lax.axis_index("row")
    left = z < half
    is_hub = (z == half) | (z == half - 1)

    near_at = jnp.where(left, width, 0)
    far_at = width - near_at
    far = lax.dynamic_slice(momentum, (0, far_at), (rows, width)).astype(jnp.bfloat16)
    near = lax.dynamic_slice(momentum, (0, near_at), (rows, width)).astype(jnp.bfloat16)

    def to_hub(block, r):
        return lax.ppermute(block, "row", [(r, half), (n_row - 1 - r, half - 1)])

    def from_hub(block, r):
        return lax.ppermute(block, "row", [(half, r), (half - 1, n_row - 1 - r)])

    early = list(range(half - 1, n_row))
    late = list(range(half - 1))
    blocks = {half: near}
    for r in early:
        if r != half:
            blocks[r] = to_hub(far if r < half else near, r)
    far_later, blocks[half - 1] = lax.optimization_barrier((far, blocks[half - 1]))
    for r in late:
        blocks[r] = to_hub(far_later, r)

    norm_sum = lax.psum(jnp.sum(momentum * momentum), ("col", "row"))
    spectral_edge = 1.0 + math.sqrt(M / N)
    inverse = 1.0 / (jnp.sqrt(norm_sum / M) * spectral_edge + 1e-07)

    def partial_gram(i, j):
        value = lax.dot_general(
            blocks[i], blocks[j], (((1,), (1,)), ((), ())), preferred_element_type=jnp.float32
        ).astype(jnp.bfloat16)
        if i != j and i + j == n_row - 1:
            value = jnp.where(left, value.T, value)
        return value

    def scattered(pairs):
        stack = jnp.stack(
            [partial_gram(i, j).reshape(n_col, rows // n_col, rows) for i, j in pairs], axis=1
        )
        summed = lax.psum_scatter(stack, "col", scatter_dimension=0, tiled=False)
        other = lax.ppermute(summed, "row", [(half, half - 1), (half - 1, half)])
        return summed, other

    pairs_early = [orientation(i, j, n_row) for i in early for j in early if i <= j]
    pairs_late = [
        orientation(i, j, n_row) for i in range(n_row) for j in range(i, n_row) if min(i, j) < half - 1
    ]
    pairs = pairs_early + pairs_late
    mine_early, other_early = scattered(pairs_early)
    mine, other = mine_early, other_early
    if pairs_late:
        mine_late, other_late = scattered(pairs_late)
        mine = jnp.concatenate([mine_early, mine_late])
        other = jnp.concatenate([other_early, other_late])
    place = {pair: k for k, pair in enumerate(pairs)}

    def mirror(pair):
        i, j = pair
        if i + j == n_row - 1:
            return pair
        return (n_row - 1 - i, n_row - 1 - j)

    gram_sum = jnp.stack(
        [
            mine[k].astype(jnp.float32) + other[place[mirror(pair)]].astype(jnp.float32)
            for k, pair in enumerate(pairs)
        ]
    )
    gram_part = (gram_sum * (inverse * inverse)).astype(jnp.bfloat16)
    gram_blocks = lax.all_gather(gram_part, "col", axis=0, tiled=False)

    def gram_block(i, j):
        pair = orientation(i, j, n_row)
        value = gram_blocks[:, place[pair]].reshape(rows, rows)
        if i != j and i + j == n_row - 1:
            return jnp.where(left, value.T, value) if (i, j) == pair else jnp.where(left, value, value.T)
        return value if (i, j) == pair else value.T

    gram = jnp.concatenate(
        [jnp.concatenate([gram_block(i, j) for j in range(n_row)], axis=1) for i in range(n_row)], axis=0
    )

    share = gram.shape[0] // 2
    core = lax.axis_index("col") % 2
    gram_rows = lax.dynamic_slice(gram, (core * share, 0), (share, gram.shape[1]))
    squared = jnp.dot(gram_rows, gram, preferred_element_type=jnp.float32)
    poly_rows = (coef_cubic * gram_rows.astype(jnp.float32) + coef_quintic * squared).astype(jnp.bfloat16)
    poly_pair = lax.ppermute(poly_rows, "col", [(c, c ^ 1) for c in range(n_col)])
    first = jnp.where(core == 0, poly_rows, poly_pair)
    second = jnp.where(core == 0, poly_pair, poly_rows)
    poly = jnp.concatenate([first, second], axis=0)

    chunks = 3
    step = width // chunks
    near_parts, far_parts = [], []
    newton_sq = jnp.float32(0.0)
    for k in range(chunks):
        raw = jnp.concatenate([blocks[r][:, k * step : (k + 1) * step] for r in range(n_row)], axis=0)
        product = jnp.dot(poly, raw, preferred_element_type=jnp.float32)
        newton = inverse * (coef_linear * raw.astype(jnp.float32) + product)
        newton_sq += jnp.sum(newton * newton)
        newton = newton.astype(jnp.bfloat16).reshape(n_row, rows, step)
        near_part, far_part = jnp.where(is_hub, newton[half], 0), 0
        for r in range(n_row):
            if r > half:
                near_part = near_part + from_hub(newton[r], r)
            if r < half:
                far_part = far_part + from_hub(newton[r], r)
        near_parts.append(near_part)
        far_parts.append(far_part)
    newton_sq = lax.psum(jnp.where(is_hub, newton_sq, 0.0), ("col", "row"))
    factor = 1.0 / (jnp.sqrt(newton_sq) / math.sqrt(M * N) + 1e-07)
    near_all = jnp.concatenate(near_parts, axis=1)
    far_all = jnp.concatenate(far_parts, axis=1)
    update = jnp.concatenate(
        [jnp.where(left, far_all, near_all), jnp.where(left, near_all, far_all)], axis=1
    )
    return update.astype(jnp.float32) * factor


def solution(mesh):
    return jax.shard_map(
        per_device,
        mesh=mesh,
        in_specs=(P(("groups", "row"), "col"),),
        out_specs=P(("groups", "row"), "col"),
        check_vma=False,
    )
```

```python
import functools
import math

import jax
import jax.numpy as jnp
from jax import lax
from jax.experimental import pallas as pl
from jax.experimental.pallas import tpu as pltpu
from jax.sharding import PartitionSpec as P

M = 3584
N = 18432

coef_linear = 3.4445
coef_cubic = -4.775
coef_quintic = 2.0315

TILE = 256
STRIP = 128
VMEM_BYTES = 56 * 2**20

EARLY = [(1, 2), (1, 1), (2, 2), (3, 3), (3, 2), (3, 1)]
LATE_A = [(0, 0), (0, 1)]
LATE_B = [(0, 2), (0, 3)]
GATHERED = [[(1, 2), (1, 1), (2, 2)], [(0, 0), (3, 3), (0, 1), (3, 2)], [(0, 2), (3, 1), (0, 3)]]


def mirror(pair):
    return pair if sum(pair) == 3 and pair[0] != pair[1] else (3 - pair[0], 3 - pair[1])


def take_kernel(index, x_ref, out_ref, sq_ref):
    @pl.when(pl.program_id(0) == 0)
    def _():
        sq_ref[...] = jnp.zeros_like(sq_ref)

    x = x_ref[...]
    out_ref[...] = x.astype(jnp.bfloat16)
    sq_ref[...] += jnp.sum(x * x, axis=0, keepdims=True)


def take(momentum, index):
    rows, cols = momentum.shape
    width = cols // 2
    step = rows // 4
    return pl.pallas_call(
        take_kernel,
        grid_spec=pltpu.PrefetchScalarGridSpec(
            num_scalar_prefetch=1,
            grid=(4,),
            in_specs=[pl.BlockSpec((step, width), lambda t, index: (t, index[0]))],
            out_specs=[
                pl.BlockSpec((step, width), lambda t, index: (t, 0)),
                pl.BlockSpec((1, width), lambda t, index: (0, 0)),
            ],
        ),
        out_shape=[
            jax.ShapeDtypeStruct((rows, width), jnp.bfloat16),
            jax.ShapeDtypeStruct((1, width), jnp.float32),
        ],
        compiler_params=pltpu.CompilerParams(vmem_limit_bytes=VMEM_BYTES),
        cost_estimate=pl.CostEstimate(
            flops=2 * rows * width, bytes_accessed=6 * rows * width, transcendentals=0
        ),
        name="take_half",
    )(index, momentum)


def transpose_block(ref, rows, source, target):
    @pl.loop(0, rows // STRIP)
    def _(s):
        part = ref[
            pl.ds(pl.multiple_of(source[0] * rows, STRIP), rows),
            pl.ds(pl.multiple_of(source[1] * rows + s * STRIP, STRIP), STRIP),
        ]
        ref[
            pl.ds(pl.multiple_of(target[0] * rows + s * STRIP, STRIP), STRIP),
            pl.ds(pl.multiple_of(target[1] * rows, STRIP), rows),
        ] = part.T


def poly_place(core, b):
    i = jnp.where(core == 0, jnp.where(b < 4, 0, 3), jnp.where(b < 3, 1, 2))
    j = jnp.where(core == 0, jnp.where(b < 4, b, 3), jnp.where(b < 3, b + 1, b - 1))
    return i, j


def poly_kernel(flags, first, second, third, out_ref, gram, sems):
    rows = out_ref.shape[1]
    part = rows // 4
    left = flags[0]
    b = pl.program_id(0)

    @pl.when(b == 0)
    def _():
        copies, turned = [], []
        for group, pairs in zip((first, second, third), GATHERED):
            for k, (i, j) in enumerate(pairs):
                if i != j and i + j == 3:
                    i, j = jnp.where(left == 1, j, i), jnp.where(left == 1, i, j)
                for q in range(4):
                    copies.append(
                        pltpu.make_async_copy(
                            group.at[q, k],
                            gram.at[
                                pl.ds(pl.multiple_of(i * rows + q * part, 16), part),
                                pl.ds(pl.multiple_of(j * rows, STRIP), rows),
                            ],
                            sems.at[len(copies)],
                        )
                    )
                if pairs[k][0] != pairs[k][1]:
                    turned.append((i, j))
        for copy in copies:
            copy.start()
        for copy in copies:
            copy.wait()
        for i, j in turned:
            transpose_block(gram, rows, (i, j), (j, i))

    i, j = poly_place(flags[1], b)
    at_i = pl.multiple_of(i * rows, STRIP)
    width = (rows // STRIP + 1) // 2 * STRIP
    for start in range(0, rows, width):
        size = min(width, rows - start)
        at_j = pl.multiple_of(j * rows + start, STRIP)
        squared = jnp.dot(
            gram[pl.ds(at_i, rows), :], gram[:, pl.ds(at_j, size)], preferred_element_type=jnp.float32
        )
        here = gram[pl.ds(at_i, rows), pl.ds(at_j, size)].astype(jnp.float32)
        out_ref[0, :, start : start + size] = (coef_cubic * here + coef_quintic * squared).astype(jnp.bfloat16)


def poly_blocks(flags, groups):
    rows = groups[0].shape[3]
    order = 4 * rows
    return pl.pallas_call(
        poly_kernel,
        grid_spec=pltpu.PrefetchScalarGridSpec(
            num_scalar_prefetch=1,
            grid=(5,),
            in_specs=[pl.BlockSpec(memory_space=pl.ANY)] * 3,
            out_specs=pl.BlockSpec((1, rows, rows), lambda b, flags: (b, 0, 0)),
            scratch_shapes=[pltpu.VMEM((order, order), jnp.bfloat16), pltpu.SemaphoreType.DMA((40,))],
        ),
        out_shape=jax.ShapeDtypeStruct((5, rows, rows), jnp.bfloat16),
        compiler_params=pltpu.CompilerParams(vmem_limit_bytes=VMEM_BYTES),
        cost_estimate=pl.CostEstimate(
            flops=10 * rows * rows * order, bytes_accessed=30 * rows * rows, transcendentals=0
        ),
        name="poly_blocks",
    )(flags, *groups)


def product_kernel(flags, own, pair, inverse, s0, s1, s2, s3, o0, o1, o2, o3, sq_ref, poly, raw, sems):
    rows = s0.shape[0]

    @pl.when(pl.program_id(0) == 0)
    def _():
        sq_ref[...] = jnp.zeros_like(sq_ref)
        copies = []
        for source, core in ((own, flags[1]), (pair, 1 - flags[1])):
            for b in range(5):
                i, j = poly_place(core, b)
                copies.append(
                    pltpu.make_async_copy(
                        source.at[b],
                        poly.at[
                            pl.ds(pl.multiple_of(i * rows, STRIP), rows),
                            pl.ds(pl.multiple_of(j * rows, STRIP), rows),
                        ],
                        sems.at[len(copies)],
                    )
                )
        for copy in copies:
            copy.start()
        for copy in copies:
            copy.wait()
        for i in range(4):
            for j in range(i + 1, 4):
                transpose_block(poly, rows, (i, j), (j, i))

    for r, s_ref in enumerate((s0, s1, s2, s3)):
        raw[r * rows : (r + 1) * rows, :] = s_ref[...]
    for r, (s_ref, o_ref) in enumerate(zip((s0, s1, s2, s3), (o0, o1, o2, o3))):
        product = jnp.dot(
            poly[r * rows : (r + 1) * rows, :], raw[...], preferred_element_type=jnp.float32
        )
        newton = inverse[0] * (coef_linear * s_ref[...].astype(jnp.float32) + product)
        sq_ref[...] += jnp.sum(newton * newton, axis=0, keepdims=True)
        o_ref[...] = newton.astype(jnp.bfloat16)


def product(flags, own, pair, inverse, blocks, first, tiles):
    rows = own.shape[1]
    order = 4 * rows
    here = pl.BlockSpec((rows, TILE), lambda t, flags: (0, first + t))
    there = pl.BlockSpec((rows, TILE), lambda t, flags: (0, t))
    *newton, squares = pl.pallas_call(
        product_kernel,
        grid_spec=pltpu.PrefetchScalarGridSpec(
            num_scalar_prefetch=1,
            grid=(tiles,),
            in_specs=[
                pl.BlockSpec(memory_space=pl.ANY),
                pl.BlockSpec(memory_space=pl.ANY),
                pl.BlockSpec(memory_space=pltpu.SMEM),
            ]
            + [here] * 4,
            out_specs=[there] * 4 + [pl.BlockSpec((1, TILE), lambda t, flags: (0, 0))],
            scratch_shapes=[
                pltpu.VMEM((order, order), jnp.bfloat16),
                pltpu.VMEM((order, TILE), jnp.bfloat16),
                pltpu.SemaphoreType.DMA((10,)),
            ],
        ),
        out_shape=[jax.ShapeDtypeStruct((rows, tiles * TILE), jnp.bfloat16)] * 4
        + [jax.ShapeDtypeStruct((1, TILE), jnp.float32)],
        compiler_params=pltpu.CompilerParams(vmem_limit_bytes=VMEM_BYTES),
        cost_estimate=pl.CostEstimate(
            flops=2 * order * order * tiles * TILE,
            bytes_accessed=20 * rows * rows + 4 * order * tiles * TILE,
            transcendentals=0,
        ),
        name="product",
    )(flags, own, pair, inverse, *blocks)
    return newton, jnp.sum(squares)


def finish_kernel(flags, factor, own, near, middle, far, *rest):
    out_ref = rest[-1]
    is_hub = flags[2] == 1

    @pl.when((pl.program_id(0) == 0) & is_hub)
    def _():
        out_ref[...] = own[...].astype(jnp.float32) * factor[0]

    @pl.when((pl.program_id(0) == 0) & jnp.logical_not(is_hub))
    def _():
        out_ref[...] = near[...].astype(jnp.float32) * factor[0]

    @pl.when((pl.program_id(0) == 1) & is_hub)
    def _():
        out_ref[...] = middle[...].astype(jnp.float32) * factor[0]

    @pl.when((pl.program_id(0) == 1) & jnp.logical_not(is_hub))
    def _():
        out_ref[...] = far[...].astype(jnp.float32) * factor[0]


def finish(flags, factor, parts, first, shape, before):
    rows, cols = shape
    tiles = parts[0].shape[1] // TILE
    half = cols // 2 // TILE
    near_part = pl.BlockSpec((rows, TILE), lambda p, t, flags: (0, jnp.where(p == 0, t, tiles - 1)))
    far_part = pl.BlockSpec((rows, TILE), lambda p, t, flags: (0, jnp.where(p == 0, 0, t)))
    place = pl.BlockSpec(
        (rows, TILE),
        lambda p, t, flags: (0, jnp.where(p == 0, flags[0], 1 - flags[0]) * half + first + t),
    )
    specs = [pl.BlockSpec(memory_space=pltpu.SMEM), near_part, near_part, far_part, far_part]
    operands = [flags, factor, *parts]
    aliases = {}
    if before is not None:
        specs.append(pl.BlockSpec(memory_space=pl.ANY))
        aliases = {len(operands): 0}
        operands.append(before)
    return pl.pallas_call(
        finish_kernel,
        grid_spec=pltpu.PrefetchScalarGridSpec(
            num_scalar_prefetch=1, grid=(2, tiles), in_specs=specs, out_specs=place
        ),
        out_shape=jax.ShapeDtypeStruct(shape, jnp.float32),
        input_output_aliases=aliases,
        compiler_params=pltpu.CompilerParams(vmem_limit_bytes=VMEM_BYTES),
        cost_estimate=pl.CostEstimate(
            flops=2 * rows * TILE * tiles, bytes_accessed=16 * rows * TILE * tiles, transcendentals=0
        ),
        name="finish",
    )(*operands)


def per_device(momentum):
    rows, cols = momentum.shape
    width = cols // 2
    z = lax.axis_index("row")
    core = lax.axis_index("col") % 2
    left = z < 2
    is_hub = (z == 1) | (z == 2)
    flags = jnp.stack([left.astype(jnp.int32), core.astype(jnp.int32), is_hub.astype(jnp.int32)])
    near_index = left.astype(jnp.int32).reshape(1)

    far, far_sq = take(momentum, 1 - near_index)
    middle = lax.ppermute(far, "row", [(1, 2), (2, 1)])
    near, near_sq = take(momentum, near_index)
    beside = lax.ppermute(near, "row", [(0, 1), (3, 2)])
    norm_sum = lax.psum(jnp.sum(far_sq) + jnp.sum(near_sq), ("col", "row"))
    spectral_edge = 1.0 + math.sqrt(M / N)
    inverse = 1.0 / (jnp.sqrt(norm_sum / M) * spectral_edge + 1e-07)

    far, middle, inverse = lax.optimization_barrier((far, middle, inverse))
    distant = lax.ppermute(far, "row", [(0, 2), (3, 1)])
    blocks = [distant, middle, near, beside]

    def partial_gram(pair):
        i, j = pair
        value = lax.dot_general(
            blocks[i], blocks[j], (((1,), (1,)), ((), ())), preferred_element_type=jnp.float32
        ).astype(jnp.bfloat16)
        if i != j and i + j == 3:
            value = jnp.where(left, value.T, value)
        return value

    mine, other = {}, {}
    for pairs in (EARLY, LATE_A, LATE_B):
        stack = jnp.stack([partial_gram(pair).reshape(4, rows // 4, rows) for pair in pairs], axis=1)
        summed = lax.psum_scatter(stack, "col", scatter_dimension=0, tiled=False)
        received = lax.ppermute(summed, "row", [(1, 2), (2, 1)])
        for k, pair in enumerate(pairs):
            mine[pair], other[mirror(pair)] = summed[k], received[k]

    groups = []
    for pairs in GATHERED:
        gram = jnp.stack([mine[pair].astype(jnp.float32) + other[pair].astype(jnp.float32) for pair in pairs])
        gram = (gram * (inverse * inverse)).astype(jnp.bfloat16)
        groups.append(lax.all_gather(gram, "col", axis=0, tiled=False))

    own = poly_blocks(flags, groups)
    pair = lax.ppermute(own, "col", [(c, c ^ 1) for c in range(4)])

    tiles = width // TILE
    bounds = sorted({0, tiles * 2 // 9, tiles * 5 // 9, tiles})
    newton_sq = jnp.float32(0.0)
    parts = []
    for first, last in zip(bounds[:-1], bounds[1:]):
        newton, squares = product(flags, own, pair, inverse.reshape(1), blocks, first, last - first)
        newton_sq += squares
        parts.append(
            (
                newton[2],
                lax.ppermute(newton[3], "row", [(1, 0), (2, 3)]),
                lax.ppermute(newton[1], "row", [(1, 2), (2, 1)]),
                lax.ppermute(newton[0], "row", [(2, 0), (1, 3)]),
            )
        )
    newton_sq = lax.psum(jnp.where(is_hub, newton_sq, 0.0), ("col", "row"))
    factor = (1.0 / (jnp.sqrt(newton_sq) / math.sqrt(M * N) + 1e-07)).reshape(1)
    out = None
    for first, part in zip(bounds[:-1], parts):
        out = finish(flags, factor, part, first, (rows, cols), out)
    return out


def per_device_general(momentum):
    norm_sum = lax.psum(jnp.sum(momentum * momentum), ("col", "row"))
    spectral_edge = 1.0 + math.sqrt(M / N)
    scaled = (momentum / (jnp.sqrt(norm_sum / M) * spectral_edge + 1e-07)).astype(jnp.bfloat16)
    columns = lax.all_gather(scaled, "row", axis=0, tiled=True)
    gram_tile = lax.psum_scatter(
        lax.dot_general(
            columns, scaled, (((1,), (1,)), ((), ())), preferred_element_type=jnp.float32
        ).astype(jnp.bfloat16),
        "col",
        scatter_dimension=0,
        tiled=True,
    )
    left_rows = lax.all_gather(gram_tile, "row", axis=1, tiled=True)
    squared = jnp.dot(
        left_rows,
        lax.all_gather(gram_tile, "col", axis=0, tiled=True),
        preferred_element_type=jnp.float32,
    )
    poly = (coef_cubic * gram_tile.astype(jnp.float32) + coef_quintic * squared).astype(jnp.bfloat16)
    product = lax.dot_general(
        lax.all_gather(poly, "col", axis=0, tiled=True),
        columns,
        (((0,), (0,)), ((), ())),
        preferred_element_type=jnp.float32,
    )
    newton = coef_linear * scaled.astype(jnp.float32) + product
    newton_sq = lax.psum(jnp.sum(newton * newton), ("col", "row"))
    update_rms = jnp.sqrt(newton_sq) / math.sqrt(M * N)
    return newton / (update_rms + 1e-07)


def solution(mesh):
    def update(momentum):
        n_row, n_col = mesh.shape["row"], mesh.shape["col"]
        rows = momentum.shape[0] // (mesh.shape["groups"] * n_row)
        cols = momentum.shape[1] // n_col
        hubs = n_row == 4 and n_col == 4 and rows % STRIP == 0 and cols % (2 * TILE) == 0
        return jax.shard_map(
            per_device if hubs else per_device_general,
            mesh=mesh,
            in_specs=(P(("groups", "row"), "col"),),
            out_specs=P(("groups", "row"), "col"),
            check_vma=False,
        )(momentum)

    return update
```

```python
import functools
import math

import jax
import jax.numpy as jnp
from jax import lax
from jax.experimental import pallas as pl
from jax.experimental.pallas import tpu as pltpu
from jax.sharding import PartitionSpec as P

M = 3584
N = 18432

coef_linear = 3.4445
coef_cubic = -4.775
coef_quintic = 2.0315

TILE = 256
STRIP = 128
VMEM_BYTES = 56 * 2**20

GATHERED = [[(1, 2), (1, 1), (2, 2)], [(0, 0), (3, 3), (0, 1), (3, 2)], [(0, 2), (3, 1), (0, 3)]]


def mirror(pair):
    return pair if sum(pair) == 3 and pair[0] != pair[1] else (3 - pair[0], 3 - pair[1])


def take_kernel(index, x_ref, out_ref, sq_ref):
    @pl.when(pl.program_id(0) == 0)
    def _():
        sq_ref[...] = jnp.zeros_like(sq_ref)

    x = x_ref[...]
    out_ref[...] = x.astype(jnp.bfloat16)
    sq_ref[...] += jnp.sum(x * x, axis=0, keepdims=True)


def take(momentum, index):
    rows, cols = momentum.shape
    width = cols // 2
    step = rows // 4
    return pl.pallas_call(
        take_kernel,
        grid_spec=pltpu.PrefetchScalarGridSpec(
            num_scalar_prefetch=1,
            grid=(4,),
            in_specs=[pl.BlockSpec((step, width), lambda t, index: (t, index[0]))],
            out_specs=[
                pl.BlockSpec((step, width), lambda t, index: (t, 0)),
                pl.BlockSpec((1, width), lambda t, index: (0, 0)),
            ],
        ),
        out_shape=[
            jax.ShapeDtypeStruct((rows, width), jnp.bfloat16),
            jax.ShapeDtypeStruct((1, width), jnp.float32),
        ],
        compiler_params=pltpu.CompilerParams(vmem_limit_bytes=VMEM_BYTES),
        cost_estimate=pl.CostEstimate(
            flops=2 * rows * width, bytes_accessed=6 * rows * width, transcendentals=0
        ),
        name="take_half",
    )(index, momentum)


def gram_kernel(pairs, where, pieces, has_total, split, flags, *refs):
    left, core = flags[0] == 1, flags[1]
    b, h = pl.program_id(0), pl.program_id(1)
    count = len(where) * pieces
    total = refs[count] if has_total else None
    outs = refs[count + has_total :]
    share = outs[0].shape[1]
    at = pl.multiple_of((jnp.where(h == 0, 1 - core, core) if split else h) * share, 16)

    def make(i, j):
        value = total[0] if has_total else 0.0
        for p in range(pieces):
            x, y = refs[where[i] * pieces + p], refs[where[j] * pieces + p]
            value += lax.dot_general(
                x[pl.ds(at, share), :], y[...], (((1,), (1,)), ((), ())), preferred_element_type=jnp.float32
            )
        if not split:
            outs[0][0] = value
            return

        @pl.when(h == 0)
        def _():
            outs[1][0] = value.astype(jnp.bfloat16)

        @pl.when(h == 1)
        def _():
            outs[0][0] = value.astype(jnp.bfloat16)

    for k, (i, j) in enumerate(pairs):
        if (i, j) in ((1, 2), (0, 3)):
            pl.when((b == k) & left)(functools.partial(make, j, i))
            pl.when((b == k) & jnp.logical_not(left))(functools.partial(make, i, j))
        else:
            pl.when(b == k)(functools.partial(make, i, j))


def gram_blocks(flags, pairs, operands, total=None, total_at=0, split=True):
    where = {r: k for k, r in enumerate(operands)}
    pieces = len(operands[pairs[0][0]])
    rows = operands[pairs[0][0]][0][0].shape[0]
    share = rows // 2
    used = [piece for r in operands for piece in operands[r]]
    specs = [pl.BlockSpec((rows, width), lambda b, h, flags, at=at: (0, at)) for _, width, at in used]
    arrays = [array for array, _, _ in used]
    if total is not None:
        specs.append(
            pl.BlockSpec(
                (1, share, rows),
                lambda b, h, flags: (total_at + b, jnp.where(h == 0, 1 - flags[1], flags[1]), 0),
            )
        )
        arrays.append(total)
    count = len(pairs)
    if split:
        out_specs = [pl.BlockSpec((1, share, rows), lambda b, h, flags: (b, 0, 0))] * 2
        out_shape = [jax.ShapeDtypeStruct((count, share, rows), jnp.bfloat16)] * 2
    else:
        out_specs = [pl.BlockSpec((1, share, rows), lambda b, h, flags: (b, h, 0))]
        out_shape = [jax.ShapeDtypeStruct((count, rows, rows), jnp.float32)]
    return pl.pallas_call(
        functools.partial(gram_kernel, pairs, where, pieces, int(total is not None), split),
        grid_spec=pltpu.PrefetchScalarGridSpec(
            num_scalar_prefetch=1, grid=(count, 2), in_specs=specs, out_specs=out_specs
        ),
        out_shape=out_shape,
        compiler_params=pltpu.CompilerParams(vmem_limit_bytes=VMEM_BYTES),
        cost_estimate=pl.CostEstimate(flops=0, bytes_accessed=0, transcendentals=0),
        name="gram_blocks",
    )(flags, *arrays)


def transpose_block(ref, rows, source, target):
    @pl.loop(0, rows // STRIP)
    def _(s):
        part = ref[
            pl.ds(pl.multiple_of(source[0] * rows, STRIP), rows),
            pl.ds(pl.multiple_of(source[1] * rows + s * STRIP, STRIP), STRIP),
        ]
        ref[
            pl.ds(pl.multiple_of(target[0] * rows + s * STRIP, STRIP), STRIP),
            pl.ds(pl.multiple_of(target[1] * rows, STRIP), rows),
        ] = part.T


def poly_place(core, b):
    i = jnp.where(core == 0, jnp.where(b < 4, 0, 3), jnp.where(b < 3, 1, 2))
    j = jnp.where(core == 0, jnp.where(b < 4, b, 3), jnp.where(b < 3, b + 1, b - 1))
    return i, j


def poly_kernel(flags, *refs):
    *parts, out_ref, gram, sems = refs
    rows = out_ref.shape[1]
    quarter = rows // 4
    left, core, side = flags[0], flags[1], flags[3]
    b = pl.program_id(0)

    @pl.when(b == 0)
    def _():
        places = [
            2 * core + side,
            2 * (1 - core) + side,
            2 * core + 1 - side,
            2 * (1 - core) + 1 - side,
        ]
        copies, turned = [], []
        for g, pairs in enumerate(GATHERED):
            for k, (i, j) in enumerate(pairs):
                if (i, j) in ((1, 2), (0, 3)):
                    i, j = jnp.where(left == 1, j, i), jnp.where(left == 1, i, j)
                for q, place in enumerate(places):
                    copies.append(
                        pltpu.make_async_copy(
                            parts[4 * g + q].at[k],
                            gram.at[
                                pl.ds(pl.multiple_of(i * rows + place * quarter, 16), quarter),
                                pl.ds(pl.multiple_of(j * rows, STRIP), rows),
                            ],
                            sems.at[len(copies)],
                        )
                    )
                if pairs[k][0] != pairs[k][1]:
                    turned.append((i, j))
        for copy in copies:
            copy.start()
        for copy in copies:
            copy.wait()
        for i, j in turned:
            transpose_block(gram, rows, (i, j), (j, i))

    i, j = poly_place(flags[1], b)
    at_i = pl.multiple_of(i * rows, STRIP)
    width = (rows // STRIP + 1) // 2 * STRIP
    for start in range(0, rows, width):
        size = min(width, rows - start)
        at_j = pl.multiple_of(j * rows + start, STRIP)
        squared = jnp.dot(
            gram[pl.ds(at_i, rows), :], gram[:, pl.ds(at_j, size)], preferred_element_type=jnp.float32
        )
        here = gram[pl.ds(at_i, rows), pl.ds(at_j, size)].astype(jnp.float32)
        out_ref[0, :, start : start + size] = (coef_cubic * here + coef_quintic * squared).astype(jnp.bfloat16)


def poly_blocks(flags, groups):
    rows = groups[0][0].shape[2]
    order = 4 * rows
    return pl.pallas_call(
        poly_kernel,
        grid_spec=pltpu.PrefetchScalarGridSpec(
            num_scalar_prefetch=1,
            grid=(5,),
            in_specs=[pl.BlockSpec(memory_space=pl.ANY)] * 12,
            out_specs=pl.BlockSpec((1, rows, rows), lambda b, flags: (b, 0, 0)),
            scratch_shapes=[pltpu.VMEM((order, order), jnp.bfloat16), pltpu.SemaphoreType.DMA((40,))],
        ),
        out_shape=jax.ShapeDtypeStruct((5, rows, rows), jnp.bfloat16),
        compiler_params=pltpu.CompilerParams(vmem_limit_bytes=VMEM_BYTES),
        cost_estimate=pl.CostEstimate(
            flops=10 * rows * rows * order, bytes_accessed=30 * rows * rows, transcendentals=0
        ),
        name="poly_blocks",
    )(flags, *[x for group in groups for x in group])


def product_kernel(first, starts, flags, own, pair, inverse, s1, s2, s3, *refs):
    distant, (o0, o1, o2, o3, sq_ref, poly, raw, sems) = refs[:-8], refs[-8:]
    rows = s1.shape[0]
    tile = first + pl.program_id(0)

    @pl.when(pl.program_id(0) == 0)
    def _():
        sq_ref[...] = jnp.zeros_like(sq_ref)
        copies = []
        for source, core in ((own, flags[1]), (pair, 1 - flags[1])):
            for b in range(5):
                i, j = poly_place(core, b)
                copies.append(
                    pltpu.make_async_copy(
                        source.at[b],
                        poly.at[
                            pl.ds(pl.multiple_of(i * rows, STRIP), rows),
                            pl.ds(pl.multiple_of(j * rows, STRIP), rows),
                        ],
                        sems.at[len(copies)],
                    )
                )
        for copy in copies:
            copy.start()
        for copy in copies:
            copy.wait()
        for i in range(4):
            for j in range(i + 1, 4):
                transpose_block(poly, rows, (i, j), (j, i))

    for r, s_ref in enumerate((s1, s2, s3), start=1):
        raw[r * rows : (r + 1) * rows, :] = s_ref[...]
    for piece, start, end in zip(distant, starts, starts[1:] + [1 << 30]):

        @pl.when((tile >= start) & (tile < end))
        def _(piece=piece):
            raw[:rows, :] = piece[...]

    for r, o_ref in enumerate((o0, o1, o2, o3)):
        product = jnp.dot(
            poly[r * rows : (r + 1) * rows, :], raw[...], preferred_element_type=jnp.float32
        )
        own_rows = raw[r * rows : (r + 1) * rows, :].astype(jnp.float32)
        newton = inverse[0] * (coef_linear * own_rows + product)
        sq_ref[...] += jnp.sum(newton * newton, axis=0, keepdims=True)
        o_ref[...] = newton.astype(jnp.bfloat16)


def product(flags, own, pair, inverse, blocks, distant, piece, first, tiles):
    rows = own.shape[1]
    order = 4 * rows
    here = pl.BlockSpec((rows, TILE), lambda t, flags: (0, first + t))
    pieces = [(p * piece, (p + 1) * piece) for p in range(3)]
    starts = [a // TILE for a, b in pieces]
    distant_specs = [
        pl.BlockSpec((rows, TILE), lambda t, flags, a=a // TILE, b=b // TILE: (0, jnp.clip(first + t, a, b - 1) - a))
        for a, b in pieces
    ]
    there = pl.BlockSpec((rows, TILE), lambda t, flags: (0, t))
    *newton, squares = pl.pallas_call(
        functools.partial(product_kernel, first, starts),
        grid_spec=pltpu.PrefetchScalarGridSpec(
            num_scalar_prefetch=1,
            grid=(tiles,),
            in_specs=[
                pl.BlockSpec(memory_space=pl.ANY),
                pl.BlockSpec(memory_space=pl.ANY),
                pl.BlockSpec(memory_space=pltpu.SMEM),
            ]
            + [here] * 3
            + distant_specs,
            out_specs=[there] * 4 + [pl.BlockSpec((1, TILE), lambda t, flags: (0, 0))],
            scratch_shapes=[
                pltpu.VMEM((order, order), jnp.bfloat16),
                pltpu.VMEM((order, TILE), jnp.bfloat16),
                pltpu.SemaphoreType.DMA((10,)),
            ],
        ),
        out_shape=[jax.ShapeDtypeStruct((rows, tiles * TILE), jnp.bfloat16)] * 4
        + [jax.ShapeDtypeStruct((1, TILE), jnp.float32)],
        compiler_params=pltpu.CompilerParams(vmem_limit_bytes=VMEM_BYTES),
        cost_estimate=pl.CostEstimate(
            flops=2 * order * order * tiles * TILE,
            bytes_accessed=20 * rows * rows + 4 * order * tiles * TILE,
            transcendentals=0,
        ),
        name="product",
    )(flags, own, pair, inverse, *blocks, *distant)
    return newton, jnp.sum(squares)


def finish_kernel(flags, factor, own, near, middle, far, *rest):
    out_ref = rest[-1]
    is_hub = flags[2] == 1

    @pl.when((pl.program_id(0) == 0) & is_hub)
    def _():
        out_ref[...] = own[...].astype(jnp.float32) * factor[0]

    @pl.when((pl.program_id(0) == 0) & jnp.logical_not(is_hub))
    def _():
        out_ref[...] = near[...].astype(jnp.float32) * factor[0]

    @pl.when((pl.program_id(0) == 1) & is_hub)
    def _():
        out_ref[...] = middle[...].astype(jnp.float32) * factor[0]

    @pl.when((pl.program_id(0) == 1) & jnp.logical_not(is_hub))
    def _():
        out_ref[...] = far[...].astype(jnp.float32) * factor[0]


def finish(flags, factor, parts, first, shape, before):
    rows, cols = shape
    tiles = parts[0].shape[1] // TILE
    half = cols // 2 // TILE
    near_part = pl.BlockSpec((rows, TILE), lambda p, t, flags: (0, jnp.where(p == 0, t, tiles - 1)))
    far_part = pl.BlockSpec((rows, TILE), lambda p, t, flags: (0, jnp.where(p == 0, 0, t)))
    place = pl.BlockSpec(
        (rows, TILE),
        lambda p, t, flags: (0, jnp.where(p == 0, flags[0], 1 - flags[0]) * half + first + t),
    )
    specs = [pl.BlockSpec(memory_space=pltpu.SMEM), near_part, near_part, far_part, far_part]
    operands = [flags, factor, *parts]
    aliases = {}
    if before is not None:
        specs.append(pl.BlockSpec(memory_space=pl.ANY))
        aliases = {len(operands): 0}
        operands.append(before)
    return pl.pallas_call(
        finish_kernel,
        grid_spec=pltpu.PrefetchScalarGridSpec(
            num_scalar_prefetch=1, grid=(2, tiles), in_specs=specs, out_specs=place
        ),
        out_shape=jax.ShapeDtypeStruct(shape, jnp.float32),
        input_output_aliases=aliases,
        compiler_params=pltpu.CompilerParams(vmem_limit_bytes=VMEM_BYTES),
        cost_estimate=pl.CostEstimate(
            flops=2 * rows * TILE * tiles, bytes_accessed=16 * rows * TILE * tiles, transcendentals=0
        ),
        name="finish",
    )(*operands)


def per_device(momentum):
    rows, cols = momentum.shape
    width = cols // 2
    quarter = rows // 4
    tiles = width // TILE
    z = lax.axis_index("row")
    c = lax.axis_index("col")
    core, side = c % 2, c // 2
    left = z < 2
    is_hub = (z == 1) | (z == 2)
    flags = jnp.stack([v.astype(jnp.int32) for v in (left, core, is_hub, side)])
    near_index = left.astype(jnp.int32).reshape(1)

    def over_core(x):
        return lax.ppermute(x, "col", [(k, k ^ 1) for k in range(4)])

    def over_side(x):
        return lax.ppermute(x, "col", [(k, k ^ 2) for k in range(4)])

    def between_hubs(x):
        return lax.ppermute(x, "row", [(1, 2), (2, 1)])

    def distant_permute(x):
        return lax.ppermute(x, "row", [(0, 2), (3, 1)])

    def col_total(x):
        x = jnp.broadcast_to(x, (8, 128))
        x = x + over_core(x)
        return x + over_side(x)

    far, far_sq = take(momentum, 1 - near_index)
    middle = between_hubs(far)
    near, near_sq = take(momentum, near_index)
    beside = lax.ppermute(near, "row", [(0, 1), (3, 2)])

    norm_part = col_total(jnp.sum(far_sq) + jnp.sum(near_sq))
    def added(x, y):
        return (x.astype(jnp.float32) + y.astype(jnp.float32)).astype(jnp.bfloat16)

    def over_pair(kept_sent):
        return added(kept_sent[0], over_core(kept_sent[1]))

    def over_sides(half):
        def rows_of(at):
            return lax.dynamic_slice(half, (0, at * quarter, 0), (half.shape[0], quarter, rows))

        return added(rows_of(side), over_side(rows_of(1 - side)))

    barrier = lax.optimization_barrier
    piece = width // 3
    far_pieces = [far[:, p * piece : (p + 1) * piece] for p in range(3)]
    far_pieces[0], middle, beside, norm_part = barrier((far_pieces[0], middle, beside, norm_part))
    whole = {1: [(middle, width, 0)], 2: [(near, width, 0)], 3: [(beside, width, 0)]}

    pairs_1, pairs_2 = [(1, 2), (1, 1), (2, 2)], [(3, 3), (3, 2), (3, 1)]
    pairs_3, pairs_4 = [(0, 0), (0, 1)], [(0, 2), (0, 3)]
    arrived_0 = distant_permute(far_pieces[0])
    norm_sum = (
        norm_part
        + lax.ppermute(norm_part, "row", [(0, 1), (3, 2)])
        + between_hubs(norm_part)
        + distant_permute(norm_part)
    )[0, 0]
    first = gram_blocks(flags, pairs_1, {1: whole[1], 2: whole[2]})
    arrived_0, far_pieces[1], first = barrier((arrived_0, far_pieces[1], first))

    arrived_1 = distant_permute(far_pieces[1])
    first = over_pair(first)
    second = gram_blocks(flags, pairs_2, whole)
    arrived_1, far_pieces[2], first, second, norm_sum = barrier(
        (arrived_1, far_pieces[2], first, second, norm_sum)
    )

    arrived_2 = distant_permute(far_pieces[2])
    first = over_sides(first)
    second = over_pair(second)
    distant = [arrived_0, arrived_1, arrived_2]

    def of_pieces(some):
        operands = {0: [(distant[p], piece, 0) for p in some]}
        for r, block in ((1, middle), (2, near), (3, beside)):
            operands[r] = [(block, piece, p) for p in some]
        return operands

    (late,) = gram_blocks(flags, pairs_3 + pairs_4, of_pieces([0, 1]), split=False)
    distant[2], late, first, second = barrier((distant[2], late, first, second))

    other_first = between_hubs(first)
    second = over_sides(second)
    last = of_pieces([2])
    third = over_pair(gram_blocks(flags, pairs_3, {r: last[r] for r in (0, 1)}, total=late))
    fourth = over_pair(
        gram_blocks(flags, pairs_4, {r: last[r] for r in (0, 2, 3)}, total=late, total_at=2)
    )
    other_first, fourth = barrier((other_first, fourth))
    other_second = between_hubs(second)
    third = over_sides(third)
    fourth = over_sides(fourth)
    other_second, fourth = barrier((other_second, fourth))
    other_third = between_hubs(third)
    other_fourth = between_hubs(fourth)

    spectral_edge = 1.0 + math.sqrt(M / N)
    inverse = 1.0 / (jnp.sqrt(norm_sum / M) * spectral_edge + 1e-07)

    mine, other = {}, {}

    def known(pairs, summed, received):
        for k, pair in enumerate(pairs):
            mine[pair], other[mirror(pair)] = summed[k], received[k]

    def gather(pairs):
        total = jnp.stack([mine[pair].astype(jnp.float32) + other[pair].astype(jnp.float32) for pair in pairs])
        here = (total * (inverse * inverse)).astype(jnp.bfloat16)
        across = over_side(here)
        return [here, over_core(here), across, over_core(across)]

    known(pairs_1, first, other_first)
    groups = [gather(GATHERED[0])]
    known(pairs_2, second, other_second)
    known(pairs_3, third, other_third)
    groups.append(gather(GATHERED[1]))
    groups[0], other_fourth = barrier((groups[0], other_fourth))
    known(pairs_4, fourth, other_fourth)
    groups.append(gather(GATHERED[2]))

    own = poly_blocks(flags, groups)
    pair = over_core(own)

    bounds = sorted({0, tiles * 2 // 9, tiles * 5 // 9, tiles})
    newton_sq = jnp.float32(0.0)
    scale = inverse.reshape(1)
    parts = []
    for first, last in zip(bounds[:-1], bounds[1:]):
        newton, squares = product(flags, own, pair, scale, (middle, near, beside), distant, piece, first, last - first)
        newton_sq += squares
        if last == tiles:
            hub_sq = col_total(newton_sq)
            total_sq = (
                jnp.where(is_hub, hub_sq, 0.0)
                + lax.ppermute(hub_sq, "row", [(1, 0), (2, 3)])
                + between_hubs(hub_sq)
                + lax.ppermute(hub_sq, "row", [(2, 0), (1, 3)])
            )[0, 0]
            newton, total_sq, parts[-1] = barrier((newton, total_sq, parts[-1]))
        part = (
            newton[2],
            lax.ppermute(newton[3], "row", [(1, 0), (2, 3)]),
            between_hubs(newton[1]),
            lax.ppermute(newton[0], "row", [(2, 0), (1, 3)]),
        )
        if last == tiles:
            pass
        elif parts:
            parts[-1], scale, newton_sq = barrier((parts[-1], scale, newton_sq))
        else:
            scale, newton_sq = barrier((scale, newton_sq))
        parts.append(part)
    factor = (1.0 / (jnp.sqrt(total_sq) / math.sqrt(M * N) + 1e-07)).reshape(1)
    out = None
    for first, part in zip(bounds[:-1], parts):
        out = finish(flags, factor, part, first, (rows, cols), out)
    return out


def per_device_general(momentum):
    norm_sum = lax.psum(jnp.sum(momentum * momentum), ("col", "row"))
    spectral_edge = 1.0 + math.sqrt(M / N)
    scaled = (momentum / (jnp.sqrt(norm_sum / M) * spectral_edge + 1e-07)).astype(jnp.bfloat16)
    columns = lax.all_gather(scaled, "row", axis=0, tiled=True)
    gram_tile = lax.psum_scatter(
        lax.dot_general(
            columns, scaled, (((1,), (1,)), ((), ())), preferred_element_type=jnp.float32
        ).astype(jnp.bfloat16),
        "col",
        scatter_dimension=0,
        tiled=True,
    )
    left_rows = lax.all_gather(gram_tile, "row", axis=1, tiled=True)
    squared = jnp.dot(
        left_rows,
        lax.all_gather(gram_tile, "col", axis=0, tiled=True),
        preferred_element_type=jnp.float32,
    )
    poly = (coef_cubic * gram_tile.astype(jnp.float32) + coef_quintic * squared).astype(jnp.bfloat16)
    product = lax.dot_general(
        lax.all_gather(poly, "col", axis=0, tiled=True),
        columns,
        (((0,), (0,)), ((), ())),
        preferred_element_type=jnp.float32,
    )
    newton = coef_linear * scaled.astype(jnp.float32) + product
    newton_sq = lax.psum(jnp.sum(newton * newton), ("col", "row"))
    update_rms = jnp.sqrt(newton_sq) / math.sqrt(M * N)
    return newton / (update_rms + 1e-07)


def solution(mesh):
    def update(momentum):
        n_row, n_col = mesh.shape["row"], mesh.shape["col"]
        rows = momentum.shape[0] // (mesh.shape["groups"] * n_row)
        cols = momentum.shape[1] // n_col
        hubs = n_row == 4 and n_col == 4 and rows % STRIP == 0 and cols % (6 * TILE) == 0
        return jax.shard_map(
            per_device if hubs else per_device_general,
            mesh=mesh,
            in_specs=(P(("groups", "row"), "col"),),
            out_specs=P(("groups", "row"), "col"),
            check_vma=False,
        )(momentum)

    return update
```

```python
import functools
import math

import jax
import jax.numpy as jnp
from jax import lax
from jax.experimental import pallas as pl
from jax.experimental.pallas import tpu as pltpu
from jax.sharding import PartitionSpec as P

M = 3584
N = 18432

coef_linear = 3.4445
coef_cubic = -4.775
coef_quintic = 2.0315

TILE = 256
STRIP = 128
VMEM_BYTES = 56 * 2**20

GATHERED = [[(1, 2), (1, 1), (2, 2)], [(0, 0), (3, 3), (0, 1), (3, 2)], [(0, 2), (3, 1), (0, 3)]]


def mirror(pair):
    return pair if sum(pair) == 3 and pair[0] != pair[1] else (3 - pair[0], 3 - pair[1])


def take_kernel(index, x_ref, out_ref, sq_ref):
    @pl.when(pl.program_id(0) == 0)
    def _():
        sq_ref[...] = jnp.zeros_like(sq_ref)

    x = x_ref[...]
    out_ref[...] = x.astype(jnp.bfloat16)
    sq_ref[...] += jnp.sum(x * x, axis=0, keepdims=True)


def take(momentum, index):
    rows, cols = momentum.shape
    width = cols // 2
    step = rows // 4
    return pl.pallas_call(
        take_kernel,
        grid_spec=pltpu.PrefetchScalarGridSpec(
            num_scalar_prefetch=1,
            grid=(4,),
            in_specs=[pl.BlockSpec((step, width), lambda t, index: (t, index[0]))],
            out_specs=[
                pl.BlockSpec((step, width), lambda t, index: (t, 0)),
                pl.BlockSpec((1, width), lambda t, index: (0, 0)),
            ],
        ),
        out_shape=[
            jax.ShapeDtypeStruct((rows, width), jnp.bfloat16),
            jax.ShapeDtypeStruct((1, width), jnp.float32),
        ],
        compiler_params=pltpu.CompilerParams(vmem_limit_bytes=VMEM_BYTES),
        cost_estimate=pl.CostEstimate(
            flops=2 * rows * width, bytes_accessed=6 * rows * width, transcendentals=0
        ),
        name="take_half",
    )(index, momentum)


def gram_kernel(pairs, where, pieces, has_total, split, flags, *refs):
    left, core = flags[0] == 1, flags[1]
    b, h = pl.program_id(0), pl.program_id(1)
    count = len(where) * pieces
    total = refs[count] if has_total else None
    outs = refs[count + has_total :]
    share = outs[0].shape[1]
    at = pl.multiple_of((jnp.where(h == 0, 1 - core, core) if split else h) * share, 16)

    def make(i, j):
        value = total[0] if has_total else 0.0
        for p in range(pieces):
            x, y = refs[where[i] * pieces + p], refs[where[j] * pieces + p]
            value += lax.dot_general(
                x[pl.ds(at, share), :], y[...], (((1,), (1,)), ((), ())), preferred_element_type=jnp.float32
            )
        if not split:
            outs[0][0] = value
            return

        @pl.when(h == 0)
        def _():
            outs[1][0] = value.astype(jnp.bfloat16)

        @pl.when(h == 1)
        def _():
            outs[0][0] = value.astype(jnp.bfloat16)

    for k, (i, j) in enumerate(pairs):
        if (i, j) in ((1, 2), (0, 3)):
            pl.when((b == k) & left)(functools.partial(make, j, i))
            pl.when((b == k) & jnp.logical_not(left))(functools.partial(make, i, j))
        else:
            pl.when(b == k)(functools.partial(make, i, j))


def gram_blocks(flags, pairs, operands, total=None, total_at=0, split=True):
    where = {r: k for k, r in enumerate(operands)}
    pieces = len(operands[pairs[0][0]])
    rows = operands[pairs[0][0]][0][0].shape[0]
    share = rows // 2
    used = [piece for r in operands for piece in operands[r]]
    specs = [pl.BlockSpec((rows, width), lambda b, h, flags, at=at: (0, at)) for _, width, at in used]
    arrays = [array for array, _, _ in used]
    if total is not None:
        specs.append(
            pl.BlockSpec(
                (1, share, rows),
                lambda b, h, flags: (total_at + b, jnp.where(h == 0, 1 - flags[1], flags[1]), 0),
            )
        )
        arrays.append(total)
    count = len(pairs)
    if split:
        out_specs = [pl.BlockSpec((1, share, rows), lambda b, h, flags: (b, 0, 0))] * 2
        out_shape = [jax.ShapeDtypeStruct((count, share, rows), jnp.bfloat16)] * 2
    else:
        out_specs = [pl.BlockSpec((1, share, rows), lambda b, h, flags: (b, h, 0))]
        out_shape = [jax.ShapeDtypeStruct((count, rows, rows), jnp.float32)]
    return pl.pallas_call(
        functools.partial(gram_kernel, pairs, where, pieces, int(total is not None), split),
        grid_spec=pltpu.PrefetchScalarGridSpec(
            num_scalar_prefetch=1, grid=(count, 2), in_specs=specs, out_specs=out_specs
        ),
        out_shape=out_shape,
        compiler_params=pltpu.CompilerParams(vmem_limit_bytes=VMEM_BYTES),
        cost_estimate=pl.CostEstimate(flops=0, bytes_accessed=0, transcendentals=0),
        name="gram_blocks",
    )(flags, *arrays)


def transpose_block(ref, rows, source, target):
    @pl.loop(0, rows // STRIP)
    def _(s):
        part = ref[
            pl.ds(pl.multiple_of(source[0] * rows, STRIP), rows),
            pl.ds(pl.multiple_of(source[1] * rows + s * STRIP, STRIP), STRIP),
        ]
        ref[
            pl.ds(pl.multiple_of(target[0] * rows + s * STRIP, STRIP), STRIP),
            pl.ds(pl.multiple_of(target[1] * rows, STRIP), rows),
        ] = part.T


def poly_place(core, b):
    i = jnp.where(core == 0, jnp.where(b < 4, 0, 3), jnp.where(b < 3, 1, 2))
    j = jnp.where(core == 0, jnp.where(b < 4, b, 3), jnp.where(b < 3, b + 1, b - 1))
    return i, j


def poly_kernel(flags, *refs):
    *parts, out_ref, gram, sems = refs
    rows = out_ref.shape[1]
    quarter = rows // 4
    left, core, side = flags[0], flags[1], flags[3]
    b = pl.program_id(0)

    @pl.when(b == 0)
    def _():
        places = [
            2 * core + side,
            2 * (1 - core) + side,
            2 * core + 1 - side,
            2 * (1 - core) + 1 - side,
        ]
        copies, turned = [], []
        for g, pairs in enumerate(GATHERED):
            for k, (i, j) in enumerate(pairs):
                if (i, j) in ((1, 2), (0, 3)):
                    i, j = jnp.where(left == 1, j, i), jnp.where(left == 1, i, j)
                for q, place in enumerate(places):
                    copies.append(
                        pltpu.make_async_copy(
                            parts[4 * g + q].at[k],
                            gram.at[
                                pl.ds(pl.multiple_of(i * rows + place * quarter, 16), quarter),
                                pl.ds(pl.multiple_of(j * rows, STRIP), rows),
                            ],
                            sems.at[len(copies)],
                        )
                    )
                if pairs[k][0] != pairs[k][1]:
                    turned.append((i, j))
        for copy in copies:
            copy.start()
        for copy in copies:
            copy.wait()
        for i, j in turned:
            transpose_block(gram, rows, (i, j), (j, i))

    i, j = poly_place(flags[1], b)
    at_i = pl.multiple_of(i * rows, STRIP)
    width = (rows // STRIP + 1) // 2 * STRIP
    for start in range(0, rows, width):
        size = min(width, rows - start)
        at_j = pl.multiple_of(j * rows + start, STRIP)
        squared = jnp.dot(
            gram[pl.ds(at_i, rows), :], gram[:, pl.ds(at_j, size)], preferred_element_type=jnp.float32
        )
        here = gram[pl.ds(at_i, rows), pl.ds(at_j, size)].astype(jnp.float32)
        out_ref[0, :, start : start + size] = (coef_cubic * here + coef_quintic * squared).astype(jnp.bfloat16)


def poly_blocks(flags, groups):
    rows = groups[0][0].shape[2]
    order = 4 * rows
    return pl.pallas_call(
        poly_kernel,
        grid_spec=pltpu.PrefetchScalarGridSpec(
            num_scalar_prefetch=1,
            grid=(5,),
            in_specs=[pl.BlockSpec(memory_space=pl.ANY)] * 12,
            out_specs=pl.BlockSpec((1, rows, rows), lambda b, flags: (b, 0, 0)),
            scratch_shapes=[pltpu.VMEM((order, order), jnp.bfloat16), pltpu.SemaphoreType.DMA((40,))],
        ),
        out_shape=jax.ShapeDtypeStruct((5, rows, rows), jnp.bfloat16),
        compiler_params=pltpu.CompilerParams(vmem_limit_bytes=VMEM_BYTES),
        cost_estimate=pl.CostEstimate(
            flops=10 * rows * rows * order, bytes_accessed=30 * rows * rows, transcendentals=0
        ),
        name="poly_blocks",
    )(flags, *[x for group in groups for x in group])


def product_kernel(first, strips, flags, own, pair, inverse, s1, s2, s3, *refs):
    distant, (o0, o1, o2, o3, sq_ref, poly, raw, sems) = refs[:-8], refs[-8:]
    rows = s1.shape[0]
    tile = first + pl.program_id(0)

    @pl.when(pl.program_id(0) == 0)
    def _():
        sq_ref[...] = jnp.zeros_like(sq_ref)
        copies = []
        for source, core in ((own, flags[1]), (pair, 1 - flags[1])):
            for b in range(5):
                i, j = poly_place(core, b)
                copies.append(
                    pltpu.make_async_copy(
                        source.at[b],
                        poly.at[
                            pl.ds(pl.multiple_of(i * rows, STRIP), rows),
                            pl.ds(pl.multiple_of(j * rows, STRIP), rows),
                        ],
                        sems.at[len(copies)],
                    )
                )
        for copy in copies:
            copy.start()
        for copy in copies:
            copy.wait()
        for i in range(4):
            for j in range(i + 1, 4):
                transpose_block(poly, rows, (i, j), (j, i))

    for r, s_ref in enumerate((s1, s2, s3), start=1):
        raw[r * rows : (r + 1) * rows, :] = s_ref[...]
    for k, strip in enumerate(distant):
        side, p = divmod(k, 2)

        @pl.when((2 * tile + side >= strips) == (p == 1))
        def _(side=side, strip=strip):
            raw[:rows, side * STRIP : (side + 1) * STRIP] = strip[...]

    for r, o_ref in enumerate((o0, o1, o2, o3)):
        product = jnp.dot(
            poly[r * rows : (r + 1) * rows, :], raw[...], preferred_element_type=jnp.float32
        )
        own_rows = raw[r * rows : (r + 1) * rows, :].astype(jnp.float32)
        newton = inverse[0] * (coef_linear * own_rows + product)
        sq_ref[...] += jnp.sum(newton * newton, axis=0, keepdims=True)
        o_ref[...] = newton.astype(jnp.bfloat16)


def product(flags, own, pair, inverse, blocks, distant, piece, first, tiles):
    rows = own.shape[1]
    order = 4 * rows
    here = pl.BlockSpec((rows, TILE), lambda t, flags: (0, first + t))
    strips = piece // STRIP
    distant_specs = [
        pl.BlockSpec(
            (rows, STRIP),
            lambda t, flags, start=p * strips, side=side: (
                0,
                jnp.clip(2 * (first + t) + side - start, 0, strips - 1),
            ),
        )
        for side in range(2)
        for p in range(2)
    ]
    there = pl.BlockSpec((rows, TILE), lambda t, flags: (0, t))
    *newton, squares = pl.pallas_call(
        functools.partial(product_kernel, first, strips),
        grid_spec=pltpu.PrefetchScalarGridSpec(
            num_scalar_prefetch=1,
            grid=(tiles,),
            in_specs=[
                pl.BlockSpec(memory_space=pl.ANY),
                pl.BlockSpec(memory_space=pl.ANY),
                pl.BlockSpec(memory_space=pltpu.SMEM),
            ]
            + [here] * 3
            + distant_specs,
            out_specs=[there] * 4 + [pl.BlockSpec((1, TILE), lambda t, flags: (0, 0))],
            scratch_shapes=[
                pltpu.VMEM((order, order), jnp.bfloat16),
                pltpu.VMEM((order, TILE), jnp.bfloat16),
                pltpu.SemaphoreType.DMA((10,)),
            ],
        ),
        out_shape=[jax.ShapeDtypeStruct((rows, tiles * TILE), jnp.bfloat16)] * 4
        + [jax.ShapeDtypeStruct((1, TILE), jnp.float32)],
        compiler_params=pltpu.CompilerParams(vmem_limit_bytes=VMEM_BYTES),
        cost_estimate=pl.CostEstimate(
            flops=2 * order * order * tiles * TILE,
            bytes_accessed=20 * rows * rows + 4 * order * tiles * TILE,
            transcendentals=0,
        ),
        name="product",
    )(flags, own, pair, inverse, *blocks, *distant, *distant)
    return newton, jnp.sum(squares)


def finish_kernel(flags, factor, own, near, middle, far, *rest):
    out_ref = rest[-1]
    is_hub = flags[2] == 1

    @pl.when((pl.program_id(0) == 0) & is_hub)
    def _():
        out_ref[...] = own[...].astype(jnp.float32) * factor[0]

    @pl.when((pl.program_id(0) == 0) & jnp.logical_not(is_hub))
    def _():
        out_ref[...] = near[...].astype(jnp.float32) * factor[0]

    @pl.when((pl.program_id(0) == 1) & is_hub)
    def _():
        out_ref[...] = middle[...].astype(jnp.float32) * factor[0]

    @pl.when((pl.program_id(0) == 1) & jnp.logical_not(is_hub))
    def _():
        out_ref[...] = far[...].astype(jnp.float32) * factor[0]


def finish(flags, factor, parts, first, shape, before):
    rows, cols = shape
    tiles = parts[0].shape[1] // TILE
    half = cols // 2 // TILE
    near_part = pl.BlockSpec((rows, TILE), lambda p, t, flags: (0, jnp.where(p == 0, t, tiles - 1)))
    far_part = pl.BlockSpec((rows, TILE), lambda p, t, flags: (0, jnp.where(p == 0, 0, t)))
    place = pl.BlockSpec(
        (rows, TILE),
        lambda p, t, flags: (0, jnp.where(p == 0, flags[0], 1 - flags[0]) * half + first + t),
    )
    specs = [pl.BlockSpec(memory_space=pltpu.SMEM), near_part, near_part, far_part, far_part]
    operands = [flags, factor, *parts]
    aliases = {}
    if before is not None:
        specs.append(pl.BlockSpec(memory_space=pl.ANY))
        aliases = {len(operands): 0}
        operands.append(before)
    return pl.pallas_call(
        finish_kernel,
        grid_spec=pltpu.PrefetchScalarGridSpec(
            num_scalar_prefetch=1, grid=(2, tiles), in_specs=specs, out_specs=place
        ),
        out_shape=jax.ShapeDtypeStruct(shape, jnp.float32),
        input_output_aliases=aliases,
        compiler_params=pltpu.CompilerParams(vmem_limit_bytes=VMEM_BYTES),
        cost_estimate=pl.CostEstimate(
            flops=2 * rows * TILE * tiles, bytes_accessed=16 * rows * TILE * tiles, transcendentals=0
        ),
        name="finish",
    )(*operands)


def per_device(momentum):
    rows, cols = momentum.shape
    width = cols // 2
    quarter = rows // 4
    tiles = width // TILE
    z = lax.axis_index("row")
    c = lax.axis_index("col")
    core, side = c % 2, c // 2
    left = z < 2
    is_hub = (z == 1) | (z == 2)
    flags = jnp.stack([v.astype(jnp.int32) for v in (left, core, is_hub, side)])
    near_index = left.astype(jnp.int32).reshape(1)

    def over_core(x):
        return lax.ppermute(x, "col", [(k, k ^ 1) for k in range(4)])

    def over_side(x):
        return lax.ppermute(x, "col", [(k, k ^ 2) for k in range(4)])

    def between_hubs(x):
        return lax.ppermute(x, "row", [(1, 2), (2, 1)])

    def distant_permute(x):
        return lax.ppermute(x, "row", [(0, 2), (3, 1)])

    def col_total(x):
        x = jnp.broadcast_to(x, (8, 128))
        x = x + over_core(x)
        return x + over_side(x)

    near, near_sq = take(momentum, near_index)
    beside = lax.ppermute(near, "row", [(0, 1), (3, 2)])
    far, far_sq = take(momentum, 1 - near_index)
    middle = between_hubs(far)
    norm_part = col_total(jnp.sum(far_sq) + jnp.sum(near_sq))

    def added(x, y):
        return (x.astype(jnp.float32) + y.astype(jnp.float32)).astype(jnp.bfloat16)

    def over_pair(kept_sent):
        return added(kept_sent[0], over_core(kept_sent[1]))

    def over_sides(half):
        def rows_of(at):
            return lax.dynamic_slice(half, (0, at * quarter, 0), (half.shape[0], quarter, rows))

        return added(rows_of(side), over_side(rows_of(1 - side)))

    barrier = lax.optimization_barrier
    piece = width // 2
    far_first, beside, norm_part = barrier((far[:, :piece], beside, norm_part))
    arrived = distant_permute(far_first)
    whole = {1: [(middle, width, 0)], 2: [(near, width, 0)], 3: [(beside, width, 0)]}
    pairs_1, pairs_2 = [(2, 2), (3, 3), (3, 2)], [(1, 2), (1, 1), (3, 1)]
    pairs_3, pairs_4 = [(0, 0), (0, 1)], [(0, 2), (0, 3)]
    first = gram_blocks(flags, pairs_1, {r: whole[r] for r in (2, 3)})
    second = gram_blocks(flags, pairs_2, whole)
    arrived, far_second, first, second = barrier((arrived, far[:, piece:], first, second))

    def halves(h):
        blocks = {1: middle, 2: near, 3: beside}
        return {0: [(distant[h], piece, 0)]} | {r: [(blocks[r], piece, h)] for r in blocks}

    distant = [arrived, distant_permute(far_second)]
    first = over_pair(first)
    second = over_pair(second)
    (late,) = gram_blocks(flags, pairs_3 + pairs_4, halves(0), split=False)
    first = over_sides(first)
    distant[1], late, first, second, norm_part = barrier((distant[1], late, first, second, norm_part))

    norm_sum = (
        norm_part
        + lax.ppermute(norm_part, "row", [(0, 1), (3, 2)])
        + between_hubs(norm_part)
        + distant_permute(norm_part)
    )[0, 0]
    other_first = between_hubs(first)
    second = over_sides(second)
    third = gram_blocks(flags, pairs_3, {r: halves(1)[r] for r in (0, 1)}, total=late)
    fourth = gram_blocks(flags, pairs_4, {r: halves(1)[r] for r in (0, 2, 3)}, total=late, total_at=2)
    other_first, second, fourth = barrier((other_first, second, fourth))
    other_second = between_hubs(second)
    third = over_sides(over_pair(third))
    norm_sum, third = barrier((norm_sum, third))
    other_third = between_hubs(third)
    fourth = over_sides(over_pair(fourth))
    other_second, fourth = barrier((other_second, fourth))
    other_fourth = between_hubs(fourth)

    spectral_edge = 1.0 + math.sqrt(M / N)
    inverse = 1.0 / (jnp.sqrt(norm_sum / M) * spectral_edge + 1e-07)

    mine, other = {}, {}

    def known(pairs, summed, received):
        for k, pair in enumerate(pairs):
            mine[pair], other[mirror(pair)] = summed[k], received[k]

    def gather(pairs):
        total = jnp.stack([mine[pair].astype(jnp.float32) + other[pair].astype(jnp.float32) for pair in pairs])
        here = (total * (inverse * inverse)).astype(jnp.bfloat16)
        across = over_side(here)
        return [here, over_core(here), across, over_core(across)]

    known(pairs_1, first, other_first)
    known(pairs_2, second, other_second)
    groups = [gather(GATHERED[0])]
    groups[0][1], groups[0][2], other_third = barrier((groups[0][1], groups[0][2], other_third))
    known(pairs_3, third, other_third)
    groups.append(gather(GATHERED[1]))
    groups[1][1], other_fourth = barrier((groups[1][1], other_fourth))
    known(pairs_4, fourth, other_fourth)
    groups.append(gather(GATHERED[2]))

    own = poly_blocks(flags, groups)
    pair = over_core(own)

    bounds = sorted({0, tiles * 2 // 9, tiles * 5 // 9, tiles * 7 // 9, tiles})
    newton_sq = jnp.float32(0.0)
    scale = inverse.reshape(1)
    parts = []
    for first, last in zip(bounds[:-1], bounds[1:]):
        newton, squares = product(flags, own, pair, scale, (middle, near, beside), distant, piece, first, last - first)
        newton_sq += squares
        if last == tiles:
            hub_sq = col_total(newton_sq)
            total_sq = (
                jnp.where(is_hub, hub_sq, 0.0)
                + lax.ppermute(hub_sq, "row", [(1, 0), (2, 3)])
                + between_hubs(hub_sq)
                + lax.ppermute(hub_sq, "row", [(2, 0), (1, 3)])
            )[0, 0]
            newton, total_sq, parts[-1] = barrier((newton, total_sq, parts[-1]))
        part = (
            newton[2],
            lax.ppermute(newton[3], "row", [(1, 0), (2, 3)]),
            between_hubs(newton[1]),
            lax.ppermute(newton[0], "row", [(2, 0), (1, 3)]),
        )
        if last == tiles:
            pass
        elif parts:
            parts[-1], scale, newton_sq = barrier((parts[-1], scale, newton_sq))
        else:
            scale, newton_sq = barrier((scale, newton_sq))
        parts.append(part)
    factor = (1.0 / (jnp.sqrt(total_sq) / math.sqrt(M * N) + 1e-07)).reshape(1)
    out = None
    for first, part in zip(bounds[:-1], parts):
        out = finish(flags, factor, part, first, (rows, cols), out)
    return out


def per_device_general(momentum):
    norm_sum = lax.psum(jnp.sum(momentum * momentum), ("col", "row"))
    spectral_edge = 1.0 + math.sqrt(M / N)
    scaled = (momentum / (jnp.sqrt(norm_sum / M) * spectral_edge + 1e-07)).astype(jnp.bfloat16)
    columns = lax.all_gather(scaled, "row", axis=0, tiled=True)
    gram_tile = lax.psum_scatter(
        lax.dot_general(
            columns, scaled, (((1,), (1,)), ((), ())), preferred_element_type=jnp.float32
        ).astype(jnp.bfloat16),
        "col",
        scatter_dimension=0,
        tiled=True,
    )
    left_rows = lax.all_gather(gram_tile, "row", axis=1, tiled=True)
    squared = jnp.dot(
        left_rows,
        lax.all_gather(gram_tile, "col", axis=0, tiled=True),
        preferred_element_type=jnp.float32,
    )
    poly = (coef_cubic * gram_tile.astype(jnp.float32) + coef_quintic * squared).astype(jnp.bfloat16)
    product = lax.dot_general(
        lax.all_gather(poly, "col", axis=0, tiled=True),
        columns,
        (((0,), (0,)), ((), ())),
        preferred_element_type=jnp.float32,
    )
    newton = coef_linear * scaled.astype(jnp.float32) + product
    newton_sq = lax.psum(jnp.sum(newton * newton), ("col", "row"))
    update_rms = jnp.sqrt(newton_sq) / math.sqrt(M * N)
    return newton / (update_rms + 1e-07)


def solution(mesh):
    def update(momentum):
        n_row, n_col = mesh.shape["row"], mesh.shape["col"]
        rows = momentum.shape[0] // (mesh.shape["groups"] * n_row)
        cols = momentum.shape[1] // n_col
        hubs = n_row == 4 and n_col == 4 and rows % STRIP == 0 and cols % (2 * TILE) == 0
        return jax.shard_map(
            per_device if hubs else per_device_general,
            mesh=mesh,
            in_specs=(P(("groups", "row"), "col"),),
            out_specs=P(("groups", "row"), "col"),
            check_vma=False,
        )(momentum)

    return update
```

```python
import functools
import math

import jax
import jax.numpy as jnp
from jax import lax
from jax.experimental import pallas as pl
from jax.experimental.pallas import tpu as pltpu
from jax.sharding import PartitionSpec as P

M = 3584
N = 18432

coef_linear = 3.4445
coef_cubic = -4.775
coef_quintic = 2.0315

TILE = 256
STRIP = 128
VMEM_BYTES = 56 * 2**20

GATHERED = [[(1, 2), (1, 1), (2, 2)], [(0, 0), (3, 3), (0, 1), (3, 2)], [(0, 2), (3, 1), (0, 3)]]


def mirror(pair):
    return pair if sum(pair) == 3 and pair[0] != pair[1] else (3 - pair[0], 3 - pair[1])


def take_kernel(index, near_ref, far_ref, near_out, far_out, sq_ref):
    @pl.when(pl.program_id(0) == 0)
    def _():
        sq_ref[...] = jnp.zeros_like(sq_ref)

    near, far = near_ref[...], far_ref[...]
    near_out[...] = near.astype(jnp.bfloat16)
    far_out[...] = far.astype(jnp.bfloat16)
    sq_ref[...] += jnp.sum(near * near + far * far, axis=0, keepdims=True)


def take(momentum, index):
    rows, cols = momentum.shape
    width = cols // 2
    step = rows // 8
    half = jax.ShapeDtypeStruct((rows, width), jnp.bfloat16)
    return pl.pallas_call(
        take_kernel,
        grid_spec=pltpu.PrefetchScalarGridSpec(
            num_scalar_prefetch=1,
            grid=(8,),
            in_specs=[
                pl.BlockSpec((step, width), lambda t, index: (t, index[0])),
                pl.BlockSpec((step, width), lambda t, index: (t, 1 - index[0])),
            ],
            out_specs=[
                pl.BlockSpec((step, width), lambda t, index: (t, 0)),
                pl.BlockSpec((step, width), lambda t, index: (t, 0)),
                pl.BlockSpec((1, width), lambda t, index: (0, 0)),
            ],
        ),
        out_shape=[half, half, jax.ShapeDtypeStruct((1, width), jnp.float32)],
        compiler_params=pltpu.CompilerParams(vmem_limit_bytes=VMEM_BYTES),
        cost_estimate=pl.CostEstimate(
            flops=4 * rows * width, bytes_accessed=12 * rows * width, transcendentals=0
        ),
        name="take_halves",
    )(index, momentum, momentum)


def gram_kernel(pairs, where, pieces, has_total, split, flags, *refs):
    left, core = flags[0] == 1, flags[1]
    b = pl.program_id(0)
    count = len(where) * pieces
    total = refs[count] if has_total else None
    outs = refs[count + has_total :]

    def make(i, j):
        value = total[0] if has_total else 0.0
        for p in range(pieces):
            x, y = refs[where[i] * pieces + p], refs[where[j] * pieces + p]
            value += lax.dot_general(
                x[...], y[...], (((1,), (1,)), ((), ())), preferred_element_type=jnp.float32
            )
        if not split:
            outs[0][0] = value
            return
        keep, send, whole = outs
        share = keep.shape[1]
        whole[...] = value.astype(jnp.bfloat16)
        keep[0] = whole[pl.ds(pl.multiple_of(core * share, 16), share), :]
        send[0] = whole[pl.ds(pl.multiple_of((1 - core) * share, 16), share), :]

    for k, (i, j) in enumerate(pairs):
        if (i, j) in ((1, 2), (0, 3)):
            pl.when((b == k) & left)(functools.partial(make, j, i))
            pl.when((b == k) & jnp.logical_not(left))(functools.partial(make, i, j))
        else:
            pl.when(b == k)(functools.partial(make, i, j))


def gram_blocks(flags, pairs, operands, total=None, total_at=0, split=True):
    where = {r: k for k, r in enumerate(operands)}
    pieces = len(operands[pairs[0][0]])
    rows = operands[pairs[0][0]][0][0].shape[0]
    share = rows // 2
    used = [piece for r in operands for piece in operands[r]]
    specs = [pl.BlockSpec((rows, width), lambda b, flags, at=at: (0, at)) for _, width, at in used]
    arrays = [array for array, _, _ in used]
    if total is not None:
        specs.append(
            pl.BlockSpec(
                (1, rows, rows), lambda b, flags: (total_at + b, 0, 0)
            )
        )
        arrays.append(total)
    count = len(pairs)
    if split:
        out_specs = [pl.BlockSpec((1, share, rows), lambda b, flags: (b, 0, 0))] * 2
        scratch = [pltpu.VMEM((rows, rows), jnp.bfloat16)]
        out_shape = [jax.ShapeDtypeStruct((count, share, rows), jnp.bfloat16)] * 2
    else:
        out_specs = [pl.BlockSpec((1, rows, rows), lambda b, flags: (b, 0, 0))]
        scratch = []
        out_shape = [jax.ShapeDtypeStruct((count, rows, rows), jnp.float32)]
    return pl.pallas_call(
        functools.partial(gram_kernel, pairs, where, pieces, int(total is not None), split),
        grid_spec=pltpu.PrefetchScalarGridSpec(
            num_scalar_prefetch=1, grid=(count,), in_specs=specs, out_specs=out_specs, scratch_shapes=scratch
        ),
        out_shape=out_shape,
        compiler_params=pltpu.CompilerParams(vmem_limit_bytes=VMEM_BYTES),
        cost_estimate=pl.CostEstimate(flops=0, bytes_accessed=0, transcendentals=0),
        name="gram_blocks",
    )(flags, *arrays)


def transpose_block(ref, rows, source, target):
    @pl.loop(0, rows // STRIP)
    def _(s):
        part = ref[
            pl.ds(pl.multiple_of(source[0] * rows, STRIP), rows),
            pl.ds(pl.multiple_of(source[1] * rows + s * STRIP, STRIP), STRIP),
        ]
        ref[
            pl.ds(pl.multiple_of(target[0] * rows + s * STRIP, STRIP), STRIP),
            pl.ds(pl.multiple_of(target[1] * rows, STRIP), rows),
        ] = part.T


def poly_place(core, b):
    i = jnp.where(core == 0, jnp.where(b < 4, 0, 3), jnp.where(b < 3, 1, 2))
    j = jnp.where(core == 0, jnp.where(b < 4, b, 3), jnp.where(b < 3, b + 1, b - 1))
    return i, j


def poly_kernel(flags, *refs):
    *parts, out_ref, gram, sems = refs
    rows = out_ref.shape[1]
    quarter = rows // 4
    left, core, side = flags[0], flags[1], flags[3]
    b = pl.program_id(0)

    @pl.when(b == 0)
    def _():
        places = [
            2 * core + side,
            2 * (1 - core) + side,
            2 * core + 1 - side,
            2 * (1 - core) + 1 - side,
        ]
        copies, turned = [], []
        for g, pairs in enumerate(GATHERED):
            for k, (i, j) in enumerate(pairs):
                if (i, j) in ((1, 2), (0, 3)):
                    i, j = jnp.where(left == 1, j, i), jnp.where(left == 1, i, j)
                for q, place in enumerate(places):
                    copies.append(
                        pltpu.make_async_copy(
                            parts[4 * g + q].at[k],
                            gram.at[
                                pl.ds(pl.multiple_of(i * rows + place * quarter, 16), quarter),
                                pl.ds(pl.multiple_of(j * rows, STRIP), rows),
                            ],
                            sems.at[len(copies)],
                        )
                    )
                if pairs[k][0] != pairs[k][1]:
                    turned.append((i, j))
        for copy in copies:
            copy.start()
        for copy in copies:
            copy.wait()
        for i, j in turned:
            transpose_block(gram, rows, (i, j), (j, i))

    i, j = poly_place(flags[1], b)
    at_i = pl.multiple_of(i * rows, STRIP)
    width = (rows // STRIP + 1) // 2 * STRIP
    for start in range(0, rows, width):
        size = min(width, rows - start)
        at_j = pl.multiple_of(j * rows + start, STRIP)
        squared = jnp.dot(
            gram[pl.ds(at_i, rows), :], gram[:, pl.ds(at_j, size)], preferred_element_type=jnp.float32
        )
        here = gram[pl.ds(at_i, rows), pl.ds(at_j, size)].astype(jnp.float32)
        out_ref[0, :, start : start + size] = (coef_cubic * here + coef_quintic * squared).astype(jnp.bfloat16)


def poly_blocks(flags, groups):
    rows = groups[0][0].shape[2]
    order = 4 * rows
    return pl.pallas_call(
        poly_kernel,
        grid_spec=pltpu.PrefetchScalarGridSpec(
            num_scalar_prefetch=1,
            grid=(5,),
            in_specs=[pl.BlockSpec(memory_space=pl.ANY)] * 12,
            out_specs=pl.BlockSpec((1, rows, rows), lambda b, flags: (b, 0, 0)),
            scratch_shapes=[pltpu.VMEM((order, order), jnp.bfloat16), pltpu.SemaphoreType.DMA((40,))],
        ),
        out_shape=jax.ShapeDtypeStruct((5, rows, rows), jnp.bfloat16),
        compiler_params=pltpu.CompilerParams(vmem_limit_bytes=VMEM_BYTES),
        cost_estimate=pl.CostEstimate(
            flops=10 * rows * rows * order, bytes_accessed=30 * rows * rows, transcendentals=0
        ),
        name="poly_blocks",
    )(flags, *[x for group in groups for x in group])


def product_kernel(first, strips, flags, own, pair, inverse, s1, s2, s3, *refs):
    distant, (o0, o1, o2, o3, sq_ref, poly, raw, sems) = refs[:-8], refs[-8:]
    rows = s1.shape[0]
    tile = first + pl.program_id(0)

    @pl.when(pl.program_id(0) == 0)
    def _():
        sq_ref[...] = jnp.zeros_like(sq_ref)
        copies = []
        for source, core in ((own, flags[1]), (pair, 1 - flags[1])):
            for b in range(5):
                i, j = poly_place(core, b)
                copies.append(
                    pltpu.make_async_copy(
                        source.at[b],
                        poly.at[
                            pl.ds(pl.multiple_of(i * rows, STRIP), rows),
                            pl.ds(pl.multiple_of(j * rows, STRIP), rows),
                        ],
                        sems.at[len(copies)],
                    )
                )
        for copy in copies:
            copy.start()
        for copy in copies:
            copy.wait()
        for i in range(4):
            for j in range(i + 1, 4):
                transpose_block(poly, rows, (i, j), (j, i))

    for r, s_ref in enumerate((s1, s2, s3), start=1):
        raw[r * rows : (r + 1) * rows, :] = s_ref[...]
    for k, strip in enumerate(distant):
        side, p = divmod(k, 2)

        @pl.when((2 * tile + side >= strips) == (p == 1))
        def _(side=side, strip=strip):
            raw[:rows, side * STRIP : (side + 1) * STRIP] = strip[...]

    for r, o_ref in enumerate((o0, o1, o2, o3)):
        product = jnp.dot(
            poly[r * rows : (r + 1) * rows, :], raw[...], preferred_element_type=jnp.float32
        )
        own_rows = raw[r * rows : (r + 1) * rows, :].astype(jnp.float32)
        newton = inverse[0] * (coef_linear * own_rows + product)
        sq_ref[...] += jnp.sum(newton * newton, axis=0, keepdims=True)
        o_ref[...] = newton.astype(jnp.bfloat16)


def product(flags, own, pair, inverse, blocks, distant, piece, first, tiles):
    rows = own.shape[1]
    order = 4 * rows
    here = pl.BlockSpec((rows, TILE), lambda t, flags: (0, first + t))
    strips = piece // STRIP
    distant_specs = [
        pl.BlockSpec(
            (rows, STRIP),
            lambda t, flags, start=p * strips, side=side: (
                0,
                jnp.clip(2 * (first + t) + side - start, 0, strips - 1),
            ),
        )
        for side in range(2)
        for p in range(2)
    ]
    there = pl.BlockSpec((rows, TILE), lambda t, flags: (0, t))
    *newton, squares = pl.pallas_call(
        functools.partial(product_kernel, first, strips),
        grid_spec=pltpu.PrefetchScalarGridSpec(
            num_scalar_prefetch=1,
            grid=(tiles,),
            in_specs=[
                pl.BlockSpec(memory_space=pl.ANY),
                pl.BlockSpec(memory_space=pl.ANY),
                pl.BlockSpec(memory_space=pltpu.SMEM),
            ]
            + [here] * 3
            + distant_specs,
            out_specs=[there] * 4 + [pl.BlockSpec((1, TILE), lambda t, flags: (0, 0))],
            scratch_shapes=[
                pltpu.VMEM((order, order), jnp.bfloat16),
                pltpu.VMEM((order, TILE), jnp.bfloat16),
                pltpu.SemaphoreType.DMA((10,)),
            ],
        ),
        out_shape=[jax.ShapeDtypeStruct((rows, tiles * TILE), jnp.bfloat16)] * 4
        + [jax.ShapeDtypeStruct((1, TILE), jnp.float32)],
        compiler_params=pltpu.CompilerParams(vmem_limit_bytes=VMEM_BYTES),
        cost_estimate=pl.CostEstimate(
            flops=2 * order * order * tiles * TILE,
            bytes_accessed=20 * rows * rows + 4 * order * tiles * TILE,
            transcendentals=0,
        ),
        name="product",
    )(flags, own, pair, inverse, *blocks, *distant, *distant)
    return newton, jnp.sum(squares)


def finish_kernel(flags, factor, own, near, middle, far, *rest):
    out_ref = rest[-1]
    is_hub = flags[2] == 1

    @pl.when((pl.program_id(0) == 0) & is_hub)
    def _():
        out_ref[...] = own[...].astype(jnp.float32) * factor[0]

    @pl.when((pl.program_id(0) == 0) & jnp.logical_not(is_hub))
    def _():
        out_ref[...] = near[...].astype(jnp.float32) * factor[0]

    @pl.when((pl.program_id(0) == 1) & is_hub)
    def _():
        out_ref[...] = middle[...].astype(jnp.float32) * factor[0]

    @pl.when((pl.program_id(0) == 1) & jnp.logical_not(is_hub))
    def _():
        out_ref[...] = far[...].astype(jnp.float32) * factor[0]


def finish(flags, factor, parts, first, shape, before):
    rows, cols = shape
    tiles = parts[0].shape[1] // TILE
    half = cols // 2 // TILE
    near_part = pl.BlockSpec((rows, TILE), lambda p, t, flags: (0, jnp.where(p == 0, t, tiles - 1)))
    far_part = pl.BlockSpec((rows, TILE), lambda p, t, flags: (0, jnp.where(p == 0, 0, t)))
    place = pl.BlockSpec(
        (rows, TILE),
        lambda p, t, flags: (0, jnp.where(p == 0, flags[0], 1 - flags[0]) * half + first + t),
    )
    specs = [pl.BlockSpec(memory_space=pltpu.SMEM), near_part, near_part, far_part, far_part]
    operands = [flags, factor, *parts]
    aliases = {}
    if before is not None:
        specs.append(pl.BlockSpec(memory_space=pl.ANY))
        aliases = {len(operands): 0}
        operands.append(before)
    return pl.pallas_call(
        finish_kernel,
        grid_spec=pltpu.PrefetchScalarGridSpec(
            num_scalar_prefetch=1, grid=(2, tiles), in_specs=specs, out_specs=place
        ),
        out_shape=jax.ShapeDtypeStruct(shape, jnp.float32),
        input_output_aliases=aliases,
        compiler_params=pltpu.CompilerParams(vmem_limit_bytes=VMEM_BYTES),
        cost_estimate=pl.CostEstimate(
            flops=2 * rows * TILE * tiles, bytes_accessed=16 * rows * TILE * tiles, transcendentals=0
        ),
        name="finish",
    )(*operands)


def per_device(momentum):
    rows, cols = momentum.shape
    width = cols // 2
    quarter = rows // 4
    tiles = width // TILE
    z = lax.axis_index("row")
    c = lax.axis_index("col")
    core, side = c % 2, c // 2
    left = z < 2
    is_hub = (z == 1) | (z == 2)
    flags = jnp.stack([v.astype(jnp.int32) for v in (left, core, is_hub, side)])
    near_index = left.astype(jnp.int32).reshape(1)

    def over_core(x):
        return lax.ppermute(x, "col", [(k, k ^ 1) for k in range(4)])

    def over_side(x):
        return lax.ppermute(x, "col", [(k, k ^ 2) for k in range(4)])

    def between_hubs(x):
        return lax.ppermute(x, "row", [(1, 2), (2, 1)])

    def distant_permute(x):
        return lax.ppermute(x, "row", [(0, 2), (3, 1)])

    def col_total(x):
        x = jnp.broadcast_to(x, (8, 128))
        x = x + over_core(x)
        return x + over_side(x)

    near, far, squares = take(momentum, near_index)
    beside = lax.ppermute(near, "row", [(0, 1), (3, 2)])
    middle = between_hubs(far)
    norm_part = col_total(jnp.sum(squares))

    def added(x, y):
        return (x.astype(jnp.float32) + y.astype(jnp.float32)).astype(jnp.bfloat16)

    def over_pair(kept_sent):
        return added(kept_sent[0], over_core(kept_sent[1]))

    def over_sides(half):
        def rows_of(at):
            return lax.dynamic_slice(half, (0, at * quarter, 0), (half.shape[0], quarter, rows))

        return added(rows_of(side), over_side(rows_of(1 - side)))

    barrier = lax.optimization_barrier
    piece = width // 2
    far_first, beside, norm_part = barrier((far[:, :piece], beside, norm_part))
    arrived = distant_permute(far_first)
    whole = {1: [(middle, width, 0)], 2: [(near, width, 0)], 3: [(beside, width, 0)]}
    pairs_1, pairs_2 = [(2, 2), (3, 3), (3, 2)], [(1, 2), (1, 1), (3, 1)]
    pairs_3, pairs_4 = [(0, 0), (0, 1)], [(0, 2), (0, 3)]
    first = gram_blocks(flags, pairs_1, {r: whole[r] for r in (2, 3)})
    second = gram_blocks(flags, pairs_2, whole)
    norm_sum = (
        norm_part
        + lax.ppermute(norm_part, "row", [(0, 1), (3, 2)])
        + between_hubs(norm_part)
        + distant_permute(norm_part)
    )[0, 0]
    arrived, far_second, first, second, norm_sum = barrier(
        (arrived, far[:, piece:], first, second, norm_sum)
    )

    def halves(h):
        blocks = {1: middle, 2: near, 3: beside}
        return {0: [(distant[h], piece, 0)]} | {r: [(blocks[r], piece, h)] for r in blocks}

    distant = [arrived, distant_permute(far_second)]
    first = over_pair(first)
    second = over_pair(second)
    (late,) = gram_blocks(flags, pairs_3 + pairs_4, halves(0), split=False)
    first = over_sides(first)
    distant[1], late, first, second = barrier((distant[1], late, first, second))

    other_first = between_hubs(first)
    second = over_sides(second)
    third = gram_blocks(flags, pairs_3, {r: halves(1)[r] for r in (0, 1)}, total=late)
    fourth = gram_blocks(flags, pairs_4, {r: halves(1)[r] for r in (0, 2, 3)}, total=late, total_at=2)
    other_first, second, fourth = barrier((other_first, second, fourth))
    other_second = between_hubs(second)
    third = over_sides(over_pair(third))
    other_third = between_hubs(third)
    fourth = over_sides(over_pair(fourth))
    other_second, fourth = barrier((other_second, fourth))
    other_fourth = between_hubs(fourth)

    spectral_edge = 1.0 + math.sqrt(M / N)
    inverse = 1.0 / (jnp.sqrt(norm_sum / M) * spectral_edge + 1e-07)

    mine, other = {}, {}

    def known(pairs, summed, received):
        for k, pair in enumerate(pairs):
            mine[pair], other[mirror(pair)] = summed[k], received[k]

    def gather(pairs):
        total = jnp.stack([mine[pair].astype(jnp.float32) + other[pair].astype(jnp.float32) for pair in pairs])
        here = (total * (inverse * inverse)).astype(jnp.bfloat16)
        across = over_side(here)
        return [here, over_core(here), across, over_core(across)]

    known(pairs_1, first, other_first)
    known(pairs_2, second, other_second)
    groups = [gather(GATHERED[0])]
    groups[0][1], groups[0][2], other_third = barrier((groups[0][1], groups[0][2], other_third))
    known(pairs_3, third, other_third)
    groups.append(gather(GATHERED[1]))
    groups[1][1], other_fourth = barrier((groups[1][1], other_fourth))
    known(pairs_4, fourth, other_fourth)
    groups.append(gather(GATHERED[2]))

    own = poly_blocks(flags, groups)
    pair = over_core(own)

    bounds = sorted({0, tiles * 2 // 9, tiles * 5 // 9, tiles * 7 // 9, tiles})
    newton_sq = jnp.float32(0.0)
    scale = inverse.reshape(1)
    parts = []
    for first, last in zip(bounds[:-1], bounds[1:]):
        newton, squares = product(flags, own, pair, scale, (middle, near, beside), distant, piece, first, last - first)
        newton_sq += squares
        if last == tiles:
            hub_sq = col_total(newton_sq)
            total_sq = (
                jnp.where(is_hub, hub_sq, 0.0)
                + lax.ppermute(hub_sq, "row", [(1, 0), (2, 3)])
                + between_hubs(hub_sq)
                + lax.ppermute(hub_sq, "row", [(2, 0), (1, 3)])
            )[0, 0]
            newton, total_sq, parts[-1] = barrier((newton, total_sq, parts[-1]))
        part = (
            newton[2],
            lax.ppermute(newton[3], "row", [(1, 0), (2, 3)]),
            between_hubs(newton[1]),
            lax.ppermute(newton[0], "row", [(2, 0), (1, 3)]),
        )
        if last == tiles:
            pass
        elif parts:
            parts[-1], scale, newton_sq = barrier((parts[-1], scale, newton_sq))
        else:
            scale, newton_sq = barrier((scale, newton_sq))
        parts.append(part)
    factor = (1.0 / (jnp.sqrt(total_sq) / math.sqrt(M * N) + 1e-07)).reshape(1)
    out = None
    for first, part in zip(bounds[:-1], parts):
        out = finish(flags, factor, part, first, (rows, cols), out)
    return out


def per_device_general(momentum):
    norm_sum = lax.psum(jnp.sum(momentum * momentum), ("col", "row"))
    spectral_edge = 1.0 + math.sqrt(M / N)
    scaled = (momentum / (jnp.sqrt(norm_sum / M) * spectral_edge + 1e-07)).astype(jnp.bfloat16)
    columns = lax.all_gather(scaled, "row", axis=0, tiled=True)
    gram_tile = lax.psum_scatter(
        lax.dot_general(
            columns, scaled, (((1,), (1,)), ((), ())), preferred_element_type=jnp.float32
        ).astype(jnp.bfloat16),
        "col",
        scatter_dimension=0,
        tiled=True,
    )
    left_rows = lax.all_gather(gram_tile, "row", axis=1, tiled=True)
    squared = jnp.dot(
        left_rows,
        lax.all_gather(gram_tile, "col", axis=0, tiled=True),
        preferred_element_type=jnp.float32,
    )
    poly = (coef_cubic * gram_tile.astype(jnp.float32) + coef_quintic * squared).astype(jnp.bfloat16)
    product = lax.dot_general(
        lax.all_gather(poly, "col", axis=0, tiled=True),
        columns,
        (((0,), (0,)), ((), ())),
        preferred_element_type=jnp.float32,
    )
    newton = coef_linear * scaled.astype(jnp.float32) + product
    newton_sq = lax.psum(jnp.sum(newton * newton), ("col", "row"))
    update_rms = jnp.sqrt(newton_sq) / math.sqrt(M * N)
    return newton / (update_rms + 1e-07)


def solution(mesh):
    def update(momentum):
        n_row, n_col = mesh.shape["row"], mesh.shape["col"]
        rows = momentum.shape[0] // (mesh.shape["groups"] * n_row)
        cols = momentum.shape[1] // n_col
        hubs = n_row == 4 and n_col == 4 and rows % STRIP == 0 and cols % (2 * TILE) == 0
        return jax.shard_map(
            per_device if hubs else per_device_general,
            mesh=mesh,
            in_specs=(P(("groups", "row"), "col"),),
            out_specs=P(("groups", "row"), "col"),
            check_vma=False,
        )(momentum)

    return update
```

```python
import functools
import math

import jax
import jax.numpy as jnp
from jax import lax
from jax.experimental import pallas as pl
from jax.experimental.pallas import tpu as pltpu
from jax.sharding import PartitionSpec as P

M = 3584
N = 18432

coef_linear = 3.4445
coef_cubic = -4.775
coef_quintic = 2.0315

TILE = 256
STRIP = 128
VMEM_BYTES = 56 * 2**20

GATHERED = [[(1, 2), (1, 1), (2, 2)], [(0, 0), (3, 3), (0, 1), (3, 2)], [(0, 2), (3, 1), (0, 3)]]


def mirror(pair):
    return pair if sum(pair) == 3 and pair[0] != pair[1] else (3 - pair[0], 3 - pair[1])


def take_kernel(index, near_ref, far_ref, near_out, far_out, sq_ref):
    @pl.when(pl.program_id(0) == 0)
    def _():
        sq_ref[...] = jnp.zeros_like(sq_ref)

    near, far = near_ref[...], far_ref[...]
    near_out[...] = near.astype(jnp.bfloat16)
    far_out[...] = far.astype(jnp.bfloat16)
    sq_ref[...] += jnp.sum(near * near + far * far, axis=0, keepdims=True)


def take(momentum, index):
    rows, cols = momentum.shape
    width = cols // 2
    step = rows // 8
    half = jax.ShapeDtypeStruct((rows, width), jnp.bfloat16)
    return pl.pallas_call(
        take_kernel,
        grid_spec=pltpu.PrefetchScalarGridSpec(
            num_scalar_prefetch=1,
            grid=(8,),
            in_specs=[
                pl.BlockSpec((step, width), lambda t, index: (t, index[0])),
                pl.BlockSpec((step, width), lambda t, index: (t, 1 - index[0])),
            ],
            out_specs=[
                pl.BlockSpec((step, width), lambda t, index: (t, 0)),
                pl.BlockSpec((step, width), lambda t, index: (t, 0)),
                pl.BlockSpec((1, width), lambda t, index: (0, 0)),
            ],
        ),
        out_shape=[half, half, jax.ShapeDtypeStruct((1, width), jnp.float32)],
        compiler_params=pltpu.CompilerParams(vmem_limit_bytes=VMEM_BYTES),
        cost_estimate=pl.CostEstimate(
            flops=4 * rows * width, bytes_accessed=12 * rows * width, transcendentals=0
        ),
        name="take_halves",
    )(index, momentum, momentum)


def gram_kernel(pairs, where, pieces, has_total, split, flags, *refs):
    left, core = flags[0] == 1, flags[1]
    b = pl.program_id(0)
    count = len(where) * pieces
    total = refs[count] if has_total else None
    outs = refs[count + has_total :]

    def make(i, j):
        value = total[0] if has_total else 0.0
        for p in range(pieces):
            x, y = refs[where[i] * pieces + p], refs[where[j] * pieces + p]
            value += lax.dot_general(
                x[...], y[...], (((1,), (1,)), ((), ())), preferred_element_type=jnp.float32
            )
        if not split:
            outs[0][0] = value
            return
        keep, send, whole = outs
        share = keep.shape[1]
        whole[...] = value.astype(jnp.bfloat16)
        keep[0] = whole[pl.ds(pl.multiple_of(core * share, 16), share), :]
        send[0] = whole[pl.ds(pl.multiple_of((1 - core) * share, 16), share), :]

    for k, (i, j) in enumerate(pairs):
        if (i, j) in ((1, 2), (0, 3)):
            pl.when((b == k) & left)(functools.partial(make, j, i))
            pl.when((b == k) & jnp.logical_not(left))(functools.partial(make, i, j))
        else:
            pl.when(b == k)(functools.partial(make, i, j))


def gram_blocks(flags, pairs, operands, total=None, total_at=0, split=True):
    where = {r: k for k, r in enumerate(operands)}
    pieces = len(operands[pairs[0][0]])
    rows = operands[pairs[0][0]][0][0].shape[0]
    share = rows // 2
    used = [piece for r in operands for piece in operands[r]]
    specs = [pl.BlockSpec((rows, width), lambda b, flags, at=at: (0, at)) for _, width, at in used]
    arrays = [array for array, _, _ in used]
    if total is not None:
        specs.append(
            pl.BlockSpec(
                (1, rows, rows), lambda b, flags: (total_at + b, 0, 0)
            )
        )
        arrays.append(total)
    count = len(pairs)
    if split:
        out_specs = [pl.BlockSpec((1, share, rows), lambda b, flags: (b, 0, 0))] * 2
        scratch = [pltpu.VMEM((rows, rows), jnp.bfloat16)]
        out_shape = [jax.ShapeDtypeStruct((count, share, rows), jnp.bfloat16)] * 2
    else:
        out_specs = [pl.BlockSpec((1, rows, rows), lambda b, flags: (b, 0, 0))]
        scratch = []
        out_shape = [jax.ShapeDtypeStruct((count, rows, rows), jnp.float32)]
    return pl.pallas_call(
        functools.partial(gram_kernel, pairs, where, pieces, int(total is not None), split),
        grid_spec=pltpu.PrefetchScalarGridSpec(
            num_scalar_prefetch=1, grid=(count,), in_specs=specs, out_specs=out_specs, scratch_shapes=scratch
        ),
        out_shape=out_shape,
        compiler_params=pltpu.CompilerParams(vmem_limit_bytes=VMEM_BYTES),
        cost_estimate=pl.CostEstimate(flops=0, bytes_accessed=0, transcendentals=0),
        name="gram_blocks",
    )(flags, *arrays)


def transpose_block(ref, rows, source, target):
    @pl.loop(0, rows // STRIP)
    def _(s):
        part = ref[
            pl.ds(pl.multiple_of(source[0] * rows, STRIP), rows),
            pl.ds(pl.multiple_of(source[1] * rows + s * STRIP, STRIP), STRIP),
        ]
        ref[
            pl.ds(pl.multiple_of(target[0] * rows + s * STRIP, STRIP), STRIP),
            pl.ds(pl.multiple_of(target[1] * rows, STRIP), rows),
        ] = part.T


def poly_kernel(flags, *refs):
    *parts, out_ref, gram, sems = refs
    rows = out_ref.shape[0]
    quarter = rows // 4
    left, core, side = flags[0], flags[1], flags[3]
    b = pl.program_id(0)

    @pl.when(b == 0)
    def _():
        places = [
            2 * core + side,
            2 * (1 - core) + side,
            2 * core + 1 - side,
            2 * (1 - core) + 1 - side,
        ]
        copies, turned = [], []
        for g, pairs in enumerate(GATHERED):
            for k, (i, j) in enumerate(pairs):
                if (i, j) in ((1, 2), (0, 3)):
                    i, j = jnp.where(left == 1, j, i), jnp.where(left == 1, i, j)
                for q, place in enumerate(places):
                    copies.append(
                        pltpu.make_async_copy(
                            parts[4 * g + q].at[k],
                            gram.at[
                                pl.ds(pl.multiple_of(i * rows + place * quarter, 16), quarter),
                                pl.ds(pl.multiple_of(j * rows, STRIP), rows),
                            ],
                            sems.at[len(copies)],
                        )
                    )
                if pairs[k][0] != pairs[k][1]:
                    turned.append((i, j))
        for copy in copies:
            copy.start()
        for copy in copies:
            copy.wait()
        for i, j in turned:
            transpose_block(gram, rows, (i, j), (j, i))

    at_i = pl.multiple_of((2 + core) * rows, STRIP)
    width = out_ref.shape[1]
    at_j = pl.multiple_of(b * width, STRIP)
    squared = jnp.dot(
        gram[pl.ds(at_i, rows), :], gram[:, pl.ds(at_j, width)], preferred_element_type=jnp.float32
    )
    here = gram[pl.ds(at_i, rows), pl.ds(at_j, width)].astype(jnp.float32)
    out_ref[...] = (coef_cubic * here + coef_quintic * squared).astype(jnp.bfloat16)


def poly_rows(flags, groups):
    rows = groups[0][0].shape[2]
    order = 4 * rows
    width = 2 * TILE
    return pl.pallas_call(
        poly_kernel,
        grid_spec=pltpu.PrefetchScalarGridSpec(
            num_scalar_prefetch=1,
            grid=(order // width,),
            in_specs=[pl.BlockSpec(memory_space=pl.ANY)] * 12,
            out_specs=pl.BlockSpec((rows, width), lambda b, flags: (0, b)),
            scratch_shapes=[pltpu.VMEM((order, order), jnp.bfloat16), pltpu.SemaphoreType.DMA((40,))],
        ),
        out_shape=jax.ShapeDtypeStruct((rows, order), jnp.bfloat16),
        compiler_params=pltpu.CompilerParams(vmem_limit_bytes=VMEM_BYTES),
        cost_estimate=pl.CostEstimate(flops=0, bytes_accessed=0, transcendentals=0),
        name="poly_rows",
    )(flags, *[x for group in groups for x in group])


def product_kernel(is_far, flags, own, pair, *refs):
    end_row, refs = (None, refs) if is_far else (refs[0], refs[1:])
    inverse, blocks, outs = refs[0], refs[1:5], refs[5:-4]
    sq_ref, poly, raw, sems = refs[-4:]
    rows = own.shape[0]

    @pl.when(pl.program_id(0) == 0)
    def _():
        sq_ref[...] = jnp.zeros_like(sq_ref)

        def load(pairs):
            copies = [
                pltpu.make_async_copy(source, target, sems.at[k]) for k, (source, target) in enumerate(pairs)
            ]
            for copy in copies:
                copy.start()
            for copy in copies:
                copy.wait()

        if is_far:
            at = pl.multiple_of(flags[1] * rows, 16)
            load([(own, poly.at[pl.ds(at, rows), :]), (pair, poly.at[pl.ds(rows - at, rows), :])])
        else:
            @pl.when((flags[2] == 1) & (flags[1] == 0))
            def _():
                load([(own, poly)])

            @pl.when((flags[2] == 1) & (flags[1] == 1))
            def _():
                load([(pair, poly)])

            @pl.when(flags[2] == 0)
            def _():
                load(
                    [
                        (end_row.at[:, m * rows : (m + 1) * rows], poly.at[:, (m ^ 1) * rows : ((m ^ 1) + 1) * rows])
                        for m in range(4)
                    ]
                )

    for r, block in enumerate(blocks):
        raw[r * rows : (r + 1) * rows, :] = block[...]
    for k, out in enumerate(outs):
        product = jnp.dot(poly[k * rows : (k + 1) * rows, :], raw[...], preferred_element_type=jnp.float32)
        own_rows = raw[(2 + k) * rows : (3 + k) * rows, :].astype(jnp.float32)
        newton = inverse[0] * (coef_linear * own_rows + product)
        sq_ref[...] += jnp.sum(newton * newton, axis=0, keepdims=True)
        out[...] = newton.astype(jnp.bfloat16)


def product(flags, polys, inverse, blocks, tiles, is_far):
    rows, order = polys[0].shape
    count = 2 if is_far else 1
    block_specs = [
        pl.BlockSpec((rows, TILE), lambda t, flags, at=at: (0, at + t))
        if lead is None
        else pl.BlockSpec((None, rows, TILE), lambda t, flags, at=at, lead=lead: (lead, 0, at + t))
        for _, lead, at in blocks
    ]
    there = pl.BlockSpec((rows, TILE), lambda t, flags: (0, t))
    *newton, squares = pl.pallas_call(
        functools.partial(product_kernel, is_far),
        grid_spec=pltpu.PrefetchScalarGridSpec(
            num_scalar_prefetch=1,
            grid=(tiles,),
            in_specs=[pl.BlockSpec(memory_space=pl.ANY)] * len(polys)
            + [pl.BlockSpec(memory_space=pltpu.SMEM)]
            + block_specs,
            out_specs=[there] * count + [pl.BlockSpec((1, TILE), lambda t, flags: (0, 0))],
            scratch_shapes=[
                pltpu.VMEM((count * rows, order), jnp.bfloat16),
                pltpu.VMEM((order, TILE), jnp.bfloat16),
                pltpu.SemaphoreType.DMA((4,)),
            ],
        ),
        out_shape=[jax.ShapeDtypeStruct((rows, tiles * TILE), jnp.bfloat16)] * count
        + [jax.ShapeDtypeStruct((1, TILE), jnp.float32)],
        compiler_params=pltpu.CompilerParams(vmem_limit_bytes=VMEM_BYTES),
        cost_estimate=pl.CostEstimate(flops=0, bytes_accessed=0, transcendentals=0),
        name="product_far" if is_far else "product_near",
    )(flags, *polys, inverse, *[array for array, _, _ in blocks])
    return newton, jnp.sum(squares)


def finish_kernel(starts, flags, factor, *refs):
    out_ref = refs[-1]
    t = pl.program_id(0)
    chunks = len(starts) - 1
    for k, ref in enumerate(refs[: chunks if chunks == 1 else 2 * chunks]):
        here = (t >= starts[k % chunks]) & (t < starts[k % chunks + 1])
        if chunks > 1:
            here &= (flags[2] == 1) == (k < chunks)

        @pl.when(here)
        def _(ref=ref):
            out_ref[...] = ref[...].astype(jnp.float32) * factor[0]


def finish(flags, factor, parts, starts, shape, before):
    rows, cols = shape
    chunks = len(starts) - 1
    half = cols // 2 // TILE
    place = pl.BlockSpec(
        (rows, TILE), lambda t, flags: (0, (flags[0] if chunks == 1 else 1 - flags[0]) * half + t)
    )
    specs = [pl.BlockSpec(memory_space=pltpu.SMEM)]
    for k in range(len(parts)):
        first, last = starts[k % chunks : k % chunks + 2]
        specs.append(
            pl.BlockSpec(
                (rows, TILE),
                lambda t, flags, first=first, last=last: (0, jnp.clip(t, first, last - 1) - first),
            )
        )
    operands = [flags, factor, *parts]
    aliases = {}
    if before is not None:
        specs.append(pl.BlockSpec(memory_space=pl.ANY))
        aliases = {len(operands): 0}
        operands.append(before)
    return pl.pallas_call(
        functools.partial(finish_kernel, starts),
        grid_spec=pltpu.PrefetchScalarGridSpec(
            num_scalar_prefetch=1, grid=(starts[-1],), in_specs=specs, out_specs=place
        ),
        out_shape=jax.ShapeDtypeStruct(shape, jnp.float32),
        input_output_aliases=aliases,
        compiler_params=pltpu.CompilerParams(vmem_limit_bytes=VMEM_BYTES),
        cost_estimate=pl.CostEstimate(flops=0, bytes_accessed=0, transcendentals=0),
        name="finish",
    )(*operands)


def per_device(momentum):
    rows, cols = momentum.shape
    width = cols // 2
    quarter = rows // 4
    tiles = width // TILE
    z = lax.axis_index("row")
    c = lax.axis_index("col")
    core, side = c % 2, c // 2
    left = z < 2
    is_hub = (z == 1) | (z == 2)
    flags = jnp.stack([v.astype(jnp.int32) for v in (left, core, is_hub, side)])
    near_index = left.astype(jnp.int32).reshape(1)

    def over_core(x):
        return lax.ppermute(x, "col", [(k, k ^ 1) for k in range(4)])

    def over_side(x):
        return lax.ppermute(x, "col", [(k, k ^ 2) for k in range(4)])

    def between_hubs(x):
        return lax.ppermute(x, "row", [(1, 2), (2, 1)])

    def skip_one(x):
        return lax.ppermute(x, "row", [(0, 2), (2, 0), (1, 3), (3, 1)])

    def with_end(x):
        return lax.ppermute(x, "row", [(0, 1), (1, 0), (2, 3), (3, 2)])

    def to_end(x):
        return lax.ppermute(x, "row", [(1, 0), (2, 3)])

    def past_hub(x):
        return lax.ppermute(x, "row", [(0, 2), (3, 1), (1, 0), (2, 3)])

    def col_total(x):
        x = jnp.broadcast_to(x, (8, 128))
        x = x + over_core(x)
        return x + over_side(x)

    near, far, squares = take(momentum, near_index)
    beside = with_end(near)
    middle = between_hubs(far)
    norm_part = col_total(jnp.sum(squares))
    norm_part += with_end(norm_part)

    def added(x, y):
        return (x.astype(jnp.float32) + y.astype(jnp.float32)).astype(jnp.bfloat16)

    def over_pair(kept_sent):
        return added(kept_sent[0], over_core(kept_sent[1]))

    def over_sides(half):
        def rows_of(at):
            return lax.dynamic_slice(half, (0, at * quarter, 0), (half.shape[0], quarter, rows))

        return added(rows_of(side), over_side(rows_of(1 - side)))

    barrier = lax.optimization_barrier
    piece = width // 2
    outward = [jnp.where(is_hub, middle[:, at : at + piece], far[:, at : at + piece]) for at in (0, piece)]
    outward[0], beside, norm_part = barrier((outward[0], beside, norm_part))
    arrived = past_hub(outward[0])
    whole = {1: [(middle, width, 0)], 2: [(near, width, 0)], 3: [(beside, width, 0)]}
    pairs_1, pairs_2 = [(2, 2), (3, 3), (3, 2)], [(1, 2), (1, 1), (3, 1)]
    pairs_3, pairs_4 = [(0, 0), (0, 1)], [(0, 2), (0, 3)]
    first = gram_blocks(flags, pairs_1, {r: whole[r] for r in (2, 3)})
    second = gram_blocks(flags, pairs_2, whole)
    norm_sum = (norm_part + skip_one(norm_part))[0, 0]
    arrived, outward_second, first, second, norm_sum = barrier(
        (arrived, outward[1], first, second, norm_sum)
    )

    def halves(h):
        blocks = {1: middle, 2: near, 3: beside}
        return {0: [(distant[h], piece, 0)]} | {r: [(blocks[r], piece, h)] for r in blocks}

    distant = [arrived, past_hub(outward_second)]
    first = over_pair(first)
    second = over_pair(second)
    (late,) = gram_blocks(flags, pairs_3 + pairs_4, halves(0), split=False)
    first = over_sides(first)
    distant[1], late, first, second = barrier((distant[1], late, first, second))

    other_first = between_hubs(first)
    second = over_sides(second)
    third = gram_blocks(flags, pairs_3, {r: halves(1)[r] for r in (0, 1)}, total=late)
    fourth = gram_blocks(flags, pairs_4, {r: halves(1)[r] for r in (0, 2, 3)}, total=late, total_at=2)
    other_first, second, fourth = barrier((other_first, second, fourth))
    other_second = between_hubs(second)
    third = over_sides(over_pair(third))
    other_third = between_hubs(third)
    fourth = over_sides(over_pair(fourth))
    other_second, fourth = barrier((other_second, fourth))
    other_fourth = between_hubs(fourth)

    spectral_edge = 1.0 + math.sqrt(M / N)
    inverse = 1.0 / (jnp.sqrt(norm_sum / M) * spectral_edge + 1e-07)

    mine, other = {}, {}

    def known(pairs, summed, received):
        for k, pair in enumerate(pairs):
            mine[pair], other[mirror(pair)] = summed[k], received[k]

    def gather(pairs):
        total = jnp.stack([mine[pair].astype(jnp.float32) + other[pair].astype(jnp.float32) for pair in pairs])
        here = (total * (inverse * inverse)).astype(jnp.bfloat16)
        across = over_side(here)
        return [here, over_core(here), across, over_core(across)]

    known(pairs_1, first, other_first)
    known(pairs_2, second, other_second)
    groups = [gather(GATHERED[0])]
    groups[0][1], groups[0][2], other_third = barrier((groups[0][1], groups[0][2], other_third))
    known(pairs_3, third, other_third)
    groups.append(gather(GATHERED[1]))
    passed = jnp.concatenate(distant, axis=1)
    inward = jnp.where(is_hub, passed, far)
    tile_bounds = [0, max(1, tiles * 4 // 9), max(2, tiles * 7 // 9), tiles]
    cuts = [t * TILE for t in tile_bounds]
    inward_first = with_end(inward[:, : cuts[1]])
    groups[1][1], inward_first, other_fourth = barrier((groups[1][1], inward_first, other_fourth))
    known(pairs_4, fourth, other_fourth)
    groups.append(gather(GATHERED[2]))

    inward_second = with_end(inward[:, cuts[1] :])
    swaps = [jnp.stack([block[:, a:b] for block in (beside, near)]) for a, b in zip(cuts[:-1], cuts[1:])]
    swaps[0], other_fourth = barrier((swaps[0], other_fourth))
    swaps[0] = between_hubs(swaps[0])
    groups[2], inward_second = barrier((groups[2], inward_second))
    own, swaps[0] = barrier((poly_rows(flags, groups), swaps[0]))
    pair = over_core(own)
    swaps[1] = between_hubs(swaps[1])
    row_share = to_end(
        jnp.where(
            core == 0,
            lax.dynamic_slice(pair, (c * quarter, 0), (quarter, 4 * rows)),
            lax.dynamic_slice(own, (c * quarter, 0), (quarter, 4 * rows)),
        )
    )
    scale = inverse.reshape(1)
    inwards = [(inward_first, 0), (inward_second, 0), (inward_second, tile_bounds[2] - tile_bounds[1])]
    at_hub, at_end = [], []

    def far_product(k, scale):
        block, at = inwards[k]
        first, last = tile_bounds[k : k + 2]
        blocks = [(swaps[k], 0, 0), (swaps[k], 1, 0), (far, None, first), (block, None, at)]
        (here, there), squares = product(flags, (own, pair), scale, blocks, last - first, True)
        at_hub.append(here)
        at_end.append(to_end(there))
        return squares

    hub_sq = far_product(0, scale)
    scale, hub_sq, row_share, swaps[1] = barrier((scale, hub_sq, row_share, swaps[1]))
    swaps[2] = between_hubs(swaps[2])
    end_row = lax.all_gather(row_share, "col", axis=0, tiled=True)
    hub_sq += far_product(1, scale)
    scale, hub_sq, swaps[2], inward_first = barrier((scale, hub_sq, swaps[2], inward_first))
    hub_sq += far_product(2, scale)
    scale, hub_sq, at_end[0], at_end[1] = barrier((scale, hub_sq, at_end[0], at_end[1]))
    inward = jnp.concatenate([inward_first, inward_second], axis=1)
    blocks = [(passed, None, 0), (jnp.where(is_hub, middle, inward), None, 0), (near, None, 0), (beside, None, 0)]
    (near_part,), near_sq = product(flags, (own, pair, end_row), scale, blocks, tiles, False)
    total_sq = col_total(near_sq + jnp.where(is_hub, hub_sq, 0.0))
    total_sq += with_end(total_sq)
    total_sq += skip_one(total_sq)
    factor = (1.0 / (jnp.sqrt(total_sq[0, 0]) / math.sqrt(M * N) + 1e-07)).reshape(1)
    out = finish(flags, factor, [near_part], [0, tiles], (rows, cols), None)
    return finish(flags, factor, at_hub + at_end, tile_bounds, (rows, cols), out)


def per_device_general(momentum):
    norm_sum = lax.psum(jnp.sum(momentum * momentum), ("col", "row"))
    spectral_edge = 1.0 + math.sqrt(M / N)
    scaled = (momentum / (jnp.sqrt(norm_sum / M) * spectral_edge + 1e-07)).astype(jnp.bfloat16)
    columns = lax.all_gather(scaled, "row", axis=0, tiled=True)
    gram_tile = lax.psum_scatter(
        lax.dot_general(
            columns, scaled, (((1,), (1,)), ((), ())), preferred_element_type=jnp.float32
        ).astype(jnp.bfloat16),
        "col",
        scatter_dimension=0,
        tiled=True,
    )
    left_rows = lax.all_gather(gram_tile, "row", axis=1, tiled=True)
    squared = jnp.dot(
        left_rows,
        lax.all_gather(gram_tile, "col", axis=0, tiled=True),
        preferred_element_type=jnp.float32,
    )
    poly = (coef_cubic * gram_tile.astype(jnp.float32) + coef_quintic * squared).astype(jnp.bfloat16)
    product = lax.dot_general(
        lax.all_gather(poly, "col", axis=0, tiled=True),
        columns,
        (((0,), (0,)), ((), ())),
        preferred_element_type=jnp.float32,
    )
    newton = coef_linear * scaled.astype(jnp.float32) + product
    newton_sq = lax.psum(jnp.sum(newton * newton), ("col", "row"))
    update_rms = jnp.sqrt(newton_sq) / math.sqrt(M * N)
    return newton / (update_rms + 1e-07)


def solution(mesh):
    def update(momentum):
        n_row, n_col = mesh.shape["row"], mesh.shape["col"]
        rows = momentum.shape[0] // (mesh.shape["groups"] * n_row)
        cols = momentum.shape[1] // n_col
        hubs = n_row == 4 and n_col == 4 and rows % STRIP == 0 and cols % (6 * TILE) == 0
        return jax.shard_map(
            per_device if hubs else per_device_general,
            mesh=mesh,
            in_specs=(P(("groups", "row"), "col"),),
            out_specs=P(("groups", "row"), "col"),
            check_vma=False,
        )(momentum)

    return update
```

```python
import functools
import math

import jax
import jax.numpy as jnp
from jax import lax
from jax.experimental import pallas as pl
from jax.experimental.pallas import tpu as pltpu
from jax.sharding import PartitionSpec as P

M = 3584
N = 18432

coef_linear = 3.4445
coef_cubic = -4.775
coef_quintic = 2.0315

TILE = 256
STRIP = 128
VMEM_BYTES = 56 * 2**20

GATHERED = [[(1, 2), (1, 1), (2, 2)], [(0, 0), (3, 3), (0, 1), (3, 2)], [(0, 2), (3, 1), (0, 3)]]


def mirror(pair):
    return pair if sum(pair) == 3 and pair[0] != pair[1] else (3 - pair[0], 3 - pair[1])


def take_kernel(index, near_ref, far_ref, near_out, far_out, sq_ref):
    @pl.when(pl.program_id(0) == 0)
    def _():
        sq_ref[...] = jnp.zeros_like(sq_ref)

    near, far = near_ref[...], far_ref[...]
    near_out[...] = near.astype(jnp.bfloat16)
    far_out[...] = far.astype(jnp.bfloat16)
    sq_ref[...] += jnp.sum(near * near + far * far, axis=0, keepdims=True)


def take(momentum, index):
    rows, cols = momentum.shape
    width = cols // 2
    step = rows // 8
    half = jax.ShapeDtypeStruct((rows, width), jnp.bfloat16)
    return pl.pallas_call(
        take_kernel,
        grid_spec=pltpu.PrefetchScalarGridSpec(
            num_scalar_prefetch=1,
            grid=(8,),
            in_specs=[
                pl.BlockSpec((step, width), lambda t, index: (t, index[0])),
                pl.BlockSpec((step, width), lambda t, index: (t, 1 - index[0])),
            ],
            out_specs=[
                pl.BlockSpec((step, width), lambda t, index: (t, 0)),
                pl.BlockSpec((step, width), lambda t, index: (t, 0)),
                pl.BlockSpec((1, width), lambda t, index: (0, 0)),
            ],
        ),
        out_shape=[half, half, jax.ShapeDtypeStruct((1, width), jnp.float32)],
        compiler_params=pltpu.CompilerParams(vmem_limit_bytes=VMEM_BYTES),
        cost_estimate=pl.CostEstimate(
            flops=4 * rows * width, bytes_accessed=12 * rows * width, transcendentals=0
        ),
        name="take_halves",
    )(index, momentum, momentum)


def gram_kernel(pairs, where, pieces, has_total, split, flags, *refs):
    left, core = flags[0] == 1, flags[1]
    b = pl.program_id(0)
    count = len(where) * pieces
    total = refs[count] if has_total else None
    outs = refs[count + has_total :]

    def make(i, j):
        value = total[0] if has_total else 0.0
        for p in range(pieces):
            x, y = refs[where[i] * pieces + p], refs[where[j] * pieces + p]
            value += lax.dot_general(
                x[...], y[...], (((1,), (1,)), ((), ())), preferred_element_type=jnp.float32
            )
        if not split:
            outs[0][0] = value
            return
        keep, send, whole = outs
        share = keep.shape[1]
        whole[...] = value.astype(jnp.bfloat16)
        keep[0] = whole[pl.ds(pl.multiple_of(core * share, 16), share), :]
        send[0] = whole[pl.ds(pl.multiple_of((1 - core) * share, 16), share), :]

    for k, (i, j) in enumerate(pairs):
        if (i, j) in ((1, 2), (0, 3)):
            pl.when((b == k) & left)(functools.partial(make, j, i))
            pl.when((b == k) & jnp.logical_not(left))(functools.partial(make, i, j))
        else:
            pl.when(b == k)(functools.partial(make, i, j))


def gram_blocks(flags, pairs, operands, total=None, total_at=0, split=True):
    where = {r: k for k, r in enumerate(operands)}
    pieces = len(operands[pairs[0][0]])
    rows = operands[pairs[0][0]][0][0].shape[0]
    share = rows // 2
    used = [piece for r in operands for piece in operands[r]]
    specs = [pl.BlockSpec((rows, width), lambda b, flags, at=at: (0, at)) for _, width, at in used]
    arrays = [array for array, _, _ in used]
    if total is not None:
        specs.append(
            pl.BlockSpec(
                (1, rows, rows), lambda b, flags: (total_at + b, 0, 0)
            )
        )
        arrays.append(total)
    count = len(pairs)
    if split:
        out_specs = [pl.BlockSpec((1, share, rows), lambda b, flags: (b, 0, 0))] * 2
        scratch = [pltpu.VMEM((rows, rows), jnp.bfloat16)]
        out_shape = [jax.ShapeDtypeStruct((count, share, rows), jnp.bfloat16)] * 2
    else:
        out_specs = [pl.BlockSpec((1, rows, rows), lambda b, flags: (b, 0, 0))]
        scratch = []
        out_shape = [jax.ShapeDtypeStruct((count, rows, rows), jnp.float32)]
    return pl.pallas_call(
        functools.partial(gram_kernel, pairs, where, pieces, int(total is not None), split),
        grid_spec=pltpu.PrefetchScalarGridSpec(
            num_scalar_prefetch=1, grid=(count,), in_specs=specs, out_specs=out_specs, scratch_shapes=scratch
        ),
        out_shape=out_shape,
        compiler_params=pltpu.CompilerParams(vmem_limit_bytes=VMEM_BYTES),
        cost_estimate=pl.CostEstimate(flops=0, bytes_accessed=0, transcendentals=0),
        name="gram_blocks",
    )(flags, *arrays)


def transpose_block(ref, rows, source, target):
    @pl.loop(0, rows // STRIP)
    def _(s):
        part = ref[
            pl.ds(pl.multiple_of(source[0] * rows, STRIP), rows),
            pl.ds(pl.multiple_of(source[1] * rows + s * STRIP, STRIP), STRIP),
        ]
        ref[
            pl.ds(pl.multiple_of(target[0] * rows + s * STRIP, STRIP), STRIP),
            pl.ds(pl.multiple_of(target[1] * rows, STRIP), rows),
        ] = part.T


def poly_kernel(flags, *refs):
    *parts, out_ref, gram, sems = refs
    rows = out_ref.shape[0]
    quarter = rows // 4
    left, core, side = flags[0], flags[1], flags[3]
    b = pl.program_id(0)

    @pl.when(b == 0)
    def _():
        places = [
            2 * core + side,
            2 * (1 - core) + side,
            2 * core + 1 - side,
            2 * (1 - core) + 1 - side,
        ]
        copies, turned = [], []
        for g, pairs in enumerate(GATHERED):
            for k, (i, j) in enumerate(pairs):
                if (i, j) in ((1, 2), (0, 3)):
                    i, j = jnp.where(left == 1, j, i), jnp.where(left == 1, i, j)
                for q, place in enumerate(places):
                    copies.append(
                        pltpu.make_async_copy(
                            parts[4 * g + q].at[k],
                            gram.at[
                                pl.ds(pl.multiple_of(i * rows + place * quarter, 16), quarter),
                                pl.ds(pl.multiple_of(j * rows, STRIP), rows),
                            ],
                            sems.at[len(copies)],
                        )
                    )
                if pairs[k][0] != pairs[k][1]:
                    turned.append((i, j))
        for copy in copies:
            copy.start()
        for copy in copies:
            copy.wait()
        for i, j in turned:
            transpose_block(gram, rows, (i, j), (j, i))

    at_i = pl.multiple_of((2 + core) * rows, STRIP)
    width = out_ref.shape[1]
    at_j = pl.multiple_of(b * width, STRIP)
    squared = jnp.dot(
        gram[pl.ds(at_i, rows), :], gram[:, pl.ds(at_j, width)], preferred_element_type=jnp.float32
    )
    here = gram[pl.ds(at_i, rows), pl.ds(at_j, width)].astype(jnp.float32)
    out_ref[...] = (coef_cubic * here + coef_quintic * squared).astype(jnp.bfloat16)


def poly_rows(flags, groups):
    rows = groups[0][0].shape[2]
    order = 4 * rows
    width = 2 * TILE
    return pl.pallas_call(
        poly_kernel,
        grid_spec=pltpu.PrefetchScalarGridSpec(
            num_scalar_prefetch=1,
            grid=(order // width,),
            in_specs=[pl.BlockSpec(memory_space=pl.ANY)] * 12,
            out_specs=pl.BlockSpec((rows, width), lambda b, flags: (0, b)),
            scratch_shapes=[pltpu.VMEM((order, order), jnp.bfloat16), pltpu.SemaphoreType.DMA((40,))],
        ),
        out_shape=jax.ShapeDtypeStruct((rows, order), jnp.bfloat16),
        compiler_params=pltpu.CompilerParams(vmem_limit_bytes=VMEM_BYTES),
        cost_estimate=pl.CostEstimate(flops=0, bytes_accessed=0, transcendentals=0),
        name="poly_rows",
    )(flags, *[x for group in groups for x in group])


def product_kernel(is_far, flags, own, pair, *refs):
    end_rows, refs = ((), refs) if is_far else (refs[:4], refs[4:])
    inverse, blocks, outs = refs[0], refs[1:5], refs[5:-4]
    sq_ref, poly, raw, sems = refs[-4:]
    rows = own.shape[0]

    @pl.when(pl.program_id(0) == 0)
    def _():
        sq_ref[...] = jnp.zeros_like(sq_ref)

        def load(pairs):
            copies = [
                pltpu.make_async_copy(source, target, sems.at[k]) for k, (source, target) in enumerate(pairs)
            ]
            for copy in copies:
                copy.start()
            for copy in copies:
                copy.wait()

        if is_far:
            at = pl.multiple_of(flags[1] * rows, 16)
            load([(own, poly.at[pl.ds(at, rows), :]), (pair, poly.at[pl.ds(rows - at, rows), :])])
        else:
            @pl.when((flags[2] == 1) & (flags[1] == 0))
            def _():
                load([(own, poly)])

            @pl.when((flags[2] == 1) & (flags[1] == 1))
            def _():
                load([(pair, poly)])

            @pl.when(flags[2] == 0)
            def _():
                core, side = flags[1], flags[3]
                quarter = rows // 4
                places = [2 * side + core, 2 * side + 1 - core, 2 * (1 - side) + core, 2 * (1 - side) + 1 - core]
                load(
                    [
                        (
                            part.at[:, m * rows : (m + 1) * rows],
                            poly.at[
                                pl.ds(pl.multiple_of(place * quarter, 16), quarter),
                                (m ^ 1) * rows : ((m ^ 1) + 1) * rows,
                            ],
                        )
                        for part, place in zip(end_rows, places)
                        for m in range(4)
                    ]
                )

    for r, block in enumerate(blocks):
        raw[r * rows : (r + 1) * rows, :] = block[...]
    for k, out in enumerate(outs):
        product = jnp.dot(poly[k * rows : (k + 1) * rows, :], raw[...], preferred_element_type=jnp.float32)
        own_rows = raw[(2 + k) * rows : (3 + k) * rows, :].astype(jnp.float32)
        newton = inverse[0] * (coef_linear * own_rows + product)
        sq_ref[...] += jnp.sum(newton * newton, axis=0, keepdims=True)
        out[...] = newton.astype(jnp.bfloat16)


def product(flags, polys, inverse, blocks, tiles, is_far):
    rows, order = polys[0].shape
    count = 2 if is_far else 1
    block_specs = [
        pl.BlockSpec((rows, TILE), lambda t, flags, at=at: (0, at + t))
        if lead is None
        else pl.BlockSpec((None, rows, TILE), lambda t, flags, at=at, lead=lead: (lead, 0, at + t))
        for _, lead, at in blocks
    ]
    there = pl.BlockSpec((rows, TILE), lambda t, flags: (0, t))
    *newton, squares = pl.pallas_call(
        functools.partial(product_kernel, is_far),
        grid_spec=pltpu.PrefetchScalarGridSpec(
            num_scalar_prefetch=1,
            grid=(tiles,),
            in_specs=[pl.BlockSpec(memory_space=pl.ANY)] * len(polys)
            + [pl.BlockSpec(memory_space=pltpu.SMEM)]
            + block_specs,
            out_specs=[there] * count + [pl.BlockSpec((1, TILE), lambda t, flags: (0, 0))],
            scratch_shapes=[
                pltpu.VMEM((count * rows, order), jnp.bfloat16),
                pltpu.VMEM((order, TILE), jnp.bfloat16),
                pltpu.SemaphoreType.DMA((16,)),
            ],
        ),
        out_shape=[jax.ShapeDtypeStruct((rows, tiles * TILE), jnp.bfloat16)] * count
        + [jax.ShapeDtypeStruct((1, TILE), jnp.float32)],
        compiler_params=pltpu.CompilerParams(vmem_limit_bytes=VMEM_BYTES),
        cost_estimate=pl.CostEstimate(flops=0, bytes_accessed=0, transcendentals=0),
        name="product_far" if is_far else "product_near",
    )(flags, *polys, inverse, *[array for array, _, _ in blocks])
    return newton, jnp.sum(squares)


def finish_kernel(cuts, flags, factor, *refs):
    out_ref = refs[-1]
    chunks = len(cuts) - 1
    for k, ref in enumerate(refs[: chunks if chunks == 1 else 2 * chunks]):

        @pl.when((chunks == 1) | ((flags[2] == 1) == (k < chunks)))
        def _(k=k, ref=ref):
            out_ref[:, cuts[k % chunks] : cuts[k % chunks + 1]] = ref[...].astype(jnp.float32) * factor[0]


def finish(flags, factor, parts, cuts, shape, before):
    rows, cols = shape
    step = rows // 8
    place = pl.BlockSpec(
        (step, cols // 2), lambda t, flags: (t, flags[0] if len(parts) == 1 else 1 - flags[0])
    )
    specs = [pl.BlockSpec(memory_space=pltpu.SMEM)]
    specs += [pl.BlockSpec((step, part.shape[1]), lambda t, flags: (t, 0)) for part in parts]
    operands = [flags, factor, *parts]
    aliases = {}
    if before is not None:
        specs.append(pl.BlockSpec(memory_space=pl.ANY))
        aliases = {len(operands): 0}
        operands.append(before)
    return pl.pallas_call(
        functools.partial(finish_kernel, cuts),
        grid_spec=pltpu.PrefetchScalarGridSpec(
            num_scalar_prefetch=1, grid=(8,), in_specs=specs, out_specs=place
        ),
        out_shape=jax.ShapeDtypeStruct(shape, jnp.float32),
        input_output_aliases=aliases,
        compiler_params=pltpu.CompilerParams(vmem_limit_bytes=VMEM_BYTES),
        cost_estimate=pl.CostEstimate(flops=0, bytes_accessed=0, transcendentals=0),
        name="finish",
    )(*operands)


def per_device(momentum):
    rows, cols = momentum.shape
    width = cols // 2
    quarter = rows // 4
    tiles = width // TILE
    z = lax.axis_index("row")
    c = lax.axis_index("col")
    core, side = c % 2, c // 2
    left = z < 2
    is_hub = (z == 1) | (z == 2)
    flags = jnp.stack([v.astype(jnp.int32) for v in (left, core, is_hub, side)])
    near_index = left.astype(jnp.int32).reshape(1)

    def over_core(x):
        return lax.ppermute(x, "col", [(k, k ^ 1) for k in range(4)])

    def over_side(x):
        return lax.ppermute(x, "col", [(k, k ^ 2) for k in range(4)])

    def between_hubs(x):
        return lax.ppermute(x, "row", [(1, 2), (2, 1)])

    def skip_one(x):
        return lax.ppermute(x, "row", [(0, 2), (2, 0), (1, 3), (3, 1)])

    def with_end(x):
        return lax.ppermute(x, "row", [(0, 1), (1, 0), (2, 3), (3, 2)])

    def to_end(x):
        return lax.ppermute(x, "row", [(1, 0), (2, 3)])

    def past_hub(x):
        return lax.ppermute(x, "row", [(0, 2), (3, 1), (1, 0), (2, 3)])

    def col_total(x):
        x = jnp.broadcast_to(x, (8, 128))
        x = x + over_core(x)
        return x + over_side(x)

    near, far, squares = take(momentum, near_index)
    beside = with_end(near)
    middle = between_hubs(far)
    norm_part = col_total(jnp.sum(squares))
    norm_part += with_end(norm_part)

    def added(x, y):
        return (x.astype(jnp.float32) + y.astype(jnp.float32)).astype(jnp.bfloat16)

    def over_pair(kept_sent):
        return added(kept_sent[0], over_core(kept_sent[1]))

    def over_sides(half):
        def rows_of(at):
            return lax.dynamic_slice(half, (0, at * quarter, 0), (half.shape[0], quarter, rows))

        return added(rows_of(side), over_side(rows_of(1 - side)))

    barrier = lax.optimization_barrier
    piece = width // 2
    outward = jnp.where(is_hub, middle[:, :piece], far[:, :piece])
    outward, beside, norm_part = barrier((outward, beside, norm_part))
    arrived = past_hub(outward)
    whole = {1: [(middle, width, 0)], 2: [(near, width, 0)], 3: [(beside, width, 0)]}
    pairs_1, pairs_2 = [(2, 2), (3, 3), (3, 2)], [(1, 2), (1, 1), (3, 1)]
    pairs_3, pairs_4 = [(0, 0), (0, 1)], [(0, 2), (0, 3)]
    first = gram_blocks(flags, pairs_1, {r: whole[r] for r in (2, 3)})
    second = gram_blocks(flags, pairs_2, whole)
    norm_sum = (norm_part + skip_one(norm_part))[0, 0]
    middle_later, far_later, first = barrier((middle, far, first))
    outward = jnp.where(is_hub, middle_later[:, piece:], far_later[:, piece:])
    arrived, outward, first, second, norm_sum = barrier((arrived, outward, first, second, norm_sum))

    def halves(h):
        blocks = {1: middle, 2: near, 3: beside}
        return {0: [(distant[h], piece, 0)]} | {r: [(blocks[r], piece, h)] for r in blocks}

    distant = [arrived, past_hub(outward)]
    first = over_pair(first)
    second = over_pair(second)
    (late,) = gram_blocks(flags, pairs_3 + pairs_4, halves(0), split=False)
    first = over_sides(first)
    distant[1], late, first, second = barrier((distant[1], late, first, second))

    other_first = between_hubs(first)
    second = over_sides(second)
    third = gram_blocks(flags, pairs_3, {r: halves(1)[r] for r in (0, 1)}, total=late)
    fourth = gram_blocks(flags, pairs_4, {r: halves(1)[r] for r in (0, 2, 3)}, total=late, total_at=2)
    other_first, second, fourth = barrier((other_first, second, fourth))
    other_second = between_hubs(second)
    third = over_sides(over_pair(third))
    other_third = between_hubs(third)
    fourth = over_sides(over_pair(fourth))
    other_second, fourth = barrier((other_second, fourth))
    other_fourth = between_hubs(fourth)

    spectral_edge = 1.0 + math.sqrt(M / N)
    inverse = 1.0 / (jnp.sqrt(norm_sum / M) * spectral_edge + 1e-07)

    mine, other = {}, {}

    def known(pairs, summed, received):
        for k, pair in enumerate(pairs):
            mine[pair], other[mirror(pair)] = summed[k], received[k]

    def gather(pairs):
        total = jnp.stack([mine[pair].astype(jnp.float32) + other[pair].astype(jnp.float32) for pair in pairs])
        here = (total * (inverse * inverse)).astype(jnp.bfloat16)
        across = over_side(here)
        return [here, over_core(here), across, over_core(across)]

    known(pairs_1, first, other_first)
    known(pairs_2, second, other_second)
    groups = [gather(GATHERED[0])]
    groups[0][1], groups[0][2], other_third = barrier((groups[0][1], groups[0][2], other_third))
    known(pairs_3, third, other_third)
    groups.append(gather(GATHERED[1]))
    passed = jnp.concatenate(distant, axis=1)
    inward = jnp.where(is_hub, passed, far)
    tile_bounds = [0, max(1, tiles * 4 // 9), max(2, tiles * 7 // 9), tiles]
    cuts = [t * TILE for t in tile_bounds]
    inward_first = with_end(inward[:, : cuts[1]])
    swaps = [jnp.stack([block[:, a:b] for block in (beside, near)]) for a, b in zip(cuts[:-1], cuts[1:])]
    swaps[0], other_fourth = barrier((swaps[0], other_fourth))
    swaps[0] = between_hubs(swaps[0])
    groups[1][1], groups[1][2], inward_first, other_fourth = barrier(
        (groups[1][1], groups[1][2], inward_first, other_fourth)
    )
    known(pairs_4, fourth, other_fourth)
    groups.append(gather(GATHERED[2]))

    inward_second = with_end(inward[:, cuts[1] :])
    own, inward_second, *swaps = barrier((poly_rows(flags, groups), inward_second, *swaps))
    pair = over_core(own)
    swaps[1] = between_hubs(swaps[1])
    row_share = to_end(
        jnp.where(
            core == 0,
            lax.dynamic_slice(pair, (c * quarter, 0), (quarter, 4 * rows)),
            lax.dynamic_slice(own, (c * quarter, 0), (quarter, 4 * rows)),
        )
    )
    scale = inverse.reshape(1)
    inwards = [(inward_first, 0), (inward_second, 0), (inward_second, tile_bounds[2] - tile_bounds[1])]
    at_hub, at_end = [], []

    def far_product(k, scale):
        block, at = inwards[k]
        first, last = tile_bounds[k : k + 2]
        blocks = [(swaps[k], 0, 0), (swaps[k], 1, 0), (far, None, first), (block, None, at)]
        (here, there), squares = product(flags, (own, pair), scale, blocks, last - first, True)
        at_hub.append(here)
        at_end.append(to_end(there))
        return squares

    hub_sq = far_product(0, scale)
    scale, hub_sq, row_share = barrier((scale, hub_sq, row_share))
    row_across = over_side(row_share)
    end_rows = [row_share, over_core(row_share), row_across, over_core(row_across)]
    swaps[2] = between_hubs(swaps[2])
    hub_sq += far_product(1, scale)
    at_end[0], scale, hub_sq, inward_first = barrier((at_end[0], scale, hub_sq, inward_first))
    inward = jnp.concatenate([inward_first, inward_second], axis=1)
    blocks = [(passed, None, 0), (jnp.where(is_hub, middle, inward), None, 0), (near, None, 0), (beside, None, 0)]
    (near_part,), near_sq = product(flags, (own, pair, *end_rows), scale, blocks, tiles, False)
    scale, near_sq = barrier((scale, near_sq))
    hub_sq += far_product(2, scale)
    at_end[1], hub_sq = barrier((at_end[1], hub_sq))
    total_sq = col_total(near_sq + jnp.where(is_hub, hub_sq, 0.0))
    total_sq += with_end(total_sq)
    total_sq += skip_one(total_sq)
    factor = (1.0 / (jnp.sqrt(total_sq[0, 0]) / math.sqrt(M * N) + 1e-07)).reshape(1)
    out = finish(flags, factor, [near_part], [0, width], (rows, cols), None)
    return finish(flags, factor, at_hub + at_end, cuts, (rows, cols), out)


def per_device_general(momentum):
    norm_sum = lax.psum(jnp.sum(momentum * momentum), ("col", "row"))
    spectral_edge = 1.0 + math.sqrt(M / N)
    scaled = (momentum / (jnp.sqrt(norm_sum / M) * spectral_edge + 1e-07)).astype(jnp.bfloat16)
    columns = lax.all_gather(scaled, "row", axis=0, tiled=True)
    gram_tile = lax.psum_scatter(
        lax.dot_general(
            columns, scaled, (((1,), (1,)), ((), ())), preferred_element_type=jnp.float32
        ).astype(jnp.bfloat16),
        "col",
        scatter_dimension=0,
        tiled=True,
    )
    left_rows = lax.all_gather(gram_tile, "row", axis=1, tiled=True)
    squared = jnp.dot(
        left_rows,
        lax.all_gather(gram_tile, "col", axis=0, tiled=True),
        preferred_element_type=jnp.float32,
    )
    poly = (coef_cubic * gram_tile.astype(jnp.float32) + coef_quintic * squared).astype(jnp.bfloat16)
    product = lax.dot_general(
        lax.all_gather(poly, "col", axis=0, tiled=True),
        columns,
        (((0,), (0,)), ((), ())),
        preferred_element_type=jnp.float32,
    )
    newton = coef_linear * scaled.astype(jnp.float32) + product
    newton_sq = lax.psum(jnp.sum(newton * newton), ("col", "row"))
    update_rms = jnp.sqrt(newton_sq) / math.sqrt(M * N)
    return newton / (update_rms + 1e-07)


def solution(mesh):
    def update(momentum):
        n_row, n_col = mesh.shape["row"], mesh.shape["col"]
        rows = momentum.shape[0] // (mesh.shape["groups"] * n_row)
        cols = momentum.shape[1] // n_col
        hubs = n_row == 4 and n_col == 4 and rows % STRIP == 0 and cols % (6 * TILE) == 0
        return jax.shard_map(
            per_device if hubs else per_device_general,
            mesh=mesh,
            in_specs=(P(("groups", "row"), "col"),),
            out_specs=P(("groups", "row"), "col"),
            check_vma=False,
        )(momentum)

    return update
```

```python
import functools
import math

import jax
import jax.numpy as jnp
from jax import lax
from jax.experimental import pallas as pl
from jax.experimental.pallas import tpu as pltpu
from jax.sharding import PartitionSpec as P

M = 3584
N = 18432

coef_linear = 3.4445
coef_cubic = -4.775
coef_quintic = 2.0315

TILE = 256
STRIP = 128
VMEM_BYTES = 56 * 2**20

GATHERED = [[(1, 2), (1, 1), (2, 2)], [(0, 0), (3, 3), (0, 1), (3, 2)], [(0, 2), (3, 1), (0, 3)]]


def mirror(pair):
    return pair if sum(pair) == 3 and pair[0] != pair[1] else (3 - pair[0], 3 - pair[1])


def take_kernel(index, near_ref, far_ref, near_out, far_out, sq_ref):
    @pl.when(pl.program_id(0) == 0)
    def _():
        sq_ref[...] = jnp.zeros_like(sq_ref)

    near, far = near_ref[...], far_ref[...]
    near_out[...] = near.astype(jnp.bfloat16)
    far_out[...] = far.astype(jnp.bfloat16)
    sq_ref[...] += jnp.sum(near * near + far * far, axis=0, keepdims=True)


def take(momentum, index):
    rows, cols = momentum.shape
    width = cols // 2
    step = rows // 8
    half = jax.ShapeDtypeStruct((rows, width), jnp.bfloat16)
    return pl.pallas_call(
        take_kernel,
        grid_spec=pltpu.PrefetchScalarGridSpec(
            num_scalar_prefetch=1,
            grid=(8,),
            in_specs=[
                pl.BlockSpec((step, width), lambda t, index: (t, index[0])),
                pl.BlockSpec((step, width), lambda t, index: (t, 1 - index[0])),
            ],
            out_specs=[
                pl.BlockSpec((step, width), lambda t, index: (t, 0)),
                pl.BlockSpec((step, width), lambda t, index: (t, 0)),
                pl.BlockSpec((1, width), lambda t, index: (0, 0)),
            ],
        ),
        out_shape=[half, half, jax.ShapeDtypeStruct((1, width), jnp.float32)],
        compiler_params=pltpu.CompilerParams(vmem_limit_bytes=VMEM_BYTES),
        cost_estimate=pl.CostEstimate(
            flops=4 * rows * width, bytes_accessed=12 * rows * width, transcendentals=0
        ),
        name="take_halves",
    )(index, momentum, momentum)


def gram_kernel(pairs, where, pieces, has_total, split, flags, *refs):
    left, core = flags[0] == 1, flags[1]
    b = pl.program_id(0)
    count = len(where) * pieces
    total = refs[count] if has_total else None
    outs = refs[count + has_total :]

    def make(i, j):
        value = total[0] if has_total else 0.0
        for p in range(pieces):
            x, y = refs[where[i] * pieces + p], refs[where[j] * pieces + p]
            value += lax.dot_general(
                x[...], y[...], (((1,), (1,)), ((), ())), preferred_element_type=jnp.float32
            )
        if not split:
            outs[0][0] = value
            return
        keep, send, whole = outs
        share = keep.shape[1]
        whole[...] = value.astype(jnp.bfloat16)
        keep[0] = whole[pl.ds(pl.multiple_of(core * share, 16), share), :]
        send[0] = whole[pl.ds(pl.multiple_of((1 - core) * share, 16), share), :]

    for k, (i, j) in enumerate(pairs):
        if (i, j) in ((1, 2), (0, 3)):
            pl.when((b == k) & left)(functools.partial(make, j, i))
            pl.when((b == k) & jnp.logical_not(left))(functools.partial(make, i, j))
        else:
            pl.when(b == k)(functools.partial(make, i, j))


def gram_blocks(flags, pairs, operands, total=None, total_at=0, split=True):
    where = {r: k for k, r in enumerate(operands)}
    pieces = len(operands[pairs[0][0]])
    rows = operands[pairs[0][0]][0][0].shape[0]
    share = rows // 2
    used = [piece for r in operands for piece in operands[r]]
    specs = [pl.BlockSpec((rows, width), lambda b, flags, at=at: (0, at)) for _, width, at in used]
    arrays = [array for array, _, _ in used]
    if total is not None:
        specs.append(
            pl.BlockSpec(
                (1, rows, rows), lambda b, flags: (total_at + b, 0, 0)
            )
        )
        arrays.append(total)
    count = len(pairs)
    if split:
        out_specs = [pl.BlockSpec((1, share, rows), lambda b, flags: (b, 0, 0))] * 2
        scratch = [pltpu.VMEM((rows, rows), jnp.bfloat16)]
        out_shape = [jax.ShapeDtypeStruct((count, share, rows), jnp.bfloat16)] * 2
    else:
        out_specs = [pl.BlockSpec((1, rows, rows), lambda b, flags: (b, 0, 0))]
        scratch = []
        out_shape = [jax.ShapeDtypeStruct((count, rows, rows), jnp.float32)]
    return pl.pallas_call(
        functools.partial(gram_kernel, pairs, where, pieces, int(total is not None), split),
        grid_spec=pltpu.PrefetchScalarGridSpec(
            num_scalar_prefetch=1, grid=(count,), in_specs=specs, out_specs=out_specs, scratch_shapes=scratch
        ),
        out_shape=out_shape,
        compiler_params=pltpu.CompilerParams(vmem_limit_bytes=VMEM_BYTES),
        cost_estimate=pl.CostEstimate(flops=0, bytes_accessed=0, transcendentals=0),
        name="gram_blocks",
    )(flags, *arrays)


def transpose_block(ref, rows, source, target):
    @pl.loop(0, rows // STRIP)
    def _(s):
        part = ref[
            pl.ds(pl.multiple_of(source[0] * rows, STRIP), rows),
            pl.ds(pl.multiple_of(source[1] * rows + s * STRIP, STRIP), STRIP),
        ]
        ref[
            pl.ds(pl.multiple_of(target[0] * rows + s * STRIP, STRIP), STRIP),
            pl.ds(pl.multiple_of(target[1] * rows, STRIP), rows),
        ] = part.T


def poly_kernel(flags, *refs):
    *parts, out_ref, gram, sems = refs
    rows = out_ref.shape[0]
    quarter = rows // 4
    left, core, side = flags[0], flags[1], flags[3]
    b = pl.program_id(0)

    @pl.when(b == 0)
    def _():
        places = [
            2 * core + side,
            2 * (1 - core) + side,
            2 * core + 1 - side,
            2 * (1 - core) + 1 - side,
        ]
        copies, turned = [], []
        for g, pairs in enumerate(GATHERED):
            for k, (i, j) in enumerate(pairs):
                if (i, j) in ((1, 2), (0, 3)):
                    i, j = jnp.where(left == 1, j, i), jnp.where(left == 1, i, j)
                for q, place in enumerate(places):
                    copies.append(
                        pltpu.make_async_copy(
                            parts[4 * g + q].at[k],
                            gram.at[
                                pl.ds(pl.multiple_of(i * rows + place * quarter, 16), quarter),
                                pl.ds(pl.multiple_of(j * rows, STRIP), rows),
                            ],
                            sems.at[len(copies)],
                        )
                    )
                if pairs[k][0] != pairs[k][1]:
                    turned.append((i, j))
        for copy in copies:
            copy.start()
        for copy in copies:
            copy.wait()
        for i, j in turned:
            transpose_block(gram, rows, (i, j), (j, i))

    at_i = pl.multiple_of((2 + core) * rows, STRIP)
    width = out_ref.shape[1]
    at_j = pl.multiple_of(b * width, STRIP)
    squared = jnp.dot(
        gram[pl.ds(at_i, rows), :], gram[:, pl.ds(at_j, width)], preferred_element_type=jnp.float32
    )
    here = gram[pl.ds(at_i, rows), pl.ds(at_j, width)].astype(jnp.float32)
    out_ref[...] = (coef_cubic * here + coef_quintic * squared).astype(jnp.bfloat16)


def poly_rows(flags, groups):
    rows = groups[0][0].shape[2]
    order = 4 * rows
    width = 2 * TILE
    return pl.pallas_call(
        poly_kernel,
        grid_spec=pltpu.PrefetchScalarGridSpec(
            num_scalar_prefetch=1,
            grid=(order // width,),
            in_specs=[pl.BlockSpec(memory_space=pl.ANY)] * 12,
            out_specs=pl.BlockSpec((rows, width), lambda b, flags: (0, b)),
            scratch_shapes=[pltpu.VMEM((order, order), jnp.bfloat16), pltpu.SemaphoreType.DMA((40,))],
        ),
        out_shape=jax.ShapeDtypeStruct((rows, order), jnp.bfloat16),
        compiler_params=pltpu.CompilerParams(vmem_limit_bytes=VMEM_BYTES),
        cost_estimate=pl.CostEstimate(flops=0, bytes_accessed=0, transcendentals=0),
        name="poly_rows",
    )(flags, *[x for group in groups for x in group])


def product_kernel(is_far, cut, flags, own, pair, *refs):
    end_rows, refs = ((), refs) if is_far else (refs[:4], refs[4:])
    inverse, blocks, inward, outs = refs[0], refs[1:5], () if is_far else refs[5:7], refs[5 if is_far else 7 : -4]
    sq_ref, poly, raw, sems = refs[-4:]
    rows = own.shape[0]

    @pl.when(pl.program_id(0) == 0)
    def _():
        sq_ref[...] = jnp.zeros_like(sq_ref)

        def load(pairs):
            copies = [
                pltpu.make_async_copy(source, target, sems.at[k]) for k, (source, target) in enumerate(pairs)
            ]
            for copy in copies:
                copy.start()
            for copy in copies:
                copy.wait()

        if is_far:
            at = pl.multiple_of(flags[1] * rows, 16)
            load([(own, poly.at[pl.ds(at, rows), :]), (pair, poly.at[pl.ds(rows - at, rows), :])])
        else:
            @pl.when((flags[2] == 1) & (flags[1] == 0))
            def _():
                load([(own, poly)])

            @pl.when((flags[2] == 1) & (flags[1] == 1))
            def _():
                load([(pair, poly)])

            @pl.when(flags[2] == 0)
            def _():
                core, side = flags[1], flags[3]
                quarter = rows // 4
                places = [2 * side + core, 2 * side + 1 - core, 2 * (1 - side) + core, 2 * (1 - side) + 1 - core]
                load(
                    [
                        (
                            part.at[:, m * rows : (m + 1) * rows],
                            poly.at[
                                pl.ds(pl.multiple_of(place * quarter, 16), quarter),
                                (m ^ 1) * rows : ((m ^ 1) + 1) * rows,
                            ],
                        )
                        for part, place in zip(end_rows, places)
                        for m in range(4)
                    ]
                )

    for r, block in enumerate(blocks):
        raw[r * rows : (r + 1) * rows, :] = block[...]
    for k, block in enumerate(inward):

        @pl.when((flags[2] == 0) & ((pl.program_id(0) >= cut) == (k == 1)))
        def _(block=block):
            raw[rows : 2 * rows, :] = block[...]

    for k, out in enumerate(outs):
        product = jnp.dot(poly[k * rows : (k + 1) * rows, :], raw[...], preferred_element_type=jnp.float32)
        own_rows = raw[(2 + k) * rows : (3 + k) * rows, :].astype(jnp.float32)
        newton = inverse[0] * (coef_linear * own_rows + product)
        sq_ref[...] += jnp.sum(newton * newton, axis=0, keepdims=True)
        out[...] = newton.astype(jnp.bfloat16)


def product(flags, polys, inverse, blocks, tiles, is_far, inward=()):
    rows, order = polys[0].shape
    count = 2 if is_far else 1
    block_specs = [
        pl.BlockSpec((rows, TILE), lambda t, flags, at=at: (0, at + t))
        if lead is None
        else pl.BlockSpec((None, rows, TILE), lambda t, flags, at=at, lead=lead: (lead, 0, at + t))
        for _, lead, at in blocks
    ] + [
        pl.BlockSpec((rows, TILE), lambda t, flags, a=a, b=b: (0, jnp.clip(t, a, b - 1) - a))
        for _, a, b in inward
    ]
    there = pl.BlockSpec((rows, TILE), lambda t, flags: (0, t))
    *newton, squares = pl.pallas_call(
        functools.partial(product_kernel, is_far, inward[0][2] if inward else 0),
        grid_spec=pltpu.PrefetchScalarGridSpec(
            num_scalar_prefetch=1,
            grid=(tiles,),
            in_specs=[pl.BlockSpec(memory_space=pl.ANY)] * len(polys)
            + [pl.BlockSpec(memory_space=pltpu.SMEM)]
            + block_specs,
            out_specs=[there] * count + [pl.BlockSpec((1, TILE), lambda t, flags: (0, 0))],
            scratch_shapes=[
                pltpu.VMEM((count * rows, order), jnp.bfloat16),
                pltpu.VMEM((order, TILE), jnp.bfloat16),
                pltpu.SemaphoreType.DMA((16,)),
            ],
        ),
        out_shape=[jax.ShapeDtypeStruct((rows, tiles * TILE), jnp.bfloat16)] * count
        + [jax.ShapeDtypeStruct((1, TILE), jnp.float32)],
        compiler_params=pltpu.CompilerParams(vmem_limit_bytes=VMEM_BYTES),
        cost_estimate=pl.CostEstimate(flops=0, bytes_accessed=0, transcendentals=0),
        name="product_far" if is_far else "product_near",
    )(flags, *polys, inverse, *[array for array, _, _ in (*blocks, *inward)])
    return newton, jnp.sum(squares)


def finish_kernel(cuts, flags, factor, near, *refs):
    out_ref = refs[-1]
    chunks = len(cuts) - 1
    width = near.shape[1]
    near_at = pl.multiple_of(flags[0] * width, STRIP)
    far_at = width - near_at
    out_ref[:, pl.ds(near_at, width)] = near[...].astype(jnp.float32) * factor[0]
    for k, ref in enumerate(refs[:-1]):
        first, last = cuts[k % chunks : k % chunks + 2]

        @pl.when((flags[2] == 1) == (k < chunks))
        def _(ref=ref, first=first, last=last):
            place = pl.ds(pl.multiple_of(far_at + first, STRIP), last - first)
            out_ref[:, place] = ref[...].astype(jnp.float32) * factor[0]


def finish(flags, factor, near, parts, cuts, shape):
    rows, cols = shape
    step = rows // 8
    specs = [pl.BlockSpec(memory_space=pltpu.SMEM)]
    specs += [pl.BlockSpec((step, part.shape[1]), lambda t, flags: (t, 0)) for part in (near, *parts)]
    return pl.pallas_call(
        functools.partial(finish_kernel, cuts),
        grid_spec=pltpu.PrefetchScalarGridSpec(
            num_scalar_prefetch=1,
            grid=(8,),
            in_specs=specs,
            out_specs=pl.BlockSpec((step, cols), lambda t, flags: (t, 0)),
        ),
        out_shape=jax.ShapeDtypeStruct(shape, jnp.float32),
        compiler_params=pltpu.CompilerParams(vmem_limit_bytes=VMEM_BYTES),
        cost_estimate=pl.CostEstimate(flops=0, bytes_accessed=0, transcendentals=0),
        name="finish",
    )(flags, factor, near, *parts)


def per_device(momentum):
    rows, cols = momentum.shape
    width = cols // 2
    quarter = rows // 4
    tiles = width // TILE
    z = lax.axis_index("row")
    c = lax.axis_index("col")
    core, side = c % 2, c // 2
    left = z < 2
    is_hub = (z == 1) | (z == 2)
    flags = jnp.stack([v.astype(jnp.int32) for v in (left, core, is_hub, side)])
    near_index = left.astype(jnp.int32).reshape(1)

    def over_core(x):
        return lax.ppermute(x, "col", [(k, k ^ 1) for k in range(4)])

    def over_side(x):
        return lax.ppermute(x, "col", [(k, k ^ 2) for k in range(4)])

    def between_hubs(x):
        return lax.ppermute(x, "row", [(1, 2), (2, 1)])

    def skip_one(x):
        return lax.ppermute(x, "row", [(0, 2), (2, 0), (1, 3), (3, 1)])

    def with_end(x):
        return lax.ppermute(x, "row", [(0, 1), (1, 0), (2, 3), (3, 2)])

    def to_end(x):
        return lax.ppermute(x, "row", [(1, 0), (2, 3)])

    def past_hub(x):
        return lax.ppermute(x, "row", [(0, 2), (3, 1), (1, 0), (2, 3)])

    def col_total(x):
        x = jnp.broadcast_to(x, (8, 128))
        x = x + over_core(x)
        return x + over_side(x)

    near, far, squares = take(momentum, near_index)
    beside = with_end(near)
    middle = between_hubs(far)
    norm_part = col_total(jnp.sum(squares))
    norm_part += with_end(norm_part)

    def added(x, y):
        return (x.astype(jnp.float32) + y.astype(jnp.float32)).astype(jnp.bfloat16)

    def over_pair(kept_sent):
        return added(kept_sent[0], over_core(kept_sent[1]))

    def over_sides(half):
        def rows_of(at):
            return lax.dynamic_slice(half, (0, at * quarter, 0), (half.shape[0], quarter, rows))

        return added(rows_of(side), over_side(rows_of(1 - side)))

    barrier = lax.optimization_barrier
    piece = width // 2
    outward = jnp.where(is_hub, middle[:, :piece], far[:, :piece])
    outward, beside, norm_part = barrier((outward, beside, norm_part))
    arrived = past_hub(outward)
    whole = {1: [(middle, width, 0)], 2: [(near, width, 0)], 3: [(beside, width, 0)]}
    pairs_1, pairs_2 = [(2, 2), (3, 3), (3, 2)], [(1, 2), (1, 1), (3, 1)]
    pairs_3, pairs_4 = [(0, 0), (0, 1)], [(0, 2), (0, 3)]
    first = gram_blocks(flags, pairs_1, {r: whole[r] for r in (2, 3)})
    second = gram_blocks(flags, pairs_2, whole)
    norm_sum = (norm_part + skip_one(norm_part))[0, 0]
    middle_later, far_later, first = barrier((middle, far, first))
    outward = jnp.where(is_hub, middle_later[:, piece:], far_later[:, piece:])
    arrived, outward, first, second, norm_sum = barrier((arrived, outward, first, second, norm_sum))

    def halves(h):
        blocks = {1: middle, 2: near, 3: beside}
        return {0: [(distant[h], piece, 0)]} | {r: [(blocks[r], piece, h)] for r in blocks}

    distant = [arrived, past_hub(outward)]
    first = over_pair(first)
    second = over_pair(second)
    (late,) = gram_blocks(flags, pairs_3 + pairs_4, halves(0), split=False)
    first = over_sides(first)
    distant[1], late, first, second = barrier((distant[1], late, first, second))

    other_first = between_hubs(first)
    second = over_sides(second)
    third = gram_blocks(flags, pairs_3, {r: halves(1)[r] for r in (0, 1)}, total=late)
    fourth = gram_blocks(flags, pairs_4, {r: halves(1)[r] for r in (0, 2, 3)}, total=late, total_at=2)
    other_first, second, fourth = barrier((other_first, second, fourth))
    other_second = between_hubs(second)
    third = over_sides(over_pair(third))
    other_third = between_hubs(third)
    fourth = over_sides(over_pair(fourth))
    other_second, fourth = barrier((other_second, fourth))
    other_fourth = between_hubs(fourth)

    spectral_edge = 1.0 + math.sqrt(M / N)
    inverse = 1.0 / (jnp.sqrt(norm_sum / M) * spectral_edge + 1e-07)

    mine, other = {}, {}

    def known(pairs, summed, received):
        for k, pair in enumerate(pairs):
            mine[pair], other[mirror(pair)] = summed[k], received[k]

    def gather(pairs):
        total = jnp.stack([mine[pair].astype(jnp.float32) + other[pair].astype(jnp.float32) for pair in pairs])
        here = (total * (inverse * inverse)).astype(jnp.bfloat16)
        across = over_side(here)
        return [here, over_core(here), across, over_core(across)]

    known(pairs_1, first, other_first)
    known(pairs_2, second, other_second)
    groups = [gather(GATHERED[0])]
    groups[0][1], groups[0][2], other_third = barrier((groups[0][1], groups[0][2], other_third))
    known(pairs_3, third, other_third)
    groups.append(gather(GATHERED[1]))
    passed = jnp.concatenate(distant, axis=1)
    inward = jnp.where(is_hub, passed, far)
    tile_bounds = [0, max(1, tiles * 4 // 9), max(2, tiles * 7 // 9), tiles]
    cuts = [t * TILE for t in tile_bounds]
    inward_first = with_end(inward[:, : cuts[1]])
    swaps = [jnp.stack([block[:, a:b] for block in (beside, near)]) for a, b in zip(cuts[:-1], cuts[1:])]
    *swaps, other_fourth = barrier((*swaps, other_fourth))
    swaps[0] = between_hubs(swaps[0])
    groups[1][1], groups[1][2], inward_first, other_fourth = barrier(
        (groups[1][1], groups[1][2], inward_first, other_fourth)
    )
    known(pairs_4, fourth, other_fourth)
    groups.append(gather(GATHERED[2]))

    inward_second = with_end(inward[:, cuts[1] :])
    own, inward_second, *swaps = barrier((poly_rows(flags, groups), inward_second, *swaps))
    pair = over_core(own)
    swaps[1] = between_hubs(swaps[1])
    row_share = to_end(
        jnp.where(
            core == 0,
            lax.dynamic_slice(pair, (c * quarter, 0), (quarter, 4 * rows)),
            lax.dynamic_slice(own, (c * quarter, 0), (quarter, 4 * rows)),
        )
    )
    scale = inverse.reshape(1)
    inwards = [(inward_first, 0), (inward_second, 0), (inward_second, tile_bounds[2] - tile_bounds[1])]
    at_hub, at_end = [], []

    def far_product(k, scale):
        block, at = inwards[k]
        first, last = tile_bounds[k : k + 2]
        blocks = [(swaps[k], 0, 0), (swaps[k], 1, 0), (far, None, first), (block, None, at)]
        (here, there), squares = product(flags, (own, pair), scale, blocks, last - first, True)
        at_hub.append(here)
        at_end.append(to_end(there))
        return squares

    hub_sq = far_product(0, scale)
    hub_sq, row_share = barrier((hub_sq, row_share))
    row_across = over_side(row_share)
    scale, hub_sq, swaps[1] = barrier((scale, hub_sq, swaps[1]))
    swaps[2] = between_hubs(swaps[2])
    hub_sq += far_product(1, scale)
    at_end[0], scale, hub_sq, row_across = barrier((at_end[0], scale, hub_sq, row_across))
    end_rows = [row_share, over_core(row_share), row_across, over_core(row_across)]
    blocks = [(passed, None, 0), (middle, None, 0), (near, None, 0), (beside, None, 0)]
    inward = [(inward_first, 0, tile_bounds[1]), (inward_second, tile_bounds[1], tiles)]
    (near_part,), near_sq = product(flags, (own, pair, *end_rows), scale, blocks, tiles, False, inward)
    scale, near_sq = barrier((scale, near_sq))
    hub_sq += far_product(2, scale)
    at_end[1], hub_sq = barrier((at_end[1], hub_sq))
    total_sq = col_total(near_sq + jnp.where(is_hub, hub_sq, 0.0))
    total_sq += with_end(total_sq)
    total_sq += skip_one(total_sq)
    factor = (1.0 / (jnp.sqrt(total_sq[0, 0]) / math.sqrt(M * N) + 1e-07)).reshape(1)
    return finish(flags, factor, near_part, at_hub + at_end, cuts, (rows, cols))


def per_device_general(momentum):
    norm_sum = lax.psum(jnp.sum(momentum * momentum), ("col", "row"))
    spectral_edge = 1.0 + math.sqrt(M / N)
    scaled = (momentum / (jnp.sqrt(norm_sum / M) * spectral_edge + 1e-07)).astype(jnp.bfloat16)
    columns = lax.all_gather(scaled, "row", axis=0, tiled=True)
    gram_tile = lax.psum_scatter(
        lax.dot_general(
            columns, scaled, (((1,), (1,)), ((), ())), preferred_element_type=jnp.float32
        ).astype(jnp.bfloat16),
        "col",
        scatter_dimension=0,
        tiled=True,
    )
    left_rows = lax.all_gather(gram_tile, "row", axis=1, tiled=True)
    squared = jnp.dot(
        left_rows,
        lax.all_gather(gram_tile, "col", axis=0, tiled=True),
        preferred_element_type=jnp.float32,
    )
    poly = (coef_cubic * gram_tile.astype(jnp.float32) + coef_quintic * squared).astype(jnp.bfloat16)
    product = lax.dot_general(
        lax.all_gather(poly, "col", axis=0, tiled=True),
        columns,
        (((0,), (0,)), ((), ())),
        preferred_element_type=jnp.float32,
    )
    newton = coef_linear * scaled.astype(jnp.float32) + product
    newton_sq = lax.psum(jnp.sum(newton * newton), ("col", "row"))
    update_rms = jnp.sqrt(newton_sq) / math.sqrt(M * N)
    return newton / (update_rms + 1e-07)


def solution(mesh):
    def update(momentum):
        n_row, n_col = mesh.shape["row"], mesh.shape["col"]
        rows = momentum.shape[0] // (mesh.shape["groups"] * n_row)
        cols = momentum.shape[1] // n_col
        hubs = n_row == 4 and n_col == 4 and rows % STRIP == 0 and cols % (6 * TILE) == 0
        return jax.shard_map(
            per_device if hubs else per_device_general,
            mesh=mesh,
            in_specs=(P(("groups", "row"), "col"),),
            out_specs=P(("groups", "row"), "col"),
            check_vma=False,
        )(momentum)

    return update
```

```python
import functools
import math

import jax
import jax.numpy as jnp
from jax import lax
from jax.experimental import pallas as pl
from jax.experimental.pallas import tpu as pltpu
from jax.sharding import PartitionSpec as P

M = 3584
N = 18432

coef_linear = 3.4445
coef_cubic = -4.775
coef_quintic = 2.0315

TILE = 256
STRIP = 128
VMEM_BYTES = 56 * 2**20

GATHERED = [[(1, 2), (1, 1), (2, 2)], [(0, 0), (3, 3), (0, 1), (3, 2)], [(0, 2), (3, 1), (0, 3)]]


def mirror(pair):
    return pair if sum(pair) == 3 and pair[0] != pair[1] else (3 - pair[0], 3 - pair[1])


def take_kernel(index, near_ref, far_ref, near_out, far_out, sq_ref):
    @pl.when(pl.program_id(0) == 0)
    def _():
        sq_ref[...] = jnp.zeros_like(sq_ref)

    near, far = near_ref[...], far_ref[...]
    near_out[...] = near.astype(jnp.bfloat16)
    far_out[...] = far.astype(jnp.bfloat16)
    sq_ref[...] += jnp.sum(near * near + far * far, axis=0, keepdims=True)


def take(momentum, index):
    rows, cols = momentum.shape
    width = cols // 2
    step = rows // 8
    half = jax.ShapeDtypeStruct((rows, width), jnp.bfloat16)
    return pl.pallas_call(
        take_kernel,
        grid_spec=pltpu.PrefetchScalarGridSpec(
            num_scalar_prefetch=1,
            grid=(8,),
            in_specs=[
                pl.BlockSpec((step, width), lambda t, index: (t, index[0])),
                pl.BlockSpec((step, width), lambda t, index: (t, 1 - index[0])),
            ],
            out_specs=[
                pl.BlockSpec((step, width), lambda t, index: (t, 0)),
                pl.BlockSpec((step, width), lambda t, index: (t, 0)),
                pl.BlockSpec((1, width), lambda t, index: (0, 0)),
            ],
        ),
        out_shape=[half, half, jax.ShapeDtypeStruct((1, width), jnp.float32)],
        compiler_params=pltpu.CompilerParams(vmem_limit_bytes=VMEM_BYTES),
        cost_estimate=pl.CostEstimate(
            flops=4 * rows * width, bytes_accessed=12 * rows * width, transcendentals=0
        ),
        name="take_halves",
    )(index, momentum, momentum)


def gram_kernel(pairs, where, pieces, has_total, split, flags, *refs):
    left, core = flags[0] == 1, flags[1]
    b = pl.program_id(0)
    count = len(where) * pieces
    total = refs[count] if has_total else None
    outs = refs[count + has_total :]

    def make(i, j):
        value = total[0] if has_total else 0.0
        for p in range(pieces):
            x, y = refs[where[i] * pieces + p], refs[where[j] * pieces + p]
            value += lax.dot_general(
                x[...], y[...], (((1,), (1,)), ((), ())), preferred_element_type=jnp.float32
            )
        if not split:
            outs[0][0] = value
            return
        keep, send, whole = outs
        share = keep.shape[1]
        whole[...] = value.astype(jnp.bfloat16)
        keep[0] = whole[pl.ds(pl.multiple_of(core * share, 16), share), :]
        send[0] = whole[pl.ds(pl.multiple_of((1 - core) * share, 16), share), :]

    for k, (i, j) in enumerate(pairs):
        if (i, j) in ((1, 2), (0, 3)):
            pl.when((b == k) & left)(functools.partial(make, j, i))
            pl.when((b == k) & jnp.logical_not(left))(functools.partial(make, i, j))
        else:
            pl.when(b == k)(functools.partial(make, i, j))


def gram_blocks(flags, pairs, operands, total=None, total_at=0, split=True):
    where = {r: k for k, r in enumerate(operands)}
    pieces = len(operands[pairs[0][0]])
    rows = operands[pairs[0][0]][0][0].shape[0]
    share = rows // 2
    used = [piece for r in operands for piece in operands[r]]
    specs = [pl.BlockSpec((rows, width), lambda b, flags, at=at: (0, at)) for _, width, at in used]
    arrays = [array for array, _, _ in used]
    if total is not None:
        specs.append(
            pl.BlockSpec(
                (1, rows, rows), lambda b, flags: (total_at + b, 0, 0)
            )
        )
        arrays.append(total)
    count = len(pairs)
    if split:
        out_specs = [pl.BlockSpec((1, share, rows), lambda b, flags: (b, 0, 0))] * 2
        scratch = [pltpu.VMEM((rows, rows), jnp.bfloat16)]
        out_shape = [jax.ShapeDtypeStruct((count, share, rows), jnp.bfloat16)] * 2
    else:
        out_specs = [pl.BlockSpec((1, rows, rows), lambda b, flags: (b, 0, 0))]
        scratch = []
        out_shape = [jax.ShapeDtypeStruct((count, rows, rows), jnp.float32)]
    return pl.pallas_call(
        functools.partial(gram_kernel, pairs, where, pieces, int(total is not None), split),
        grid_spec=pltpu.PrefetchScalarGridSpec(
            num_scalar_prefetch=1, grid=(count,), in_specs=specs, out_specs=out_specs, scratch_shapes=scratch
        ),
        out_shape=out_shape,
        compiler_params=pltpu.CompilerParams(vmem_limit_bytes=VMEM_BYTES),
        cost_estimate=pl.CostEstimate(flops=0, bytes_accessed=0, transcendentals=0),
        name="gram_blocks",
    )(flags, *arrays)


def transpose_block(ref, rows, source, target):
    @pl.loop(0, rows // STRIP)
    def _(s):
        part = ref[
            pl.ds(pl.multiple_of(source[0] * rows, STRIP), rows),
            pl.ds(pl.multiple_of(source[1] * rows + s * STRIP, STRIP), STRIP),
        ]
        ref[
            pl.ds(pl.multiple_of(target[0] * rows + s * STRIP, STRIP), STRIP),
            pl.ds(pl.multiple_of(target[1] * rows, STRIP), rows),
        ] = part.T


def poly_kernel(flags, *refs):
    *parts, out_ref, gram, sems = refs
    rows = out_ref.shape[0]
    quarter = rows // 4
    left, core, side = flags[0], flags[1], flags[3]
    b = pl.program_id(0)

    @pl.when(b == 0)
    def _():
        places = [
            2 * core + side,
            2 * (1 - core) + side,
            2 * core + 1 - side,
            2 * (1 - core) + 1 - side,
        ]
        copies, turned = [], []
        for g, pairs in enumerate(GATHERED):
            for k, (i, j) in enumerate(pairs):
                if (i, j) in ((1, 2), (0, 3)):
                    i, j = jnp.where(left == 1, j, i), jnp.where(left == 1, i, j)
                for q, place in enumerate(places):
                    copies.append(
                        pltpu.make_async_copy(
                            parts[4 * g + q].at[k],
                            gram.at[
                                pl.ds(pl.multiple_of(i * rows + place * quarter, 16), quarter),
                                pl.ds(pl.multiple_of(j * rows, STRIP), rows),
                            ],
                            sems.at[len(copies)],
                        )
                    )
                if pairs[k][0] != pairs[k][1]:
                    turned.append((i, j))
        for copy in copies:
            copy.start()
        for copy in copies:
            copy.wait()
        for i, j in turned:
            transpose_block(gram, rows, (i, j), (j, i))

    at_i = pl.multiple_of((2 + core) * rows, STRIP)
    width = out_ref.shape[1]
    at_j = pl.multiple_of(b * width, STRIP)
    squared = jnp.dot(
        gram[pl.ds(at_i, rows), :], gram[:, pl.ds(at_j, width)], preferred_element_type=jnp.float32
    )
    here = gram[pl.ds(at_i, rows), pl.ds(at_j, width)].astype(jnp.float32)
    out_ref[...] = (coef_cubic * here + coef_quintic * squared).astype(jnp.bfloat16)


def poly_rows(flags, groups):
    rows = groups[0][0].shape[2]
    order = 4 * rows
    width = 2 * TILE
    return pl.pallas_call(
        poly_kernel,
        grid_spec=pltpu.PrefetchScalarGridSpec(
            num_scalar_prefetch=1,
            grid=(order // width,),
            in_specs=[pl.BlockSpec(memory_space=pl.ANY)] * 12,
            out_specs=pl.BlockSpec((rows, width), lambda b, flags: (0, b)),
            scratch_shapes=[pltpu.VMEM((order, order), jnp.bfloat16), pltpu.SemaphoreType.DMA((40,))],
        ),
        out_shape=jax.ShapeDtypeStruct((rows, order), jnp.bfloat16),
        compiler_params=pltpu.CompilerParams(vmem_limit_bytes=VMEM_BYTES),
        cost_estimate=pl.CostEstimate(flops=0, bytes_accessed=0, transcendentals=0),
        name="poly_rows",
    )(flags, *[x for group in groups for x in group])


def product_kernel(is_far, cut, flags, own, pair, *refs):
    end_rows, refs = ((), refs) if is_far else (refs[:4], refs[4:])
    inverse, blocks, inward, outs = refs[0], refs[1:5], () if is_far else refs[5:7], refs[5 if is_far else 7 : -4]
    sq_ref, poly, raw, sems = refs[-4:]
    rows = own.shape[0]

    @pl.when(pl.program_id(0) == 0)
    def _():
        sq_ref[...] = jnp.zeros_like(sq_ref)

        def load(pairs):
            copies = [
                pltpu.make_async_copy(source, target, sems.at[k]) for k, (source, target) in enumerate(pairs)
            ]
            for copy in copies:
                copy.start()
            for copy in copies:
                copy.wait()

        if is_far:
            at = pl.multiple_of(flags[1] * rows, 16)
            load([(own, poly.at[pl.ds(at, rows), :]), (pair, poly.at[pl.ds(rows - at, rows), :])])
        else:
            @pl.when((flags[2] == 1) & (flags[1] == 0))
            def _():
                load([(own, poly)])

            @pl.when((flags[2] == 1) & (flags[1] == 1))
            def _():
                load([(pair, poly)])

            @pl.when(flags[2] == 0)
            def _():
                core, side = flags[1], flags[3]
                quarter = rows // 4
                places = [2 * side + core, 2 * side + 1 - core, 2 * (1 - side) + core, 2 * (1 - side) + 1 - core]
                load(
                    [
                        (
                            part.at[:, m * rows : (m + 1) * rows],
                            poly.at[
                                pl.ds(pl.multiple_of(place * quarter, 16), quarter),
                                (m ^ 1) * rows : ((m ^ 1) + 1) * rows,
                            ],
                        )
                        for part, place in zip(end_rows, places)
                        for m in range(4)
                    ]
                )

    for r, block in enumerate(blocks):
        raw[r * rows : (r + 1) * rows, :] = block[...]
    for k, block in enumerate(inward):

        @pl.when((flags[2] == 0) & ((pl.program_id(0) >= cut) == (k == 1)))
        def _(block=block):
            raw[rows : 2 * rows, :] = block[...]

    for k, out in enumerate(outs):
        product = jnp.dot(poly[k * rows : (k + 1) * rows, :], raw[...], preferred_element_type=jnp.float32)
        own_rows = raw[(2 + k) * rows : (3 + k) * rows, :].astype(jnp.float32)
        newton = inverse[0] * (coef_linear * own_rows + product)
        sq_ref[...] += jnp.sum(newton * newton, axis=0, keepdims=True)
        out[...] = newton.astype(jnp.bfloat16)


def product(flags, polys, inverse, blocks, tiles, is_far, inward=()):
    rows, order = polys[0].shape
    count = 2 if is_far else 1
    block_specs = [
        pl.BlockSpec((rows, TILE), lambda t, flags, at=at: (0, at + t))
        if lead is None
        else pl.BlockSpec((None, rows, TILE), lambda t, flags, at=at, lead=lead: (lead, 0, at + t))
        for _, lead, at in blocks
    ] + [
        pl.BlockSpec((rows, TILE), lambda t, flags, a=a, b=b: (0, jnp.clip(t, a, b - 1) - a))
        for _, a, b in inward
    ]
    there = pl.BlockSpec((rows, TILE), lambda t, flags: (0, t))
    *newton, squares = pl.pallas_call(
        functools.partial(product_kernel, is_far, inward[0][2] if inward else 0),
        grid_spec=pltpu.PrefetchScalarGridSpec(
            num_scalar_prefetch=1,
            grid=(tiles,),
            in_specs=[pl.BlockSpec(memory_space=pl.ANY)] * len(polys)
            + [pl.BlockSpec(memory_space=pltpu.SMEM)]
            + block_specs,
            out_specs=[there] * count + [pl.BlockSpec((1, TILE), lambda t, flags: (0, 0))],
            scratch_shapes=[
                pltpu.VMEM((count * rows, order), jnp.bfloat16),
                pltpu.VMEM((order, TILE), jnp.bfloat16),
                pltpu.SemaphoreType.DMA((16,)),
            ],
        ),
        out_shape=[jax.ShapeDtypeStruct((rows, tiles * TILE), jnp.bfloat16)] * count
        + [jax.ShapeDtypeStruct((1, TILE), jnp.float32)],
        compiler_params=pltpu.CompilerParams(vmem_limit_bytes=VMEM_BYTES),
        cost_estimate=pl.CostEstimate(flops=0, bytes_accessed=0, transcendentals=0),
        name="product_far" if is_far else "product_near",
    )(flags, *polys, inverse, *[array for array, _, _ in (*blocks, *inward)])
    return newton, jnp.sum(squares)


def finish_kernel(cuts, flags, factor, near, *refs):
    out_ref = refs[-1]
    chunks = len(cuts) - 1
    width = near.shape[1]
    near_at = pl.multiple_of(flags[0] * width, STRIP)
    far_at = width - near_at
    out_ref[:, pl.ds(near_at, width)] = near[...].astype(jnp.float32) * factor[0]
    for k, ref in enumerate(refs[:-1]):
        first, last = cuts[k % chunks : k % chunks + 2]

        @pl.when((flags[2] == 1) == (k < chunks))
        def _(ref=ref, first=first, last=last):
            place = pl.ds(pl.multiple_of(far_at + first, STRIP), last - first)
            out_ref[:, place] = ref[...].astype(jnp.float32) * factor[0]


def finish(flags, factor, near, parts, cuts, shape):
    rows, cols = shape
    step = rows // 8
    specs = [pl.BlockSpec(memory_space=pltpu.SMEM)]
    specs += [pl.BlockSpec((step, part.shape[1]), lambda t, flags: (t, 0)) for part in (near, *parts)]
    return pl.pallas_call(
        functools.partial(finish_kernel, cuts),
        grid_spec=pltpu.PrefetchScalarGridSpec(
            num_scalar_prefetch=1,
            grid=(8,),
            in_specs=specs,
            out_specs=pl.BlockSpec((step, cols), lambda t, flags: (t, 0)),
        ),
        out_shape=jax.ShapeDtypeStruct(shape, jnp.float32),
        compiler_params=pltpu.CompilerParams(vmem_limit_bytes=VMEM_BYTES),
        cost_estimate=pl.CostEstimate(flops=0, bytes_accessed=0, transcendentals=0),
        name="finish",
    )(flags, factor, near, *parts)


def per_device(momentum):
    rows, cols = momentum.shape
    width = cols // 2
    quarter = rows // 4
    tiles = width // TILE
    z = lax.axis_index("row")
    c = lax.axis_index("col")
    core, side = c % 2, c // 2
    left = z < 2
    is_hub = (z == 1) | (z == 2)
    flags = jnp.stack([v.astype(jnp.int32) for v in (left, core, is_hub, side)])
    near_index = left.astype(jnp.int32).reshape(1)

    def over_core(x):
        return lax.ppermute(x, "col", [(k, k ^ 1) for k in range(4)])

    def over_side(x):
        return lax.ppermute(x, "col", [(k, k ^ 2) for k in range(4)])

    def between_hubs(x):
        return lax.ppermute(x, "row", [(1, 2), (2, 1)])

    def skip_one(x):
        return lax.ppermute(x, "row", [(0, 2), (2, 0), (1, 3), (3, 1)])

    def with_end(x):
        return lax.ppermute(x, "row", [(0, 1), (1, 0), (2, 3), (3, 2)])

    def to_end(x):
        return lax.ppermute(x, "row", [(1, 0), (2, 3)])

    def past_hub(x):
        return lax.ppermute(x, "row", [(0, 2), (3, 1), (1, 0), (2, 3)])

    def col_total(x):
        x = jnp.broadcast_to(x, (8, 128))
        x = x + over_core(x)
        return x + over_side(x)

    near, far, squares = take(momentum, near_index)
    beside = with_end(near)
    middle = between_hubs(far)
    norm_part = col_total(jnp.sum(squares))
    norm_part += with_end(norm_part)

    def added(x, y):
        return (x.astype(jnp.float32) + y.astype(jnp.float32)).astype(jnp.bfloat16)

    def over_pair(kept_sent):
        return added(kept_sent[0], over_core(kept_sent[1]))

    def over_sides(half):
        def rows_of(at):
            return lax.dynamic_slice(half, (0, at * quarter, 0), (half.shape[0], quarter, rows))

        return added(rows_of(side), over_side(rows_of(1 - side)))

    barrier = lax.optimization_barrier
    piece = width // 2
    outward = jnp.where(is_hub, middle[:, :piece], far[:, :piece])
    outward, beside, norm_part = barrier((outward, beside, norm_part))
    arrived = past_hub(outward)
    whole = {1: [(middle, width, 0)], 2: [(near, width, 0)], 3: [(beside, width, 0)]}
    pairs_1, pairs_2 = [(2, 2), (3, 3), (3, 2)], [(1, 2), (1, 1), (3, 1)]
    pairs_3, pairs_4 = [(0, 0), (0, 1)], [(0, 2), (0, 3)]
    first = gram_blocks(flags, pairs_1, {r: whole[r] for r in (2, 3)})
    second = gram_blocks(flags, pairs_2, whole)
    norm_sum = (norm_part + skip_one(norm_part))[0, 0]
    middle_later, far_later, first = barrier((middle, far, first))
    outward = jnp.where(is_hub, middle_later[:, piece:], far_later[:, piece:])
    arrived, outward, first, second, norm_sum = barrier((arrived, outward, first, second, norm_sum))

    def halves(h):
        blocks = {1: middle, 2: near, 3: beside}
        return {0: [(distant[h], piece, 0)]} | {r: [(blocks[r], piece, h)] for r in blocks}

    distant = [arrived, past_hub(outward)]
    first = over_pair(first)
    second = over_pair(second)
    (late,) = gram_blocks(flags, pairs_3 + pairs_4, halves(0), split=False)
    first = over_sides(first)
    distant[1], late, first, second = barrier((distant[1], late, first, second))

    other_first = between_hubs(first)
    second = over_sides(second)
    third = gram_blocks(flags, pairs_3, {r: halves(1)[r] for r in (0, 1)}, total=late)
    fourth = gram_blocks(flags, pairs_4, {r: halves(1)[r] for r in (0, 2, 3)}, total=late, total_at=2)
    other_first, second, fourth = barrier((other_first, second, fourth))
    other_second = between_hubs(second)
    third = over_sides(over_pair(third))
    other_third = between_hubs(third)
    fourth = over_sides(over_pair(fourth))
    other_second, fourth = barrier((other_second, fourth))
    other_fourth = between_hubs(fourth)

    spectral_edge = 1.0 + math.sqrt(M / N)
    inverse = 1.0 / (jnp.sqrt(norm_sum / M) * spectral_edge + 1e-07)

    mine, other = {}, {}

    def known(pairs, summed, received):
        for k, pair in enumerate(pairs):
            mine[pair], other[mirror(pair)] = summed[k], received[k]

    def gather(pairs):
        total = jnp.stack([mine[pair].astype(jnp.float32) + other[pair].astype(jnp.float32) for pair in pairs])
        here = (total * (inverse * inverse)).astype(jnp.bfloat16)
        across = over_side(here)
        return [here, over_core(here), across, over_core(across)]

    known(pairs_1, first, other_first)
    known(pairs_2, second, other_second)
    groups = [gather(GATHERED[0])]
    near_later, beside_later, other_third = barrier((near, beside, other_third))
    groups[0][1], groups[0][2], other_third = barrier((groups[0][1], groups[0][2], other_third))
    known(pairs_3, third, other_third)
    groups.append(gather(GATHERED[1]))
    passed = jnp.concatenate(distant, axis=1)
    inward = jnp.where(is_hub, passed, far)
    tile_bounds = [0, max(1, tiles * 4 // 9), max(2, tiles * 7 // 9), tiles]
    cuts = [t * TILE for t in tile_bounds]
    inward_first = with_end(inward[:, : cuts[1]])
    swaps = [
        jnp.stack([block[:, a:b] for block in (beside_later, near_later)]) for a, b in zip(cuts[:-1], cuts[1:])
    ]
    *swaps, other_fourth = barrier((*swaps, other_fourth))
    swaps[0] = between_hubs(swaps[0])
    groups[1][1], groups[1][2], inward_first, other_fourth = barrier(
        (groups[1][1], groups[1][2], inward_first, other_fourth)
    )
    known(pairs_4, fourth, other_fourth)
    groups.append(gather(GATHERED[2]))

    inward_second = with_end(inward[:, cuts[1] :])
    own, inward_second, *swaps = barrier((poly_rows(flags, groups), inward_second, *swaps))
    pair = over_core(own)
    swaps[1] = between_hubs(swaps[1])
    row_share = to_end(
        jnp.where(
            core == 0,
            lax.dynamic_slice(pair, (c * quarter, 0), (quarter, 4 * rows)),
            lax.dynamic_slice(own, (c * quarter, 0), (quarter, 4 * rows)),
        )
    )
    scale = inverse.reshape(1)
    inwards = [(inward_first, 0), (inward_second, 0), (inward_second, tile_bounds[2] - tile_bounds[1])]
    at_hub, at_end = [], []

    def far_product(k, scale):
        block, at = inwards[k]
        first, last = tile_bounds[k : k + 2]
        blocks = [(swaps[k], 0, 0), (swaps[k], 1, 0), (far, None, first), (block, None, at)]
        (here, there), squares = product(flags, (own, pair), scale, blocks, last - first, True)
        at_hub.append(here)
        at_end.append(to_end(there))
        return squares

    hub_sq = far_product(0, scale)
    scale, hub_sq, row_share, swaps[1] = barrier((scale, hub_sq, row_share, swaps[1]))
    row_across = over_side(row_share)
    swaps[2] = between_hubs(swaps[2])
    hub_sq += far_product(1, scale)
    at_end[0], scale, hub_sq, swaps[2], row_across = barrier((at_end[0], scale, hub_sq, swaps[2], row_across))
    hub_sq += far_product(2, scale)
    scale, hub_sq = barrier((scale, hub_sq))
    end_rows = [row_share, over_core(row_share), row_across, over_core(row_across)]
    blocks = [(passed, None, 0), (middle, None, 0), (near, None, 0), (beside, None, 0)]
    inward = [(inward_first, 0, tile_bounds[1]), (inward_second, tile_bounds[1], tiles)]
    (near_part,), near_sq = product(flags, (own, pair, *end_rows), scale, blocks, tiles, False, inward)
    at_end[1], near_sq = barrier((at_end[1], near_sq))
    total_sq = col_total(near_sq + jnp.where(is_hub, hub_sq, 0.0))
    total_sq += with_end(total_sq)
    total_sq += skip_one(total_sq)
    factor = (1.0 / (jnp.sqrt(total_sq[0, 0]) / math.sqrt(M * N) + 1e-07)).reshape(1)
    return finish(flags, factor, near_part, at_hub + at_end, cuts, (rows, cols))


def per_device_general(momentum):
    norm_sum = lax.psum(jnp.sum(momentum * momentum), ("col", "row"))
    spectral_edge = 1.0 + math.sqrt(M / N)
    scaled = (momentum / (jnp.sqrt(norm_sum / M) * spectral_edge + 1e-07)).astype(jnp.bfloat16)
    columns = lax.all_gather(scaled, "row", axis=0, tiled=True)
    gram_tile = lax.psum_scatter(
        lax.dot_general(
            columns, scaled, (((1,), (1,)), ((), ())), preferred_element_type=jnp.float32
        ).astype(jnp.bfloat16),
        "col",
        scatter_dimension=0,
        tiled=True,
    )
    left_rows = lax.all_gather(gram_tile, "row", axis=1, tiled=True)
    squared = jnp.dot(
        left_rows,
        lax.all_gather(gram_tile, "col", axis=0, tiled=True),
        preferred_element_type=jnp.float32,
    )
    poly = (coef_cubic * gram_tile.astype(jnp.float32) + coef_quintic * squared).astype(jnp.bfloat16)
    product = lax.dot_general(
        lax.all_gather(poly, "col", axis=0, tiled=True),
        columns,
        (((0,), (0,)), ((), ())),
        preferred_element_type=jnp.float32,
    )
    newton = coef_linear * scaled.astype(jnp.float32) + product
    newton_sq = lax.psum(jnp.sum(newton * newton), ("col", "row"))
    update_rms = jnp.sqrt(newton_sq) / math.sqrt(M * N)
    return newton / (update_rms + 1e-07)


def solution(mesh):
    def update(momentum):
        n_row, n_col = mesh.shape["row"], mesh.shape["col"]
        rows = momentum.shape[0] // (mesh.shape["groups"] * n_row)
        cols = momentum.shape[1] // n_col
        hubs = n_row == 4 and n_col == 4 and rows % STRIP == 0 and cols % (6 * TILE) == 0
        return jax.shard_map(
            per_device if hubs else per_device_general,
            mesh=mesh,
            in_specs=(P(("groups", "row"), "col"),),
            out_specs=P(("groups", "row"), "col"),
            check_vma=False,
        )(momentum)

    return update
```

```python
import functools
import math

import jax
import jax.numpy as jnp
from jax import lax
from jax.experimental import pallas as pl
from jax.experimental.pallas import tpu as pltpu
from jax.sharding import PartitionSpec as P

M = 3584
N = 18432

coef_linear = 3.4445
coef_cubic = -4.775
coef_quintic = 2.0315

TILE = 256
STRIP = 128
VMEM_BYTES = 56 * 2**20

GATHERED = [[(1, 2), (1, 1), (2, 2)], [(0, 0), (3, 3), (0, 1), (3, 2)], [(0, 2), (3, 1), (0, 3)]]


def mirror(pair):
    return pair if sum(pair) == 3 and pair[0] != pair[1] else (3 - pair[0], 3 - pair[1])


def take_kernel(index, x_ref, out_ref, sq_ref):
    @pl.when(pl.program_id(0) == 0)
    def _():
        sq_ref[...] = jnp.zeros_like(sq_ref)

    x = x_ref[...]
    out_ref[...] = x.astype(jnp.bfloat16)
    sq_ref[...] += jnp.sum(x * x, axis=0, keepdims=True)


def take(momentum, index):
    rows, cols = momentum.shape
    width = cols // 2
    step = rows // 8
    return pl.pallas_call(
        take_kernel,
        grid_spec=pltpu.PrefetchScalarGridSpec(
            num_scalar_prefetch=1,
            grid=(8,),
            in_specs=[pl.BlockSpec((step, width), lambda t, index: (t, index[0]))],
            out_specs=[
                pl.BlockSpec((step, width), lambda t, index: (t, 0)),
                pl.BlockSpec((1, width), lambda t, index: (0, 0)),
            ],
        ),
        out_shape=[
            jax.ShapeDtypeStruct((rows, width), jnp.bfloat16),
            jax.ShapeDtypeStruct((1, width), jnp.float32),
        ],
        compiler_params=pltpu.CompilerParams(vmem_limit_bytes=VMEM_BYTES),
        cost_estimate=pl.CostEstimate(
            flops=2 * rows * width, bytes_accessed=6 * rows * width, transcendentals=0
        ),
        name="take_half",
    )(index, momentum)


def gram_kernel(pairs, where, pieces, has_total, split, flags, *refs):
    left, core = flags[0] == 1, flags[1]
    b = pl.program_id(0)
    count = len(where) * pieces
    total = refs[count] if has_total else None
    outs = refs[count + has_total :]

    def make(i, j):
        value = total[0] if has_total else 0.0
        for p in range(pieces):
            x, y = refs[where[i] * pieces + p], refs[where[j] * pieces + p]
            value += lax.dot_general(
                x[...], y[...], (((1,), (1,)), ((), ())), preferred_element_type=jnp.float32
            )
        if not split:
            outs[0][0] = value
            return
        keep, send, whole = outs
        share = keep.shape[1]
        whole[...] = value.astype(jnp.bfloat16)
        keep[0] = whole[pl.ds(pl.multiple_of(core * share, 16), share), :]
        send[0] = whole[pl.ds(pl.multiple_of((1 - core) * share, 16), share), :]

    for k, (i, j) in enumerate(pairs):
        if (i, j) in ((1, 2), (0, 3)):
            pl.when((b == k) & left)(functools.partial(make, j, i))
            pl.when((b == k) & jnp.logical_not(left))(functools.partial(make, i, j))
        else:
            pl.when(b == k)(functools.partial(make, i, j))


def gram_blocks(flags, pairs, operands, total=None, total_at=0, split=True):
    where = {r: k for k, r in enumerate(operands)}
    pieces = len(operands[pairs[0][0]])
    rows = operands[pairs[0][0]][0][0].shape[0]
    share = rows // 2
    used = [piece for r in operands for piece in operands[r]]
    specs = [pl.BlockSpec((rows, width), lambda b, flags, at=at: (0, at)) for _, width, at in used]
    arrays = [array for array, _, _ in used]
    if total is not None:
        specs.append(
            pl.BlockSpec(
                (1, rows, rows), lambda b, flags: (total_at + b, 0, 0)
            )
        )
        arrays.append(total)
    count = len(pairs)
    if split:
        out_specs = [pl.BlockSpec((1, share, rows), lambda b, flags: (b, 0, 0))] * 2
        scratch = [pltpu.VMEM((rows, rows), jnp.bfloat16)]
        out_shape = [jax.ShapeDtypeStruct((count, share, rows), jnp.bfloat16)] * 2
    else:
        out_specs = [pl.BlockSpec((1, rows, rows), lambda b, flags: (b, 0, 0))]
        scratch = []
        out_shape = [jax.ShapeDtypeStruct((count, rows, rows), jnp.float32)]
    return pl.pallas_call(
        functools.partial(gram_kernel, pairs, where, pieces, int(total is not None), split),
        grid_spec=pltpu.PrefetchScalarGridSpec(
            num_scalar_prefetch=1, grid=(count,), in_specs=specs, out_specs=out_specs, scratch_shapes=scratch
        ),
        out_shape=out_shape,
        compiler_params=pltpu.CompilerParams(vmem_limit_bytes=VMEM_BYTES),
        cost_estimate=pl.CostEstimate(flops=0, bytes_accessed=0, transcendentals=0),
        name="gram_blocks",
    )(flags, *arrays)


def transpose_block(ref, rows, source, target):
    @pl.loop(0, rows // STRIP)
    def _(s):
        part = ref[
            pl.ds(pl.multiple_of(source[0] * rows, STRIP), rows),
            pl.ds(pl.multiple_of(source[1] * rows + s * STRIP, STRIP), STRIP),
        ]
        ref[
            pl.ds(pl.multiple_of(target[0] * rows + s * STRIP, STRIP), STRIP),
            pl.ds(pl.multiple_of(target[1] * rows, STRIP), rows),
        ] = part.T


def poly_kernel(flags, *refs):
    *parts, out_ref, gram, sems = refs
    rows = out_ref.shape[0]
    quarter = rows // 4
    left, core, side = flags[0], flags[1], flags[3]
    b = pl.program_id(0)

    @pl.when(b == 0)
    def _():
        places = [
            2 * core + side,
            2 * (1 - core) + side,
            2 * core + 1 - side,
            2 * (1 - core) + 1 - side,
        ]
        copies, turned = [], []
        for g, pairs in enumerate(GATHERED):
            for k, (i, j) in enumerate(pairs):
                if (i, j) in ((1, 2), (0, 3)):
                    i, j = jnp.where(left == 1, j, i), jnp.where(left == 1, i, j)
                for q, place in enumerate(places):
                    copies.append(
                        pltpu.make_async_copy(
                            parts[4 * g + q].at[k],
                            gram.at[
                                pl.ds(pl.multiple_of(i * rows + place * quarter, 16), quarter),
                                pl.ds(pl.multiple_of(j * rows, STRIP), rows),
                            ],
                            sems.at[len(copies)],
                        )
                    )
                if pairs[k][0] != pairs[k][1]:
                    turned.append((i, j))
        for copy in copies:
            copy.start()
        for copy in copies:
            copy.wait()
        for i, j in turned:
            transpose_block(gram, rows, (i, j), (j, i))

    at_i = pl.multiple_of((2 + core) * rows, STRIP)
    width = out_ref.shape[1]
    at_j = pl.multiple_of(b * width, STRIP)
    squared = jnp.dot(
        gram[pl.ds(at_i, rows), :], gram[:, pl.ds(at_j, width)], preferred_element_type=jnp.float32
    )
    here = gram[pl.ds(at_i, rows), pl.ds(at_j, width)].astype(jnp.float32)
    out_ref[...] = (coef_cubic * here + coef_quintic * squared).astype(jnp.bfloat16)


def poly_rows(flags, groups):
    rows = groups[0][0].shape[2]
    order = 4 * rows
    width = 2 * TILE
    return pl.pallas_call(
        poly_kernel,
        grid_spec=pltpu.PrefetchScalarGridSpec(
            num_scalar_prefetch=1,
            grid=(order // width,),
            in_specs=[pl.BlockSpec(memory_space=pl.ANY)] * 12,
            out_specs=pl.BlockSpec((rows, width), lambda b, flags: (0, b)),
            scratch_shapes=[pltpu.VMEM((order, order), jnp.bfloat16), pltpu.SemaphoreType.DMA((40,))],
        ),
        out_shape=jax.ShapeDtypeStruct((rows, order), jnp.bfloat16),
        compiler_params=pltpu.CompilerParams(vmem_limit_bytes=VMEM_BYTES),
        cost_estimate=pl.CostEstimate(flops=0, bytes_accessed=0, transcendentals=0),
        name="poly_rows",
    )(flags, *[x for group in groups for x in group])


def product_kernel(is_far, cut, flags, own, pair, *refs):
    end_rows, refs = ((), refs) if is_far else (refs[:4], refs[4:])
    inverse, blocks, inward, outs = refs[0], refs[1:5], () if is_far else refs[5:7], refs[5 if is_far else 7 : -4]
    sq_ref, poly, raw, sems = refs[-4:]
    rows = own.shape[0]

    @pl.when(pl.program_id(0) == 0)
    def _():
        sq_ref[...] = jnp.zeros_like(sq_ref)

        def load(pairs):
            copies = [
                pltpu.make_async_copy(source, target, sems.at[k]) for k, (source, target) in enumerate(pairs)
            ]
            for copy in copies:
                copy.start()
            for copy in copies:
                copy.wait()

        if is_far:
            at = pl.multiple_of(flags[1] * rows, 16)
            load([(own, poly.at[pl.ds(at, rows), :]), (pair, poly.at[pl.ds(rows - at, rows), :])])
        else:
            @pl.when((flags[2] == 1) & (flags[1] == 0))
            def _():
                load([(own, poly)])

            @pl.when((flags[2] == 1) & (flags[1] == 1))
            def _():
                load([(pair, poly)])

            @pl.when(flags[2] == 0)
            def _():
                core, side = flags[1], flags[3]
                quarter = rows // 4
                places = [2 * side + core, 2 * side + 1 - core, 2 * (1 - side) + core, 2 * (1 - side) + 1 - core]
                load(
                    [
                        (
                            part.at[:, m * rows : (m + 1) * rows],
                            poly.at[
                                pl.ds(pl.multiple_of(place * quarter, 16), quarter),
                                (m ^ 1) * rows : ((m ^ 1) + 1) * rows,
                            ],
                        )
                        for part, place in zip(end_rows, places)
                        for m in range(4)
                    ]
                )

    for r, block in enumerate(blocks):
        raw[r * rows : (r + 1) * rows, :] = block[...]
    for k, block in enumerate(inward):

        @pl.when((flags[2] == 0) & ((pl.program_id(0) >= cut) == (k == 1)))
        def _(block=block):
            raw[rows : 2 * rows, :] = block[...]

    for k, out in enumerate(outs):
        product = jnp.dot(poly[k * rows : (k + 1) * rows, :], raw[...], preferred_element_type=jnp.float32)
        own_rows = raw[(2 + k) * rows : (3 + k) * rows, :].astype(jnp.float32)
        newton = inverse[0] * (coef_linear * own_rows + product)
        sq_ref[...] += jnp.sum(newton * newton, axis=0, keepdims=True)
        out[...] = newton.astype(jnp.bfloat16)


def product(flags, polys, inverse, blocks, tiles, is_far, inward=()):
    rows, order = polys[0].shape
    count = 2 if is_far else 1
    block_specs = [
        pl.BlockSpec((rows, TILE), lambda t, flags, at=at: (0, at + t))
        if lead is None
        else pl.BlockSpec((None, rows, TILE), lambda t, flags, at=at, lead=lead: (lead, 0, at + t))
        for _, lead, at in blocks
    ] + [
        pl.BlockSpec((rows, TILE), lambda t, flags, a=a, b=b: (0, jnp.clip(t, a, b - 1) - a))
        for _, a, b in inward
    ]
    there = pl.BlockSpec((rows, TILE), lambda t, flags: (0, t))
    *newton, squares = pl.pallas_call(
        functools.partial(product_kernel, is_far, inward[0][2] if inward else 0),
        grid_spec=pltpu.PrefetchScalarGridSpec(
            num_scalar_prefetch=1,
            grid=(tiles,),
            in_specs=[pl.BlockSpec(memory_space=pl.ANY)] * len(polys)
            + [pl.BlockSpec(memory_space=pltpu.SMEM)]
            + block_specs,
            out_specs=[there] * count + [pl.BlockSpec((1, TILE), lambda t, flags: (0, 0))],
            scratch_shapes=[
                pltpu.VMEM((count * rows, order), jnp.bfloat16),
                pltpu.VMEM((order, TILE), jnp.bfloat16),
                pltpu.SemaphoreType.DMA((16,)),
            ],
        ),
        out_shape=[jax.ShapeDtypeStruct((rows, tiles * TILE), jnp.bfloat16)] * count
        + [jax.ShapeDtypeStruct((1, TILE), jnp.float32)],
        compiler_params=pltpu.CompilerParams(vmem_limit_bytes=VMEM_BYTES),
        cost_estimate=pl.CostEstimate(flops=0, bytes_accessed=0, transcendentals=0),
        name="product_far" if is_far else "product_near",
    )(flags, *polys, inverse, *[array for array, _, _ in (*blocks, *inward)])
    return newton, jnp.sum(squares)


def finish_kernel(cuts, flags, factor, near, *refs):
    out_ref = refs[-1]
    chunks = len(cuts) - 1
    width = near.shape[1]
    near_at = pl.multiple_of(flags[0] * width, STRIP)
    far_at = width - near_at
    out_ref[:, pl.ds(near_at, width)] = near[...].astype(jnp.float32) * factor[0]
    for k, ref in enumerate(refs[:-1]):
        first, last = cuts[k % chunks : k % chunks + 2]

        @pl.when((flags[2] == 1) == (k < chunks))
        def _(ref=ref, first=first, last=last):
            place = pl.ds(pl.multiple_of(far_at + first, STRIP), last - first)
            out_ref[:, place] = ref[...].astype(jnp.float32) * factor[0]


def finish(flags, factor, near, parts, cuts, shape):
    rows, cols = shape
    step = rows // 8
    specs = [pl.BlockSpec(memory_space=pltpu.SMEM)]
    specs += [pl.BlockSpec((step, part.shape[1]), lambda t, flags: (t, 0)) for part in (near, *parts)]
    return pl.pallas_call(
        functools.partial(finish_kernel, cuts),
        grid_spec=pltpu.PrefetchScalarGridSpec(
            num_scalar_prefetch=1,
            grid=(8,),
            in_specs=specs,
            out_specs=pl.BlockSpec((step, cols), lambda t, flags: (t, 0)),
        ),
        out_shape=jax.ShapeDtypeStruct(shape, jnp.float32),
        compiler_params=pltpu.CompilerParams(vmem_limit_bytes=VMEM_BYTES),
        cost_estimate=pl.CostEstimate(flops=0, bytes_accessed=0, transcendentals=0),
        name="finish",
    )(flags, factor, near, *parts)


def per_device(momentum):
    rows, cols = momentum.shape
    width = cols // 2
    quarter = rows // 4
    tiles = width // TILE
    z = lax.axis_index("row")
    c = lax.axis_index("col")
    core, side = c % 2, c // 2
    left = z < 2
    is_hub = (z == 1) | (z == 2)
    flags = jnp.stack([v.astype(jnp.int32) for v in (left, core, is_hub, side)])
    near_index = left.astype(jnp.int32).reshape(1)

    def over_core(x):
        return lax.ppermute(x, "col", [(k, k ^ 1) for k in range(4)])

    def over_side(x):
        return lax.ppermute(x, "col", [(k, k ^ 2) for k in range(4)])

    def between_hubs(x):
        return lax.ppermute(x, "row", [(1, 2), (2, 1)])

    def skip_one(x):
        return lax.ppermute(x, "row", [(0, 2), (2, 0), (1, 3), (3, 1)])

    def with_end(x):
        return lax.ppermute(x, "row", [(0, 1), (1, 0), (2, 3), (3, 2)])

    def to_end(x):
        return lax.ppermute(x, "row", [(1, 0), (2, 3)])

    def past_hub(x):
        return lax.ppermute(x, "row", [(0, 2), (3, 1), (1, 0), (2, 3)])

    def col_total(x):
        x = jnp.broadcast_to(x, (8, 128))
        x = x + over_core(x)
        return x + over_side(x)

    near, near_sq = take(momentum, near_index)
    beside = with_end(near)
    far, far_sq = take(momentum, 1 - near_index)
    middle = between_hubs(far)
    norm_part = col_total(jnp.sum(near_sq) + jnp.sum(far_sq))
    norm_part += with_end(norm_part)

    def added(x, y):
        return (x.astype(jnp.float32) + y.astype(jnp.float32)).astype(jnp.bfloat16)

    def over_pair(kept_sent):
        return added(kept_sent[0], over_core(kept_sent[1]))

    def over_sides(half):
        def rows_of(at):
            return lax.dynamic_slice(half, (0, at * quarter, 0), (half.shape[0], quarter, rows))

        return added(rows_of(side), over_side(rows_of(1 - side)))

    barrier = lax.optimization_barrier
    piece = width // 2
    outward = jnp.where(is_hub, middle[:, :piece], far[:, :piece])
    outward, beside, norm_part = barrier((outward, beside, norm_part))
    arrived = past_hub(outward)
    whole = {1: [(middle, width, 0)], 2: [(near, width, 0)], 3: [(beside, width, 0)]}
    pairs_1, pairs_2 = [(2, 2), (3, 3), (3, 2)], [(1, 2), (1, 1), (3, 1)]
    pairs_3, pairs_4 = [(0, 0), (0, 1)], [(0, 2), (0, 3)]
    first = gram_blocks(flags, pairs_1, {r: whole[r] for r in (2, 3)})
    second = gram_blocks(flags, pairs_2, whole)
    norm_sum = (norm_part + skip_one(norm_part))[0, 0]
    middle_later, far_later, first = barrier((middle, far, first))
    outward = jnp.where(is_hub, middle_later[:, piece:], far_later[:, piece:])
    arrived, outward, first, second, norm_sum = barrier((arrived, outward, first, second, norm_sum))

    def halves(h):
        blocks = {1: middle, 2: near, 3: beside}
        return {0: [(distant[h], piece, 0)]} | {r: [(blocks[r], piece, h)] for r in blocks}

    distant = [arrived, past_hub(outward)]
    first = over_pair(first)
    second = over_pair(second)
    (late,) = gram_blocks(flags, pairs_3 + pairs_4, halves(0), split=False)
    first = over_sides(first)
    distant[1], late, first, second = barrier((distant[1], late, first, second))

    other_first = between_hubs(first)
    second = over_sides(second)
    third = gram_blocks(flags, pairs_3, {r: halves(1)[r] for r in (0, 1)}, total=late)
    fourth = gram_blocks(flags, pairs_4, {r: halves(1)[r] for r in (0, 2, 3)}, total=late, total_at=2)
    other_first, second, fourth = barrier((other_first, second, fourth))
    other_second = between_hubs(second)
    third = over_sides(over_pair(third))
    other_third = between_hubs(third)
    fourth = over_sides(over_pair(fourth))
    other_second, fourth = barrier((other_second, fourth))
    other_fourth = between_hubs(fourth)

    spectral_edge = 1.0 + math.sqrt(M / N)
    inverse = 1.0 / (jnp.sqrt(norm_sum / M) * spectral_edge + 1e-07)

    mine, other = {}, {}

    def known(pairs, summed, received):
        for k, pair in enumerate(pairs):
            mine[pair], other[mirror(pair)] = summed[k], received[k]

    def gather(pairs):
        total = jnp.stack([mine[pair].astype(jnp.float32) + other[pair].astype(jnp.float32) for pair in pairs])
        here = (total * (inverse * inverse)).astype(jnp.bfloat16)
        across = over_side(here)
        return [here, over_core(here), across, over_core(across)]

    known(pairs_1, first, other_first)
    known(pairs_2, second, other_second)
    groups = [gather(GATHERED[0])]
    near_later, beside_later, other_third = barrier((near, beside, other_third))
    groups[0][1], groups[0][2], other_third = barrier((groups[0][1], groups[0][2], other_third))
    known(pairs_3, third, other_third)
    groups.append(gather(GATHERED[1]))
    passed = jnp.concatenate(distant, axis=1)
    inward = jnp.where(is_hub, passed, far)
    tile_bounds = [0, max(1, tiles * 4 // 9), max(2, tiles * 7 // 9), tiles]
    cuts = [t * TILE for t in tile_bounds]
    inward_first = with_end(inward[:, : cuts[1]])
    swaps = [
        jnp.stack([block[:, a:b] for block in (beside_later, near_later)]) for a, b in zip(cuts[:-1], cuts[1:])
    ]
    *swaps, other_fourth = barrier((*swaps, other_fourth))
    swaps[0] = between_hubs(swaps[0])
    groups[1][1], groups[1][2], inward_first, other_fourth = barrier(
        (groups[1][1], groups[1][2], inward_first, other_fourth)
    )
    known(pairs_4, fourth, other_fourth)
    groups.append(gather(GATHERED[2]))

    inward_second = with_end(inward[:, cuts[1] :])
    own, inward_second, *swaps = barrier((poly_rows(flags, groups), inward_second, *swaps))
    pair = over_core(own)
    swaps[1] = between_hubs(swaps[1])
    row_share = to_end(
        jnp.where(
            core == 0,
            lax.dynamic_slice(pair, (c * quarter, 0), (quarter, 4 * rows)),
            lax.dynamic_slice(own, (c * quarter, 0), (quarter, 4 * rows)),
        )
    )
    scale = inverse.reshape(1)
    inwards = [(inward_first, 0), (inward_second, 0), (inward_second, tile_bounds[2] - tile_bounds[1])]
    at_hub, at_end = [], []

    def far_product(k, scale):
        block, at = inwards[k]
        first, last = tile_bounds[k : k + 2]
        blocks = [(swaps[k], 0, 0), (swaps[k], 1, 0), (far, None, first), (block, None, at)]
        (here, there), squares = product(flags, (own, pair), scale, blocks, last - first, True)
        at_hub.append(here)
        at_end.append(to_end(there))
        return squares

    hub_sq = far_product(0, scale)
    scale, hub_sq, row_share, swaps[1] = barrier((scale, hub_sq, row_share, swaps[1]))
    row_across = over_side(row_share)
    swaps[2] = between_hubs(swaps[2])
    hub_sq += far_product(1, scale)
    at_end[0], scale, hub_sq, swaps[2], row_across = barrier((at_end[0], scale, hub_sq, swaps[2], row_across))
    hub_sq += far_product(2, scale)
    scale, hub_sq = barrier((scale, hub_sq))
    end_rows = [row_share, over_core(row_share), row_across, over_core(row_across)]
    blocks = [(passed, None, 0), (middle, None, 0), (near, None, 0), (beside, None, 0)]
    inward = [(inward_first, 0, tile_bounds[1]), (inward_second, tile_bounds[1], tiles)]
    (near_part,), near_sq = product(flags, (own, pair, *end_rows), scale, blocks, tiles, False, inward)
    at_end[1], near_sq = barrier((at_end[1], near_sq))
    total_sq = col_total(near_sq + jnp.where(is_hub, hub_sq, 0.0))
    total_sq += with_end(total_sq)
    total_sq += skip_one(total_sq)
    factor = (1.0 / (jnp.sqrt(total_sq[0, 0]) / math.sqrt(M * N) + 1e-07)).reshape(1)
    return finish(flags, factor, near_part, at_hub + at_end, cuts, (rows, cols))


def per_device_general(momentum):
    norm_sum = lax.psum(jnp.sum(momentum * momentum), ("col", "row"))
    spectral_edge = 1.0 + math.sqrt(M / N)
    scaled = (momentum / (jnp.sqrt(norm_sum / M) * spectral_edge + 1e-07)).astype(jnp.bfloat16)
    columns = lax.all_gather(scaled, "row", axis=0, tiled=True)
    gram_tile = lax.psum_scatter(
        lax.dot_general(
            columns, scaled, (((1,), (1,)), ((), ())), preferred_element_type=jnp.float32
        ).astype(jnp.bfloat16),
        "col",
        scatter_dimension=0,
        tiled=True,
    )
    left_rows = lax.all_gather(gram_tile, "row", axis=1, tiled=True)
    squared = jnp.dot(
        left_rows,
        lax.all_gather(gram_tile, "col", axis=0, tiled=True),
        preferred_element_type=jnp.float32,
    )
    poly = (coef_cubic * gram_tile.astype(jnp.float32) + coef_quintic * squared).astype(jnp.bfloat16)
    product = lax.dot_general(
        lax.all_gather(poly, "col", axis=0, tiled=True),
        columns,
        (((0,), (0,)), ((), ())),
        preferred_element_type=jnp.float32,
    )
    newton = coef_linear * scaled.astype(jnp.float32) + product
    newton_sq = lax.psum(jnp.sum(newton * newton), ("col", "row"))
    update_rms = jnp.sqrt(newton_sq) / math.sqrt(M * N)
    return newton / (update_rms + 1e-07)


def solution(mesh):
    def update(momentum):
        n_row, n_col = mesh.shape["row"], mesh.shape["col"]
        rows = momentum.shape[0] // (mesh.shape["groups"] * n_row)
        cols = momentum.shape[1] // n_col
        hubs = n_row == 4 and n_col == 4 and rows % STRIP == 0 and cols % (6 * TILE) == 0
        return jax.shard_map(
            per_device if hubs else per_device_general,
            mesh=mesh,
            in_specs=(P(("groups", "row"), "col"),),
            out_specs=P(("groups", "row"), "col"),
            check_vma=False,
        )(momentum)

    return update
```
